32 devices in a mesh: view: 4 (over y, core), row: 4 (over z), col: 2 (over x).
Axes of the slice: x: 2, y: 2, z: 4, core: 2. Of those that a mesh axis runs over, the one named last changes fastest.
Arguments:
- volume: bfloat16 [64, 1024, 1024], P('view', 'row', 'col'), may hold values from -5 to 5
- tf_color: float32 [3, 16], replicated, may hold values from 0 to 1
- tf_opacity: float32 [16], replicated, may hold values from 0.2 to 4
Outputs:
- picture: float32 [4, 4, 256, 1024], P(None, 'view', 'row', 'col')
The draws below stay inside these ranges and needn't reach their ends.
All inputs are finite; a program needn't handle non-finite values.
Results may differ from the reference program's by a relative error of at most 0.00095.
Values may be sent and summed in bfloat16 or wider, within the bound.
No kernel may reach another device: no remote copies, remote signals or barrier semaphores. Data moves between devices by JAX's collectives and lax.ppermute only.
A program may use at most 64 MiB of HBM per device.

```python
import math
import jax
import jax.numpy as jnp
from jax import lax

NY = 1024
NX = 1024
KNOTS = 16
NZ = 64
N_VIEW = 4
N_ROW = 4


def levels(own_key, extent, pieces, least, top_value):
    def one(dim, shards_of):
        draws = jax.random.uniform(jax.random.fold_in(jax.random.fold_in(own_key, 6), dim), (shards_of,), jnp.float32, least / len(pieces), top_value / len(pieces))
        return jnp.repeat(jnp.exp(draws), extent[dim] // shards_of).reshape((-1,) + (1,) * (len(extent) - dim - 1))

    level = one(*pieces[0])
    for cut in pieces[1:]:
        level = level * one(*cut)
    return level


def bell_draw(own_key, dims, width, most, pieces=(), kind=jnp.bfloat16):
    values = width * jax.random.normal(own_key, dims, jnp.float32)
    if pieces:
        values = values * levels(own_key, dims, pieces, -0.22, 0.18)
    return jnp.clip(values, -most, most).astype(kind)


def setup_inputs(seed: int = 0) -> dict:
    keys = jax.random.split(jax.random.key(seed), 4)
    return {
        "volume": bell_draw(keys[0], (NZ, NY, NX), 1.0, 5.0, ((0, 4), (1, 4), (2, 2))),
        "tf_color": jnp.clip(jax.random.uniform(keys[1], (3, KNOTS), jnp.float32, 0.0, 1.0), 0.0, 1.0),
        "tf_opacity": jnp.clip(jnp.exp(jax.random.uniform(keys[2], (KNOTS,), jnp.float32, math.log(0.2), math.log(4.0))), 0.2, 4.0),
    }


LIGHT_Z = 0.48
LIGHT_Y = 0.6
LIGHT_X = 0.64
VALUE_LOW = -3.0
VALUE_HIGH = 3.0

def classify(three_slices, tf_color, tf_opacity, depth_total):
    centre = three_slices[1, 1:-1, 1:-1]
    grad_z = (three_slices[2, 1:-1, 1:-1] - three_slices[0, 1:-1, 1:-1]) * 0.5
    grad_y = (three_slices[1, 2:, 1:-1] - three_slices[1, :-2, 1:-1]) * 0.5
    grad_x = (three_slices[1, 1:-1, 2:] - three_slices[1, 1:-1, :-2]) * 0.5
    grad_sq = grad_z * grad_z + grad_y * grad_y + grad_x * grad_x
    shading = 0.35 + 0.65 * jnp.abs(LIGHT_Z * grad_z + LIGHT_Y * grad_y + LIGHT_X * grad_x) / jnp.sqrt(grad_sq + 1.0)
    knot_count = tf_color.shape[1]
    scaled = jnp.clip((centre - VALUE_LOW) * ((knot_count - 1) / (VALUE_HIGH - VALUE_LOW)), 0.0, knot_count - 1.0)
    places = jnp.arange(knot_count, dtype=jnp.float32).reshape(knot_count, 1)
    weights = jnp.maximum(0.0, 1.0 - jnp.abs(scaled.reshape(1, -1) - places))
    colour = jnp.dot(tf_color, weights, precision=lax.Precision.HIGHEST).reshape((3,) + centre.shape)
    extinction = jnp.dot(tf_opacity.reshape(1, knot_count), weights, precision=lax.Precision.HIGHEST).reshape(centre.shape)
    opacity_cell = 1.0 - jnp.exp(-2.0 * extinction * (0.2 + grad_sq / (grad_sq + 1.0)) / depth_total)
    return (colour * shading * opacity_cell, opacity_cell)

def reference(volume, tf_color, tf_opacity):
    slice_count, height, columns = volume.shape
    padded = jnp.pad(volume, 1)

    def advance(running, slice_index):
        colour_sum, through = running
        three_slices = lax.dynamic_slice_in_dim(padded, slice_index, 3, 0).astype(jnp.float32)
        emission, opacity_cell = classify(three_slices, tf_color, tf_opacity, slice_count)
        return ((colour_sum + through * emission, through * (1.0 - opacity_cell)), None)
    initial = (jnp.zeros((3, height, columns), jnp.float32), jnp.ones((height, columns), jnp.float32))
    (colour_sum, through), _ = lax.scan(advance, initial, jnp.arange(slice_count, dtype=jnp.int32))
    whole = jnp.concatenate([colour_sum, (1.0 - through)[None]], axis=0)
    block_rows = NY // (N_VIEW * N_ROW)
    whole = whole.reshape(4, N_ROW, N_VIEW, block_rows, columns).transpose(0, 2, 1, 3, 4)
    return whole.reshape(4, N_VIEW, N_ROW * block_rows, columns)
```

```python
import functools

import jax
import jax.numpy as jnp
import numpy as np
from jax import lax
from jax.experimental import pallas as pl
from jax.experimental.pallas import tpu as pltpu
from jax.sharding import PartitionSpec as P

BASIS = ((12.0, 15.0, 16.0), (-20.0, 0.0, 15.0), (9.0, -20.0, 12.0))
NORM = 25.0
VALUE_LOW = -3.0
VALUE_HIGH = 3.0
AMBIENT = 0.35
DIFFUSE = 0.65
LANES = 128
PACK = 16
HALF = 8


def stencil(tile, knot_count):
    scale = (knot_count - 1) / (VALUE_HIGH - VALUE_LOW)
    width = 5 * tile + 3 * PACK
    after, before, above, centre, below, right, left, one = np.cumsum(
        [0, tile, tile, PACK, tile, PACK, tile, tile]
    )
    matrix = np.zeros((4 * tile, width), np.float32)
    for row in range(tile):
        for part, (along_z, along_y, along_x) in enumerate(BASIS):
            line = matrix[part * tile + row]
            line[after + row] += along_z / 2
            line[before + row] -= along_z / 2
            line[centre + row + 1 if row + 1 < tile else below] += along_y / 2
            line[centre + row - 1 if row > 0 else above + PACK - 1] -= along_y / 2
            line[right + row] += along_x / 2
            line[left + row] -= along_x / 2
        line = matrix[3 * tile + row]
        line[centre + row] = scale
        line[one] = -VALUE_LOW * scale
    rounded = matrix.astype(jnp.bfloat16)
    assert np.array_equal(rounded.astype(np.float32), matrix)
    return rounded


def edges_kernel(first_ref, last_ref, top_ref, bottom_ref, lo_ref, hi_ref, up_ref, down_ref):
    slices, height, lanes = first_ref.shape
    lane = lax.broadcasted_iota(jnp.int16, (height, lanes), 1)
    row = lax.broadcasted_iota(jnp.int16, up_ref.shape, 0)
    lo = hi = jnp.zeros((height, lanes), first_ref.dtype)
    up = down = jnp.zeros(up_ref.shape, up_ref.dtype)
    for z in range(slices):
        first, last = first_ref[z], last_ref[z]
        lo = jnp.where(lane == z, pltpu.roll(first, z, 1) if z else first, lo)
        hi = jnp.where(lane == z, pltpu.roll(last, z + 1, 1), hi)
        up = jnp.where(row == z, jnp.broadcast_to(top_ref[z, :1], up.shape), up)
        down = jnp.where(row == z, jnp.broadcast_to(bottom_ref[z, PACK - 1 :], up.shape), down)
    lo_ref[...] = lo
    hi_ref[...] = hi
    up_ref[...] = up
    down_ref[...] = down


def edges(volume):
    slices, height, width = volume.shape
    column = jax.ShapeDtypeStruct((height, LANES), volume.dtype)
    line = jax.ShapeDtypeStruct((slices, width), volume.dtype)
    last_lane, last_row = width // LANES - 1, height // PACK - 1
    return pl.pallas_call(
        edges_kernel,
        grid=(1,),
        out_shape=(column, column, line, line),
        in_specs=[
            pl.BlockSpec((slices, height, LANES), lambda i: (0, 0, 0)),
            pl.BlockSpec((slices, height, LANES), lambda i: (0, 0, last_lane)),
            pl.BlockSpec((slices, PACK, width), lambda i: (0, 0, 0)),
            pl.BlockSpec((slices, PACK, width), lambda i: (0, last_row, 0)),
        ],
        out_specs=(
            pl.BlockSpec((height, LANES), lambda i: (0, 0)),
            pl.BlockSpec((height, LANES), lambda i: (0, 0)),
            pl.BlockSpec((slices, width), lambda i: (0, 0)),
            pl.BlockSpec((slices, width), lambda i: (0, 0)),
        ),
        compiler_params=pltpu.CompilerParams(vmem_limit_bytes=32 * 2**20),
    )(volume, volume, volume, volume)


def from_neighbours(first, last, axis):
    count = lax.axis_size(axis)
    if count == 2:
        here = lax.axis_index(axis)
        other = lax.ppermute(jnp.where(here == 0, last, first), axis, [(0, 1), (1, 0)])
        nothing = jnp.zeros_like(other)
        return jnp.where(here == 0, nothing, other), jnp.where(here == 0, other, nothing)
    ends = range(count - 1)
    return (
        lax.ppermute(last, axis, [(i, i + 1) for i in ends]),
        lax.ppermute(first, axis, [(i + 1, i) for i in ends]),
    )


def march_kernel(
    ids_ref,
    stencil_ref,
    table_ref,
    cells_ref,
    above_ref,
    below_ref,
    before_ref,
    after_ref,
    lo_ref,
    hi_ref,
    up_ref,
    down_ref,
    out_ref,
    parts_ref,
    *,
    last_id,
    knot_count,
):
    slices, tile, width = cells_ref.shape
    place = ids_ref[pl.program_id(0)]
    lane = lax.broadcasted_iota(jnp.int16, (tile, LANES), 1)
    ones = jnp.ones((PACK, width), cells_ref.dtype)
    halves = -(-knot_count // HALF)
    rest = width - LANES

    def gradients(z):
        cells = cells_ref[z]
        above = jnp.where(
            place == 0, jnp.broadcast_to(up_ref[z : z + 1], (PACK, width)), above_ref[z]
        )
        below = jnp.where(
            place == last_id, jnp.broadcast_to(down_ref[z : z + 1], (PACK, width)), below_ref[z]
        )
        before = cells_ref[z - 1] if z > 0 else before_ref[...]
        after = cells_ref[z + 1] if z + 1 < slices else after_ref[...]
        right = pltpu.roll(cells, width - 1, 1)
        left = pltpu.roll(cells, 1, 1)
        hi = pltpu.roll(hi_ref[...], LANES - 1 - z, 1)
        lo = pltpu.roll(lo_ref[...], LANES - z, 1) if z else lo_ref[...]
        right_end = jnp.where(lane == LANES - 1, hi, right[:, rest:])
        left_end = jnp.where(lane == 0, lo, left[:, :LANES])
        if rest:
            right_end = jnp.concatenate([right[:, :rest], right_end], axis=1)
            left_end = jnp.concatenate([left_end, left[:, LANES:]], axis=1)
        stacked = jnp.concatenate(
            [after, before, above, cells, below, right_end, left_end, ones], axis=0
        )
        parts_ref[z % 2] = jnp.dot(
            stencil_ref[...], stacked, preferred_element_type=jnp.float32
        )

    def look_up(which, index, in_half):
        for half in range(halves):
            start = (which * halves + half) * HALF
            found = jnp.take_along_axis(
                table_ref[start : start + HALF], index, axis=0, mode="promise_in_bounds"
            )
            value = found if half == 0 else jnp.where(in_half[half - 1], found, value)
        return value

    def shade(z):
        slot = z % 2
        for row in range(0, tile, HALF):
            for column in range(0, width, LANES):
                here = (pl.ds(row, HALF), pl.ds(column, LANES))
                lit, second, third, knot = (
                    parts_ref[slot, pl.ds(part * tile + row, HALF), pl.ds(column, LANES)]
                    for part in range(4)
                )
                knot = jnp.minimum(jnp.maximum(knot, 0.0), knot_count - 1.0)
                segment = knot.astype(jnp.int32)
                index = segment & (HALF - 1)
                in_half = [knot >= float(HALF * half) for half in range(1, halves)]
                inverse = lax.rsqrt(
                    (lit * lit + second * second) + (third * third + NORM * NORM)
                )
                shading = jnp.abs(lit) * inverse + AMBIENT / DIFFUSE
                density = 1.2 / NORM**2 - inverse * inverse
                values = [
                    look_up(2 * c, index, in_half) + look_up(2 * c + 1, index, in_half) * knot
                    for c in range(4)
                ]
                kept = jnp.exp2(values[3] * density)
                if z == 0:
                    through = kept
                    weight = (1.0 - kept) * shading
                    for c in range(3):
                        out_ref[(c,) + here] = values[c] * weight
                else:
                    earlier = out_ref[(3,) + here]
                    through = earlier * kept
                    weight = (earlier - through) * shading
                    for c in range(3):
                        out_ref[(c,) + here] += values[c] * weight
                out_ref[(3,) + here] = through

    gradients(0)
    for z in range(slices):
        if z + 1 < slices:
            gradients(z + 1)
        shade(z)


def march(volume, halos, ids, tables, knot_count, tile):
    slices, height, width = volume.shape
    before, after, lo, hi, up, down = halos
    matrix = jnp.asarray(stencil(tile, knot_count))
    count = ids.shape[0]
    step, last = tile // PACK, height // PACK - 1
    whole = lambda shape: pl.BlockSpec(shape, lambda i, ids: (0,) * len(shape))
    grid_spec = pltpu.PrefetchScalarGridSpec(
        num_scalar_prefetch=1,
        grid=(count,),
        in_specs=[
            whole(matrix.shape),
            whole(tables.shape),
            pl.BlockSpec((slices, tile, width), lambda i, ids: (0, ids[i], 0)),
            pl.BlockSpec(
                (slices, PACK, width), lambda i, ids: (0, jnp.maximum(ids[i] * step - 1, 0), 0)
            ),
            pl.BlockSpec(
                (slices, PACK, width),
                lambda i, ids: (0, jnp.minimum((ids[i] + 1) * step, last), 0),
            ),
            pl.BlockSpec((tile, width), lambda i, ids: (ids[i], 0)),
            pl.BlockSpec((tile, width), lambda i, ids: (ids[i], 0)),
            pl.BlockSpec((tile, LANES), lambda i, ids: (ids[i], 0)),
            pl.BlockSpec((tile, LANES), lambda i, ids: (ids[i], 0)),
            whole(up.shape),
            whole(down.shape),
        ],
        out_specs=pl.BlockSpec((4, tile, width), lambda i, ids: (0, i, 0)),
        scratch_shapes=[pltpu.VMEM((2, 4 * tile, width), jnp.float32)],
    )
    return pl.pallas_call(
        functools.partial(march_kernel, last_id=height // tile - 1, knot_count=knot_count),
        grid_spec=grid_spec,
        out_shape=jax.ShapeDtypeStruct((4, count * tile, width), jnp.float32),
        compiler_params=pltpu.CompilerParams(vmem_limit_bytes=48 * 2**20),
    )(ids, matrix, tables, volume, volume, volume, before, after, lo, hi, up, down)


def make_tables(tf_color, tf_opacity, depth_total):
    knot_count = tf_color.shape[1]
    optical = -2.0 / depth_total * NORM**2 * np.log2(np.e)
    knots = jnp.concatenate([tf_color * DIFFUSE, tf_opacity[None] * np.float32(optical)], axis=0)
    slope = jnp.concatenate([knots[:, 1:] - knots[:, :-1], jnp.zeros((4, 1), knots.dtype)], axis=1)
    base = knots - slope * jnp.arange(knot_count, dtype=knots.dtype)
    lines = jnp.stack([base, slope], axis=1)
    lines = jnp.pad(lines, ((0, 0), (0, 0), (0, -knot_count % HALF)))
    return jnp.broadcast_to(lines.reshape(-1, 1), (lines.size, LANES))


def over(nearer, farther):
    through = nearer[3:]
    return jnp.concatenate([nearer[:3] + through * farther[:3], through * farther[3:]], axis=0)


def merged(own, other, side):
    nearer = jnp.where(side == 0, own, other)
    farther = jnp.where(side == 0, other, own)
    return over(nearer, farther)


def from_partner(value, axis, bit):
    pairs = [(source, source ^ (1 << bit)) for source in range(lax.axis_size(axis))]
    return lax.ppermute(value, axis, pairs)


def on_device(volume, tf_color, tf_opacity):
    view_count = lax.axis_size("view")
    position = lax.axis_index("view")
    slices, height, width = volume.shape
    knot_count = tf_color.shape[1]
    tile_rows = height // view_count
    tile = min(32, tile_rows)
    bits = view_count.bit_length() - 1
    group_bits = min(2, bits)
    groups = 1 << group_bits
    per_group = view_count // groups

    before, after = from_neighbours(volume[0], volume[-1], "view")
    lo_face, hi_face, up_face, down_face = edges(volume)
    lo, hi = from_neighbours(lo_face, hi_face, "col")
    up, down = from_neighbours(up_face, down_face, "row")
    halos = (before, after, lo, hi, up, down)
    tables = make_tables(tf_color, tf_opacity, slices * view_count)

    steps = tile_rows // tile
    pieces = {}
    earlier = None
    for distance in reversed(range(groups)):
        blocks = np.arange(per_group) * groups + (position % groups ^ distance)
        ids = (blocks[:, None] * steps + np.arange(steps)).reshape(-1).astype(jnp.int32)
        if earlier is not None:
            ids, earlier = lax.optimization_barrier((ids, earlier))
            pieces[distance + 1] = earlier
        earlier = march(volume, halos, ids, tables, knot_count, tile)
    pieces[0] = earlier

    for bit in range(group_bits):
        side = position >> bit & 1
        for distance in reversed(range(0, groups, 2 << bit)):
            sent = pieces.pop(distance + (1 << bit))
            pieces[distance] = merged(pieces[distance], from_partner(sent, "view", bit), side)
    image = pieces[0].reshape((4,) + (2,) * (bits - group_bits) + (tile_rows, width))
    for bit in range(group_bits, bits):
        side = position >> bit & 1
        axis = bits - bit
        kept = lax.dynamic_index_in_dim(image, side, axis, keepdims=False)
        sent = lax.dynamic_index_in_dim(image, 1 - side, axis, keepdims=False)
        image = merged(kept, from_partner(sent, "view", bit), side)
    image = jnp.concatenate([image[:3], 1.0 - image[3:]], axis=0)
    return image.reshape(4, 1, tile_rows, width)


def solution(mesh):
    placed = (P("view", "row", "col"), P(), P())
    return jax.shard_map(
        on_device,
        mesh=mesh,
        in_specs=placed,
        out_specs=P(None, "view", "row", "col"),
        check_vma=False,
    )
```

```python
import functools

import jax
import jax.numpy as jnp
import numpy as np
from jax import lax
from jax.experimental import pallas as pl
from jax.experimental.pallas import tpu as pltpu
from jax.sharding import PartitionSpec as P

BASIS = ((12.0, 15.0, 16.0), (-20.0, 0.0, 15.0), (9.0, -20.0, 12.0))
NORM = 25.0
VALUE_LOW = -3.0
VALUE_HIGH = 3.0
AMBIENT = 0.35
DIFFUSE = 0.65
LANES = 128
PACK = 16
HALF = 8
DEPTH = 2
SLOTS = 4


def stencil(tile, knot_count):
    scale = (knot_count - 1) / (VALUE_HIGH - VALUE_LOW)
    width = 5 * tile + 3 * PACK
    after, before, above, centre, below, right, left, one = np.cumsum(
        [0, tile, tile, PACK, tile, PACK, tile, tile]
    )
    matrix = np.zeros((4 * tile, width), np.float32)
    for row in range(tile):
        for part, (along_z, along_y, along_x) in enumerate(BASIS):
            line = matrix[part * tile + row]
            line[after + row] += along_z / 2
            line[before + row] -= along_z / 2
            line[centre + row + 1 if row + 1 < tile else below] += along_y / 2
            line[centre + row - 1 if row > 0 else above + PACK - 1] -= along_y / 2
            line[right + row] += along_x / 2
            line[left + row] -= along_x / 2
        line = matrix[3 * tile + row]
        line[centre + row] = scale / 2
        line[one] = -VALUE_LOW * scale / 2 - 0.5
    rounded = matrix.astype(jnp.bfloat16)
    assert np.array_equal(rounded.astype(np.float32), matrix)
    return rounded


def exchange(first, last, axis):
    count = lax.axis_size(axis)
    received = []
    for face, start in ((first, 0), (last, 1)):
        pairs = [(i, i + 1) for i in range(start, count - 1, 2)]
        if pairs:
            received.append(lax.ppermute(face, axis, pairs + [(j, i) for i, j in pairs]))
        else:
            received.append(jnp.zeros_like(face))
    return received


def edges_kernel(odd_ref, *refs):
    depth_refs, row_refs, column_refs = refs[0:2], refs[2:4], refs[4:6]
    depth_outs, row_outs, column_outs = refs[6:8], refs[8:10], refs[10:12]
    slices, height, lanes = column_refs[0].shape
    lane = lax.broadcasted_iota(jnp.int16, (height, lanes), 1)
    row = lax.broadcasted_iota(jnp.int16, row_outs[0].shape, 0)
    for turn in range(2):
        depth_outs[turn][...] = depth_refs[turn][0]
        is_first = odd_ref[1] == 1 - turn
        lines = jnp.zeros(row_outs[turn].shape, row_outs[turn].dtype)
        for z in range(slices):
            line = jnp.where(
                is_first, row_refs[turn][z, :1], row_refs[turn][z, PACK - 1 :]
            )
            lines = jnp.where(row == z, jnp.broadcast_to(line, lines.shape), lines)
        row_outs[turn][...] = lines

        def columns(turn, source, shift):
            found = jnp.zeros((height, lanes), column_outs[turn].dtype)
            for z in range(slices):
                target = (2 * z + shift) % lanes
                moved = pltpu.roll(column_refs[turn][z], (target - source) % lanes, 1)
                found = jnp.where(lane == target, moved, found)
            column_outs[turn][...] = found

        pl.when(odd_ref[2] == 1 - turn)(functools.partial(columns, turn, 0, -1))
        pl.when(odd_ref[2] == turn)(functools.partial(columns, turn, lanes - 1, 0))


def edges(volume, odd):
    slices, height, width = volume.shape
    assert 2 * slices <= LANES
    column = jax.ShapeDtypeStruct((height, LANES), volume.dtype)
    line = jax.ShapeDtypeStruct((slices, width), volume.dtype)
    face = jax.ShapeDtypeStruct((height, width), volume.dtype)

    def at(block, dim, turn):
        last = volume.shape[dim] // block[dim] - 1

        def index(i, odd):
            place = jnp.where(odd[dim] == 1 - turn, 0, last)
            return tuple(place if d == dim else 0 for d in range(3))

        return pl.BlockSpec(block, index)

    blocks = ((1, height, width), (slices, PACK, width), (slices, height, LANES))
    shapes = (face, face, line, line, column, column)
    return pl.pallas_call(
        edges_kernel,
        grid_spec=pltpu.PrefetchScalarGridSpec(
            num_scalar_prefetch=1,
            grid=(1,),
            in_specs=[at(block, dim, turn) for dim, block in enumerate(blocks) for turn in range(2)],
            out_specs=[pl.BlockSpec(shape.shape, lambda i, odd: (0, 0)) for shape in shapes],
        ),
        out_shape=shapes,
        compiler_params=pltpu.CompilerParams(vmem_limit_bytes=32 * 2**20),
    )(odd, *[volume] * 6)


def march_kernel(
    ids_ref,
    odd_ref,
    stencil_ref,
    table_ref,
    cells_ref,
    above_ref,
    below_ref,
    depth_refs,
    line_refs,
    ends_ref,
    out_ref,
    parts_ref,
    *,
    last_id,
    knot_count,
):
    slices, tile, width = cells_ref.shape
    place = ids_ref[pl.program_id(0)]
    lane = lax.broadcasted_iota(jnp.int16, (tile, LANES), 1)
    ones = jnp.ones((PACK, width), cells_ref.dtype)
    halves = -(-knot_count // (2 * HALF))
    rest = width - LANES

    def ordered(axis, pair):
        early, late = pair[0][...], pair[1][...]
        odd = odd_ref[axis] == 1
        return jnp.where(odd, early, late), jnp.where(odd, late, early)

    behind, ahead = ordered(0, depth_refs)
    up, down = ordered(1, line_refs)

    def gradients(z):
        cells = cells_ref[z]
        above = jnp.where(
            place == 0, jnp.broadcast_to(up[z : z + 1], (PACK, width)), above_ref[z]
        )
        below = jnp.where(
            place == last_id, jnp.broadcast_to(down[z : z + 1], (PACK, width)), below_ref[z]
        )
        before = cells_ref[z - 1] if z > 0 else behind
        after = cells_ref[z + 1] if z + 1 < slices else ahead
        right = pltpu.roll(cells, width - 1, 1)
        left = pltpu.roll(cells, 1, 1)
        ends = pltpu.roll(ends_ref[...], LANES - 2 * z, 1) if z else ends_ref[...]
        right_end = jnp.where(lane == LANES - 1, ends, right[:, rest:])
        left_end = jnp.where(lane == 0, ends, left[:, :LANES])
        if rest:
            right_end = jnp.concatenate([right[:, :rest], right_end], axis=1)
            left_end = jnp.concatenate([left_end, left[:, LANES:]], axis=1)
        stacked = jnp.concatenate(
            [after, before, above, cells, below, right_end, left_end, ones], axis=0
        )
        parts_ref[z % SLOTS] = jnp.dot(
            stencil_ref[...], stacked, preferred_element_type=jnp.float32
        )

    tables = [table_ref[start * HALF : start * HALF + HALF] for start in range(12 * halves)]

    def look_up(which, index, in_half):
        for half in range(halves):
            found = jnp.take_along_axis(
                tables[which * halves + half], index, axis=0, mode="promise_in_bounds"
            )
            value = found if half == 0 else jnp.where(in_half[half - 1], found, value)
        return value

    def shade(first):
        for row in range(0, tile, HALF):
            for column in range(0, width, LANES):
                here = (pl.ds(row, HALF), pl.ds(column, LANES))
                state = None if first == 0 else [out_ref[(c,) + here] for c in range(4)]
                for z in range(first, first + DEPTH):
                    state = one(z, row, column, state)
                for c in range(4):
                    out_ref[(c,) + here] = state[c]

    def one(z, row, column, state):
        slot = z % SLOTS
        lit, second, third, knot = (
            parts_ref[slot, pl.ds(part * tile + row, HALF), pl.ds(column, LANES)]
            for part in range(4)
        )
        knot = jnp.minimum(jnp.maximum(knot, -0.5), knot_count / 2 - 1.0)
        middle = jnp.round(knot)
        segment = middle.astype(jnp.int32)
        offset = knot - middle
        before_middle = offset < 0.0
        index = segment & (HALF - 1) if halves > 1 else segment
        in_half = [middle >= float(HALF * half) for half in range(1, halves)]
        inverse = lax.rsqrt((lit * lit + second * second) + (third * third + NORM * NORM))
        shading = jnp.abs(lit) * inverse + AMBIENT / DIFFUSE
        density = 1.2 / NORM**2 - inverse * inverse
        values = [
            look_up(3 * c, index, in_half)
            + offset
            * jnp.where(
                before_middle,
                look_up(3 * c + 1, index, in_half),
                look_up(3 * c + 2, index, in_half),
            )
            for c in range(4)
        ]
        kept = jnp.exp2(values[3] * density)
        if state is None:
            weight = (1.0 - kept) * shading
            return [value * weight for value in values[:3]] + [kept]
        through = state[3] * kept
        weight = (state[3] - through) * shading
        return [total + value * weight for total, value in zip(state, values[:3])] + [through]

    for z in range(DEPTH):
        gradients(z)
    for z in range(0, slices, DEPTH):
        if z + DEPTH < slices:
            for later in range(z + DEPTH, z + 2 * DEPTH):
                gradients(later)
        shade(z)


def march(volume, halos, ids, odd, tables, knot_count, tile):
    slices, height, width = volume.shape
    depth, lines, ends = halos
    matrix = jnp.asarray(stencil(tile, knot_count))
    count = ids.shape[0]
    step, last = tile // PACK, height // PACK - 1
    whole = lambda shape: pl.BlockSpec(shape, lambda i, ids, odd: (0,) * len(shape))
    grid_spec = pltpu.PrefetchScalarGridSpec(
        num_scalar_prefetch=2,
        grid=(count,),
        in_specs=[
            whole(matrix.shape),
            whole(tables.shape),
            pl.BlockSpec((slices, tile, width), lambda i, ids, odd: (0, ids[i], 0)),
            pl.BlockSpec(
                (slices, PACK, width), lambda i, ids, odd: (0, jnp.maximum(ids[i] * step - 1, 0), 0)
            ),
            pl.BlockSpec(
                (slices, PACK, width),
                lambda i, ids, odd: (0, jnp.minimum((ids[i] + 1) * step, last), 0),
            ),
            [pl.BlockSpec((tile, width), lambda i, ids, odd: (ids[i], 0))] * 2,
            [whole(lines[0].shape)] * 2,
            pl.BlockSpec((tile, LANES), lambda i, ids, odd: (ids[i], 0)),
        ],
        out_specs=pl.BlockSpec((4, tile, width), lambda i, ids, odd: (0, i, 0)),
        scratch_shapes=[pltpu.VMEM((SLOTS, 4 * tile, width), jnp.float32)],
    )
    return pl.pallas_call(
        functools.partial(march_kernel, last_id=height // tile - 1, knot_count=knot_count),
        grid_spec=grid_spec,
        out_shape=jax.ShapeDtypeStruct((4, count * tile, width), jnp.float32),
        compiler_params=pltpu.CompilerParams(vmem_limit_bytes=48 * 2**20),
    )(ids, odd, matrix, tables, volume, volume, volume, depth, lines, ends)


def make_tables(tf_color, tf_opacity, depth_total):
    knot_count = tf_color.shape[1]
    optical = -2.0 / depth_total * NORM**2 * np.log2(np.e)
    knots = jnp.concatenate([tf_color * DIFFUSE, tf_opacity[None] * np.float32(optical)], axis=0)
    segments = (knot_count + 1) // 2
    knots = jnp.pad(knots, ((0, 0), (0, 2 * segments + 1 - knot_count)), mode="edge")
    middle = knots[:, 1::2]
    slopes = [2.0 * (middle - knots[:, :-1:2]), 2.0 * (knots[:, 2::2] - middle)]
    lines = jnp.stack([middle] + slopes, axis=1)
    lines = jnp.pad(lines, ((0, 0), (0, 0), (0, -segments % HALF)))
    return jnp.broadcast_to(lines.reshape(-1, 1), (lines.size, LANES))


def over(nearer, farther):
    through = nearer[3:]
    return jnp.concatenate([nearer[:3] + through * farther[:3], through * farther[3:]], axis=0)


def merged(own, other, side):
    nearer = jnp.where(side == 0, own, other)
    farther = jnp.where(side == 0, other, own)
    return over(nearer, farther)


def from_partner(value, axis, bit):
    pairs = [(source, source ^ (1 << bit)) for source in range(lax.axis_size(axis))]
    return lax.ppermute(value, axis, pairs)


def on_device(volume, tf_color, tf_opacity):
    view_count = lax.axis_size("view")
    position = lax.axis_index("view")
    slices, height, width = volume.shape
    knot_count = tf_color.shape[1]
    tile_rows = height // view_count
    tile = min(32, tile_rows)
    bits = view_count.bit_length() - 1
    group_bits = min(2, bits)
    groups = 1 << group_bits
    per_group = view_count // groups

    volume = pltpu.with_memory_space_constraint(volume, pltpu.HBM)
    odd = jnp.stack([lax.axis_index(axis) % 2 for axis in ("view", "row", "col")])
    faces = edges(volume, odd)
    depth = exchange(*faces[0:2], "view")
    lines = exchange(*faces[2:4], "row")
    ends = exchange(*faces[4:6], "col")
    halos = (depth, lines, ends[0] + ends[1] if lax.axis_size("col") > 2 else ends[0])
    tables = make_tables(tf_color, tf_opacity, slices * view_count)

    steps = tile_rows // tile

    def march_group(distance, after):
        blocks = np.arange(per_group) * groups + (position % groups ^ distance)
        ids = (blocks[:, None] * steps + np.arange(steps)).reshape(-1).astype(jnp.int32)
        if after is not None:
            ids, after = lax.optimization_barrier((ids, after))
        return march(volume, halos, ids, odd, tables, knot_count, tile), after

    def gather_group(distance, bit, after):
        if bit == 0:
            return march_group(distance, after)
        bit -= 1
        sent, after = gather_group(distance + (1 << bit), bit, after)
        received = from_partner(sent, "view", bit)
        kept, _ = gather_group(distance, bit, sent)
        return merged(kept, received, position >> bit & 1), after

    pieces = {0: gather_group(0, group_bits, None)[0]}
    image = pieces[0].reshape((4,) + (2,) * (bits - group_bits) + (tile_rows, width))
    for bit in range(group_bits, bits):
        side = position >> bit & 1
        axis = bits - bit
        kept = lax.dynamic_index_in_dim(image, side, axis, keepdims=False)
        sent = lax.dynamic_index_in_dim(image, 1 - side, axis, keepdims=False)
        image = merged(kept, from_partner(sent, "view", bit), side)
    image = jnp.concatenate([image[:3], 1.0 - image[3:]], axis=0)
    return image.reshape(4, 1, tile_rows, width)


def solution(mesh):
    placed = (P("view", "row", "col"), P(), P())
    return jax.shard_map(
        on_device,
        mesh=mesh,
        in_specs=placed,
        out_specs=P(None, "view", "row", "col"),
        check_vma=False,
    )
```

```python
import functools

import jax
import jax.numpy as jnp
import numpy as np
from jax import lax
from jax.experimental import pallas as pl
from jax.experimental.pallas import tpu as pltpu
from jax.sharding import PartitionSpec as P

BASIS = ((12.0, 15.0, 16.0), (-20.0, 0.0, 15.0), (9.0, -20.0, 12.0))
NORM = 25.0
VALUE_LOW = -3.0
VALUE_HIGH = 3.0
AMBIENT = 0.35
DIFFUSE = 0.65
LANES = 128
PACK = 16
HALF = 8
AXES = ("view", "row", "col")
DEPTH = 2
SLOTS = 4


def stencil(tile, knot_count):
    scale = (knot_count - 1) / (VALUE_HIGH - VALUE_LOW)
    width = 5 * tile + 3 * PACK
    after, before, above, centre, below, right, left, one = np.cumsum(
        [0, tile, tile, PACK, tile, PACK, tile, tile]
    )
    matrix = np.zeros((4 * tile, width), np.float32)
    for row in range(tile):
        for part, (along_z, along_y, along_x) in enumerate(BASIS):
            line = matrix[part * tile + row]
            line[after + row] += along_z / 2
            line[before + row] -= along_z / 2
            line[centre + row + 1 if row + 1 < tile else below] += along_y / 2
            line[centre + row - 1 if row > 0 else above + PACK - 1] -= along_y / 2
            line[right + row] += along_x / 2
            line[left + row] -= along_x / 2
        line = matrix[3 * tile + row]
        line[centre + row] = scale / 2
        line[one] = -VALUE_LOW * scale / 2 - 0.5
    rounded = matrix.astype(jnp.bfloat16)
    assert np.array_equal(rounded.astype(np.float32), matrix)
    return rounded


def exchange(faces, axis):
    count = lax.axis_size(axis)
    received = []
    for start, face in enumerate(faces):
        pairs = [(i, i + 1) for i in range(start, count - 1, 2)]
        both = pairs + [(j, i) for i, j in pairs]
        received.append(lax.ppermute(face, axis, both) if both else jnp.zeros_like(face))
    return received


def segment_lines(knot_count):
    segments = (knot_count + 1) // 2
    rows = -(-segments // HALF) * HALF
    lines = np.zeros((3, rows, knot_count), np.float32)
    for segment in range(segments):
        left, middle, right = (min(2 * segment + i, knot_count - 1) for i in range(3))
        lines[0, segment, middle] += 1.0
        lines[1, segment, middle] += 2.0
        lines[1, segment, left] -= 2.0
        lines[2, segment, right] += 2.0
        lines[2, segment, middle] -= 2.0
    return lines.reshape(3 * rows, knot_count)


def prepare_kernel(
    odd_ref,
    volume_ref,
    lines_ref,
    color_ref,
    opacity_ref,
    cells_ref,
    table_ref,
    depth_outs,
    row_outs,
    column_outs,
    arrived,
    *,
    optical,
):
    slices, height, width = cells_ref.shape
    chunks = arrived.shape[0]
    size = slices // chunks
    copies = [
        pltpu.make_async_copy(
            volume_ref.at[pl.ds(chunk * size, size)],
            cells_ref.at[pl.ds(chunk * size, size)],
            arrived.at[chunk],
        )
        for chunk in range(chunks)
    ]
    for copy in copies:
        copy.start()
    block = lines_ref.shape[0]
    for channel in range(4):
        knots = color_ref[channel : channel + 1] * DIFFUSE if channel < 3 else opacity_ref[...] * optical
        value = jnp.sum(lines_ref[...] * knots, axis=1, keepdims=True)
        table_ref[pl.ds(channel * block, block)] = jnp.broadcast_to(value, (block, LANES))
    lane = lax.broadcasted_iota(jnp.int16, (height, LANES), 1)
    row = lax.broadcasted_iota(jnp.int16, (slices, width), 0)
    lines = [jnp.zeros((slices, width), cells_ref.dtype)] * len(row_outs)
    for chunk, copy in enumerate(copies):
        copy.wait()
        here = range(chunk * size, (chunk + 1) * size)
        for turn in range(len(row_outs)):
            is_first = odd_ref[1] == 1 - turn
            for z in here:
                line = jnp.where(is_first, cells_ref[z, :1], cells_ref[z, height - 1 :])
                lines[turn] = jnp.where(
                    row == z, jnp.broadcast_to(line, (slices, width)), lines[turn]
                )

        def columns(turn, column, source, shift):
            found = (
                column_outs[turn][...] if chunk else jnp.zeros((height, LANES), cells_ref.dtype)
            )
            for z in here:
                target = (2 * z + shift) % LANES
                cells = cells_ref[z, :, pl.ds(column, LANES)]
                moved = pltpu.roll(cells, (target - source) % LANES, 1)
                found = jnp.where(lane == target, moved, found)
            column_outs[turn][...] = found

        for turn in range(len(column_outs)):
            pl.when(odd_ref[2] == 1 - turn)(functools.partial(columns, turn, 0, 0, -1))
            pl.when(odd_ref[2] == turn)(
                functools.partial(columns, turn, width - LANES, LANES - 1, 0)
            )
    for turn in range(len(row_outs)):
        row_outs[turn][...] = lines[turn]
    for turn in range(len(depth_outs)):
        face = jnp.where(odd_ref[0] == 1 - turn, 0, slices - 1)
        depth_outs[turn][...] = cells_ref[face]


def prepare(volume, tf_color, tf_opacity, odd, depth_total):
    slices, height, width = volume.shape
    assert 2 * slices <= LANES
    knot_count = tf_color.shape[1]
    lines = jnp.asarray(segment_lines(knot_count))
    shapes = [(height, width), (slices, width), (height, LANES)]
    turns = [2 if lax.axis_size(axis) > 2 else 1 for axis in AXES]
    faces = [
        [jax.ShapeDtypeStruct(shape, volume.dtype)] * count for shape, count in zip(shapes, turns)
    ]
    vectors = pl.BlockSpec(memory_space=pltpu.VMEM)
    out_shape = [
        jax.ShapeDtypeStruct(volume.shape, volume.dtype),
        jax.ShapeDtypeStruct((4 * lines.shape[0], LANES), jnp.float32),
        *faces,
    ]
    return pl.pallas_call(
        functools.partial(
            prepare_kernel, optical=float(-2.0 / depth_total * NORM**2 * np.log2(np.e))
        ),
        in_specs=[pl.BlockSpec(memory_space=pltpu.SMEM), pl.BlockSpec(memory_space=pltpu.HBM)]
        + [vectors] * 3,
        out_specs=jax.tree.map(lambda _: vectors, out_shape),
        out_shape=out_shape,
        scratch_shapes=[pltpu.SemaphoreType.DMA((4 if slices % 4 == 0 else 1,))],
        compiler_params=pltpu.CompilerParams(vmem_limit_bytes=48 * 2**20),
    )(odd, volume, lines, tf_color, tf_opacity.reshape(1, knot_count))


def march_kernel(
    ids_ref,
    odd_ref,
    stencil_ref,
    table_ref,
    cells_ref,
    depth_refs,
    line_refs,
    ends_ref,
    out_ref,
    parts_ref,
    sides_ref,
    *,
    tile,
    knot_count,
):
    slices, height, width = cells_ref.shape
    lane = lax.broadcasted_iota(jnp.int16, (tile, LANES), 1)
    ones = jnp.ones((PACK, width), cells_ref.dtype)
    halves = -(-knot_count // (2 * HALF))
    rest = width - LANES
    half_width = width // 2 if width % (2 * LANES) == 0 else width
    tables = [table_ref[start * HALF : start * HALF + HALF] for start in range(12 * halves)]

    def look_up(which, index, in_half):
        for half in range(halves):
            found = jnp.take_along_axis(
                tables[which * halves + half], index, axis=0, mode="promise_in_bounds"
            )
            value = found if half == 0 else jnp.where(in_half[half - 1], found, value)
        return value

    def shade(z, slot, row, column, state):
        lit, second, third, knot = (
            parts_ref[slot, pl.ds(part * tile + row, HALF), pl.ds(column, LANES)]
            for part in range(4)
        )
        knot = jnp.minimum(jnp.maximum(knot, -0.5), knot_count / 2 - 1.0)
        middle = jnp.round(knot)
        segment = middle.astype(jnp.int32)
        offset = knot - middle
        before_middle = offset < 0.0
        index = segment & (HALF - 1) if halves > 1 else segment
        in_half = [middle >= float(HALF * half) for half in range(1, halves)]
        inverse = lax.rsqrt((lit * lit + second * second) + (third * third + NORM * NORM))
        shading = jnp.abs(lit) * inverse + AMBIENT / DIFFUSE
        density = 1.2 / NORM**2 - inverse * inverse
        values = [
            look_up(3 * c, index, in_half)
            + offset
            * jnp.where(
                before_middle,
                look_up(3 * c + 1, index, in_half),
                look_up(3 * c + 2, index, in_half),
            )
            for c in range(4)
        ]
        kept = jnp.exp2(values[3] * density)
        if state is None:
            weight = (1.0 - kept) * shading
            return [value * weight for value in values[:3]] + [kept]
        through = state[3] * kept
        weight = (state[3] - through) * shading
        return [total + value * weight for total, value in zip(state, values[:3])] + [through]

    def one_tile(i, carry):
        place = ids_ref[i]
        start = pl.multiple_of(place * tile, tile)
        steps = ids_ref.shape[0] // out_ref.shape[0]
        group = i // steps
        target = pl.multiple_of((i - group * steps) * tile, tile)
        rows = pl.ds(start, tile)
        odd = [odd_ref[axis] == 1 for axis in range(2)]
        behind, ahead = (
            jnp.where(odd[0], depth_refs[a][rows, :], depth_refs[1 - a][rows, :]) for a in range(2)
        )
        for side, at_face, neighbour in (
            (0, place == 0, pl.ds(jnp.maximum(start - PACK, 0), PACK)),
            (1, start == height - tile, pl.ds(jnp.minimum(start + tile, height - PACK), PACK)),
        ):

            @pl.when(at_face)
            def _():
                lines = jnp.where(odd[1], line_refs[side][...], line_refs[1 - side][...])
                for z in range(slices):
                    sides_ref[side, z] = jnp.broadcast_to(lines[z : z + 1], (PACK, width))

            @pl.when(jnp.logical_not(at_face))
            def _():
                near = pl.ds(pl.multiple_of(neighbour.start, PACK), PACK)
                for z in range(slices):
                    sides_ref[side, z] = cells_ref[z, near, :]

        def gradients(z):
            cells = cells_ref[z, rows, :]
            before = cells_ref[z - 1, rows, :] if z > 0 else behind
            after = cells_ref[z + 1, rows, :] if z + 1 < slices else ahead
            right = pltpu.roll(cells, width - 1, 1)
            left = pltpu.roll(cells, 1, 1)
            ends = ends_ref[rows, :]
            ends = pltpu.roll(ends, LANES - 2 * z, 1) if z else ends
            right_end = jnp.where(lane == LANES - 1, ends, right[:, rest:])
            left_end = jnp.where(lane == 0, ends, left[:, :LANES])
            if rest:
                right_end = jnp.concatenate([right[:, :rest], right_end], axis=1)
                left_end = jnp.concatenate([left_end, left[:, LANES:]], axis=1)
            stacked = jnp.concatenate(
                [after, before, sides_ref[0, z], cells, sides_ref[1, z], right_end, left_end, ones],
                axis=0,
            )
            for column in range(0, width, half_width):
                parts_ref[z % SLOTS, :, pl.ds(column, half_width)] = jnp.dot(
                    stencil_ref[...],
                    stacked[:, column : column + half_width],
                    preferred_element_type=jnp.float32,
                )
                yield

        def shades(first):
            for column in range(0, width, LANES):
                for row in range(0, tile, HALF):
                    here = (pl.ds(target + row, HALF), pl.ds(column, LANES))
                    state = None if first == 0 else [out_ref[(group, c) + here] for c in range(4)]
                    for z in range(first, first + DEPTH):
                        state = shade(z, z % SLOTS, row, column, state)
                    for c in range(4):
                        out_ref[(group, c) + here] = state[c]
                    yield

        def later(first):
            for z in range(first, min(first + DEPTH, slices)):
                yield from gradients(z)

        for _ in later(0):
            pass
        for z in range(0, slices, DEPTH):
            work = list_steps(later(z + DEPTH), DEPTH * (width // half_width), shades(z), (tile // HALF) * (width // LANES))
            for _ in work:
                pass
        return carry

    lax.fori_loop(0, ids_ref.shape[0], one_tile, 0)


def list_steps(first, first_count, second, second_count):
    done = 0
    for step in range(second_count):
        while done * second_count <= step * first_count and done < first_count:
            next(first, None)
            done += 1
        next(second)
        yield
    for _ in first:
        pass


def march(volume, halos, ids, odd, tables, knot_count, tile, groups):
    slices, height, width = volume.shape
    depth, lines, ends = halos
    assert slices % DEPTH == 0
    matrix = jnp.asarray(stencil(tile, knot_count))
    count = ids.shape[0]
    scalars = pl.BlockSpec(memory_space=pltpu.SMEM)
    vectors = pl.BlockSpec(memory_space=pltpu.VMEM)
    return pl.pallas_call(
        functools.partial(march_kernel, tile=tile, knot_count=knot_count),
        in_specs=[scalars, scalars, vectors, vectors, vectors, [vectors] * 2, [vectors] * 2, vectors],
        out_specs=vectors,
        out_shape=jax.ShapeDtypeStruct((groups, 4, count // groups * tile, width), jnp.float32),
        scratch_shapes=[
            pltpu.VMEM((SLOTS, 4 * tile, width), jnp.float32),
            pltpu.VMEM((2, slices, PACK, width), volume.dtype),
        ],
        compiler_params=pltpu.CompilerParams(vmem_limit_bytes=48 * 2**20),
        cost_estimate=pl.CostEstimate(flops=1, transcendentals=0, bytes_accessed=1),
    )(ids, odd, matrix, tables, volume, depth, lines, ends)


def over(nearer, farther):
    through = nearer[3:]
    return jnp.concatenate([nearer[:3] + through * farther[:3], through * farther[3:]], axis=0)


def merged(own, other, side):
    nearer = jnp.where(side == 0, own, other)
    farther = jnp.where(side == 0, other, own)
    return over(nearer, farther)


def from_partner(value, axis, bit):
    pairs = [(source, source ^ (1 << bit)) for source in range(lax.axis_size(axis))]
    return lax.ppermute(value, axis, pairs)


def on_device(volume, tf_color, tf_opacity):
    view_count = lax.axis_size("view")
    position = lax.axis_index("view")
    slices, height, width = volume.shape
    knot_count = tf_color.shape[1]
    tile_rows = height // view_count
    tile = min(32, tile_rows)
    bits = view_count.bit_length() - 1
    group_bits = min(2, bits)
    groups = 1 << group_bits
    per_group = view_count // groups

    odd = jnp.stack([lax.axis_index(axis) % 2 for axis in AXES])
    cells, tables, *faces = prepare(volume, tf_color, tf_opacity, odd, slices * view_count)
    depth, lines, ends = (exchange(face, axis) for face, axis in zip(faces, AXES))
    depth, lines = (
        found if len(found) == 2 else found + [jnp.zeros_like(found[0])] for found in (depth, lines)
    )
    halos = (depth, lines, sum(ends[1:], ends[0]))

    steps = tile_rows // tile

    def march_groups(distances, after=None):
        blocks = np.arange(per_group) * groups
        places = jnp.stack([blocks + (position % groups ^ distance) for distance in distances])
        ids = (places[..., None] * steps + np.arange(steps)).reshape(-1).astype(jnp.int32)
        if after is not None:
            ids, _ = lax.optimization_barrier((ids, after))
        return march(cells, halos, ids, odd, tables, knot_count, tile, len(distances))

    side = [position >> bit & 1 for bit in range(bits)]
    if groups == 4:
        (far,) = march_groups([3])
        far_received = from_partner(far, "view", 0)
        (near,) = march_groups([2], far)
        sent = merged(near, far_received, side[0])
        far, near = march_groups([1, 0], sent)
        received = from_partner(sent, "view", 1)
        image = merged(merged(near, from_partner(far, "view", 0), side[0]), received, side[1])
    elif groups == 2:
        far, near = march_groups([1, 0])
        image = merged(near, from_partner(far, "view", 0), side[0])
    else:
        (image,) = march_groups([0])
    image = image.reshape((4,) + (2,) * (bits - group_bits) + (tile_rows, width))
    for bit in range(group_bits, bits):
        axis = bits - bit
        kept = lax.dynamic_index_in_dim(image, side[bit], axis, keepdims=False)
        sent = lax.dynamic_index_in_dim(image, 1 - side[bit], axis, keepdims=False)
        image = merged(kept, from_partner(sent, "view", bit), side[bit])
    image = jnp.concatenate([image[:3], 1.0 - image[3:]], axis=0)
    return image.reshape(4, 1, tile_rows, width)


def solution(mesh):
    placed = (P("view", "row", "col"), P(), P())
    return jax.shard_map(
        on_device,
        mesh=mesh,
        in_specs=placed,
        out_specs=P(None, "view", "row", "col"),
        check_vma=False,
    )
```

```python
import functools

import jax
import jax.numpy as jnp
import numpy as np
from jax import lax
from jax.experimental import pallas as pl
from jax.experimental.pallas import tpu as pltpu
from jax.sharding import PartitionSpec as P

BASIS = ((12.0, 15.0, 16.0), (-20.0, 0.0, 15.0), (9.0, -20.0, 12.0))
NORM = 25.0
VALUE_LOW = -3.0
VALUE_HIGH = 3.0
AMBIENT = 0.35
DIFFUSE = 0.65
LANES = 128
PACK = 16
HALF = 8
AXES = ("view", "row", "col")
DEPTH = 2
SLOTS = 4
CODE_SCALE = 240.0
CODE_SHIFT = 120.0
SCALARS = pl.BlockSpec(memory_space=pltpu.SMEM)
VECTORS = pl.BlockSpec(memory_space=pltpu.VMEM)


def stencil(tile, knot_count):
    scale = (knot_count - 1) / (VALUE_HIGH - VALUE_LOW)
    width = 5 * tile + 3 * PACK
    after, before, above, centre, below, right, left, one = np.cumsum(
        [0, tile, tile, PACK, tile, PACK, tile, tile]
    )
    matrix = np.zeros((4 * tile, width), np.float32)
    for row in range(tile):
        for part, (along_z, along_y, along_x) in enumerate(BASIS):
            line = matrix[part * tile + row]
            line[after + row] += along_z / 2
            line[before + row] -= along_z / 2
            line[centre + row + 1 if row + 1 < tile else below] += along_y / 2
            line[centre + row - 1 if row > 0 else above + PACK - 1] -= along_y / 2
            line[right + row] += along_x / 2
            line[left + row] -= along_x / 2
        line = matrix[3 * tile + row]
        line[centre + row] = scale / 2
        line[one] = -VALUE_LOW * scale / 2 - 0.5
    rounded = matrix.astype(jnp.bfloat16)
    assert np.array_equal(rounded.astype(np.float32), matrix)
    return rounded


def exchange(faces, axis):
    count = lax.axis_size(axis)
    received = []
    for start, face in enumerate(faces):
        pairs = [(i, i + 1) for i in range(start, count - 1, 2)]
        both = pairs + [(j, i) for i, j in pairs]
        received.append(lax.ppermute(face, axis, both) if both else jnp.zeros_like(face))
    return received


def segment_lines(knot_count):
    segments = (knot_count + 1) // 2
    rows = -(-segments // HALF) * HALF
    lines = np.zeros((3, rows, knot_count), np.float32)
    for segment in range(segments):
        left, middle, right = (min(2 * segment + i, knot_count - 1) for i in range(3))
        lines[0, segment, middle] += 1.0
        lines[1, segment, middle] += 2.0
        lines[1, segment, left] -= 2.0
        lines[2, segment, right] += 2.0
        lines[2, segment, middle] -= 2.0
    return lines.reshape(3 * rows, knot_count)


def prepare_kernel(
    scalars_ref, volume_ref, cells_ref, depth_outs, row_outs, column_outs, arrived
):
    slices, height, width = cells_ref.shape
    chunks = arrived.shape[0]
    size = slices // chunks
    copies = [
        pltpu.make_async_copy(
            volume_ref.at[pl.ds(chunk * size, size)],
            cells_ref.at[pl.ds(chunk * size, size)],
            arrived.at[chunk],
        )
        for chunk in range(chunks)
    ]
    for copy in copies:
        copy.start()
    lane = lax.broadcasted_iota(jnp.int16, (height, LANES), 1)
    row = lax.broadcasted_iota(jnp.int16, (slices, width), 0)
    lines = [jnp.zeros((slices, width), cells_ref.dtype)] * len(row_outs)
    for chunk, copy in enumerate(copies):
        copy.wait()
        here = range(chunk * size, (chunk + 1) * size)
        for turn in range(len(row_outs)):
            is_first = scalars_ref[1] == 1 - turn
            for z in here:
                line = jnp.where(is_first, cells_ref[z, :1], cells_ref[z, height - 1 :])
                lines[turn] = jnp.where(
                    row == z, jnp.broadcast_to(line, (slices, width)), lines[turn]
                )

        def columns(turn, column, source, shift):
            found = (
                column_outs[turn][...] if chunk else jnp.zeros((height, LANES), cells_ref.dtype)
            )
            for z in here:
                target = (2 * z + shift) % LANES
                cells = cells_ref[z, :, pl.ds(column, LANES)]
                moved = pltpu.roll(cells, (target - source) % LANES, 1)
                found = jnp.where(lane == target, moved, found)
            column_outs[turn][...] = found

        for turn in range(len(column_outs)):
            pl.when(scalars_ref[2] == 1 - turn)(functools.partial(columns, turn, 0, 0, -1))
            pl.when(scalars_ref[2] == turn)(
                functools.partial(columns, turn, width - LANES, LANES - 1, 0)
            )
    for turn in range(len(row_outs)):
        row_outs[turn][...] = lines[turn]
    for turn in range(len(depth_outs)):
        face = jnp.where(scalars_ref[0] == 1 - turn, 0, slices - 1)
        depth_outs[turn][...] = cells_ref[face]


def prepare(volume, scalars):
    slices, height, width = volume.shape
    assert 2 * slices <= LANES
    shapes = [(height, width), (slices, width), (height, LANES)]
    turns = [2 if lax.axis_size(axis) > 2 else 1 for axis in AXES]
    out_shape = [jax.ShapeDtypeStruct(volume.shape, volume.dtype)] + [
        [jax.ShapeDtypeStruct(shape, volume.dtype)] * count for shape, count in zip(shapes, turns)
    ]
    return pl.pallas_call(
        prepare_kernel,
        in_specs=[pl.BlockSpec(memory_space=pltpu.SMEM), pl.BlockSpec(memory_space=pltpu.HBM)],
        out_specs=jax.tree.map(lambda _: VECTORS, out_shape),
        out_shape=out_shape,
        scratch_shapes=[pltpu.SemaphoreType.DMA((4 if slices % 4 == 0 else 1,))],
        compiler_params=pltpu.CompilerParams(vmem_limit_bytes=24 * 2**20),
    )(scalars, volume)


def march_kernel(
    scalars_ref,
    stencil_ref,
    lines_ref,
    color_ref,
    opacity_ref,
    cells_ref,
    depth_refs,
    line_refs,
    ends_ref,
    out_ref,
    parts_ref,
    sides_ref,
    *,
    first_id,
    count,
    tile,
    optical,
):
    slices, height, width = cells_ref.shape
    lane = lax.broadcasted_iota(jnp.int16, (tile, LANES), 1)
    ones = jnp.ones((PACK, width), cells_ref.dtype)
    knot_count = color_ref.shape[1]
    halves = -(-knot_count // (2 * HALF))
    rest = width - LANES
    half_width = width // 2 if width % (2 * LANES) == 0 else width
    tables = []
    for channel in range(4):
        knots = (
            color_ref[channel : channel + 1] * DIFFUSE if channel < 3 else opacity_ref[...] * optical
        )
        values = jnp.sum(lines_ref[...] * knots, axis=1, keepdims=True)
        for start in range(0, values.shape[0], HALF):
            tables.append(jnp.broadcast_to(values[start : start + HALF], (HALF, LANES)))

    def look_up(which, index, in_half):
        for half in range(halves):
            found = jnp.take_along_axis(
                tables[which * halves + half], index, axis=0, mode="promise_in_bounds"
            )
            value = found if half == 0 else jnp.where(in_half[half - 1], found, value)
        return value

    def shade(z, slot, row, column, state):
        lit, second, third, knot = (
            parts_ref[slot, pl.ds(part * tile + row, HALF), pl.ds(column, LANES)]
            for part in range(4)
        )
        knot = jnp.minimum(jnp.maximum(knot, -0.5), knot_count / 2 - 1.0)
        middle = jnp.round(knot)
        segment = middle.astype(jnp.int32)
        offset = knot - middle
        before_middle = offset < 0.0
        index = segment & (HALF - 1) if halves > 1 else segment
        in_half = [middle >= float(HALF * half) for half in range(1, halves)]
        inverse = lax.rsqrt((lit * lit + second * second) + (third * third + NORM * NORM))
        shading = jnp.abs(lit) * inverse + AMBIENT / DIFFUSE
        density = 1.2 / NORM**2 - inverse * inverse
        values = [
            look_up(3 * c, index, in_half)
            + offset
            * jnp.where(
                before_middle,
                look_up(3 * c + 1, index, in_half),
                look_up(3 * c + 2, index, in_half),
            )
            for c in range(4)
        ]
        kept = jnp.exp2(values[3] * density)
        if state is None:
            weight = (1.0 - kept) * shading
            return [value * weight for value in values[:3]] + [kept]
        through = state[3] * kept
        weight = (state[3] - through) * shading
        return [total + value * weight for total, value in zip(state, values[:3])] + [through]

    def one_tile(i, carry):
        place = scalars_ref[first_id + i]
        start = pl.multiple_of(place * tile, tile)
        steps = count // out_ref.shape[0]
        group = i // steps
        target = pl.multiple_of((i - group * steps) * tile, tile)
        rows = pl.ds(start, tile)
        odd = [scalars_ref[axis] == 1 for axis in range(2)]
        behind, ahead = (
            jnp.where(odd[0], depth_refs[a][rows, :], depth_refs[1 - a][rows, :]) for a in range(2)
        )
        for side, at_face, neighbour in (
            (0, place == 0, pl.ds(jnp.maximum(start - PACK, 0), PACK)),
            (1, start == height - tile, pl.ds(jnp.minimum(start + tile, height - PACK), PACK)),
        ):

            @pl.when(at_face)
            def _():
                lines = jnp.where(odd[1], line_refs[side][...], line_refs[1 - side][...])
                for z in range(slices):
                    sides_ref[side, z] = jnp.broadcast_to(lines[z : z + 1], (PACK, width))

            @pl.when(jnp.logical_not(at_face))
            def _():
                near = pl.ds(pl.multiple_of(neighbour.start, PACK), PACK)
                for z in range(slices):
                    sides_ref[side, z] = cells_ref[z, near, :]

        def gradients(z):
            cells = cells_ref[z, rows, :]
            before = cells_ref[z - 1, rows, :] if z > 0 else behind
            after = cells_ref[z + 1, rows, :] if z + 1 < slices else ahead
            right = pltpu.roll(cells, width - 1, 1)
            left = pltpu.roll(cells, 1, 1)
            ends = ends_ref[rows, :]
            ends = pltpu.roll(ends, LANES - 2 * z, 1) if z else ends
            right_end = jnp.where(lane == LANES - 1, ends, right[:, rest:])
            left_end = jnp.where(lane == 0, ends, left[:, :LANES])
            if rest:
                right_end = jnp.concatenate([right[:, :rest], right_end], axis=1)
                left_end = jnp.concatenate([left_end, left[:, LANES:]], axis=1)
            stacked = jnp.concatenate(
                [after, before, sides_ref[0, z], cells, sides_ref[1, z], right_end, left_end, ones],
                axis=0,
            )
            for column in range(0, width, half_width):
                parts_ref[z % SLOTS, :, pl.ds(column, half_width)] = jnp.dot(
                    stencil_ref[...],
                    stacked[:, column : column + half_width],
                    preferred_element_type=jnp.float32,
                )
                yield

        def shades(first):
            for column in range(0, width, LANES):
                for row in range(0, tile, HALF):
                    here = (pl.ds(target + row, HALF), pl.ds(column, LANES))
                    state = None if first == 0 else [out_ref[(group, c) + here] for c in range(4)]
                    for z in range(first, first + DEPTH):
                        state = shade(z, z % SLOTS, row, column, state)
                    for c in range(4):
                        out_ref[(group, c) + here] = state[c]
                    yield

        def later(first):
            for z in range(first, min(first + DEPTH, slices)):
                yield from gradients(z)

        for _ in later(0):
            pass
        for z in range(0, slices, DEPTH):
            work = list_steps(later(z + DEPTH), DEPTH * (width // half_width), shades(z), (tile // HALF) * (width // LANES))
            for _ in work:
                pass
        return carry

    lax.fori_loop(0, count, one_tile, 0)


def list_steps(first, first_count, second, second_count):
    done = 0
    for step in range(second_count):
        while done * second_count <= step * first_count and done < first_count:
            next(first, None)
            done += 1
        next(second)
        yield
    for _ in first:
        pass


def march(cells, halos, scalars, first_id, count, groups, transfer, depth_total, tile):
    slices, height, width = cells.shape
    depth, lines, ends = halos
    assert slices % DEPTH == 0
    tf_color, tf_opacity = transfer
    knot_count = tf_color.shape[1]
    optical = float(-2.0 / depth_total * NORM**2 * np.log2(np.e))
    return pl.pallas_call(
        functools.partial(
            march_kernel, first_id=first_id, count=count, tile=tile, optical=optical
        ),
        in_specs=[SCALARS] + [VECTORS] * 5 + [[VECTORS] * 2, [VECTORS] * 2, VECTORS],
        out_specs=VECTORS,
        out_shape=jax.ShapeDtypeStruct((groups, 4, count // groups * tile, width), jnp.float32),
        scratch_shapes=[
            pltpu.VMEM((SLOTS, 4 * tile, width), jnp.float32),
            pltpu.VMEM((2, slices, PACK, width), cells.dtype),
        ],
        compiler_params=pltpu.CompilerParams(vmem_limit_bytes=24 * 2**20),
    )(
        scalars,
        jnp.asarray(stencil(tile, knot_count)),
        jnp.asarray(segment_lines(knot_count)),
        tf_color,
        tf_opacity.reshape(1, knot_count),
        cells,
        depth,
        lines,
        ends,
    )


def ordered_over(first, second, swapped):
    colours = [
        jnp.where(swapped, b, a) + jnp.where(swapped, second[3], first[3]) * jnp.where(swapped, a, b)
        for a, b in zip(first[:3], second[:3])
    ]
    return colours + [first[3] * second[3]]


def pair_kernel(scalars_ref, own_ref, other_ref, code_ref, *, side):
    own = [own_ref[0, c] for c in range(4)]
    other = [other_ref[0, c] for c in range(4)]
    merged = ordered_over(own, other, scalars_ref[side] == 1)
    for c in range(4):
        code_ref[c] = jnp.exp2(CODE_SCALE * merged[c] - CODE_SHIFT).astype(code_ref.dtype)


def last_kernel(scalars_ref, own_ref, other_ref, code_ref, out_ref, *, side, finish):
    rows = pl.ds(pl.multiple_of(pl.program_id(0) * out_ref.shape[1], HALF), out_ref.shape[1])
    own = [own_ref[0, c, rows] for c in range(4)]
    other = [other_ref[1, c, rows] for c in range(4)]
    coded = pl.ds(pl.multiple_of(pl.program_id(0) * out_ref.shape[1], PACK), out_ref.shape[1])
    far = [
        (jnp.log2(code_ref[c, coded].astype(jnp.float32)) + CODE_SHIFT) * (1.0 / CODE_SCALE)
        for c in range(4)
    ]
    pair = ordered_over(own, other, scalars_ref[side] == 1)
    merged = ordered_over(pair, far, scalars_ref[side + 1] == 1)
    for c in range(3):
        out_ref[c] = merged[c]
    out_ref[3] = 1.0 - merged[3] if finish else merged[3]


def merge_pair(scalars, own, other, side):
    return pl.pallas_call(
        functools.partial(pair_kernel, side=side),
        in_specs=[SCALARS, VECTORS, VECTORS],
        out_specs=VECTORS,
        out_shape=jax.ShapeDtypeStruct(own.shape[1:], jnp.bfloat16),
        compiler_params=pltpu.CompilerParams(vmem_limit_bytes=24 * 2**20),
    )(scalars, own, other)


def merge_last(scalars, own, other, code, side, finish):
    _, _, rows, width = own.shape
    steps = 2 if rows % (2 * PACK) == 0 else 1
    return pl.pallas_call(
        functools.partial(last_kernel, side=side, finish=finish),
        grid=(steps,),
        in_specs=[SCALARS, VECTORS, VECTORS, VECTORS],
        out_specs=pl.BlockSpec((4, rows // steps, width), lambda i: (0, i, 0)),
        out_shape=jax.ShapeDtypeStruct(own.shape[1:], jnp.float32),
        compiler_params=pltpu.CompilerParams(vmem_limit_bytes=24 * 2**20),
    )(scalars, own, other, code)


def over(nearer, farther):
    through = nearer[3:]
    return jnp.concatenate([nearer[:3] + through * farther[:3], through * farther[3:]], axis=0)


def merged(own, other, side):
    nearer = jnp.where(side == 0, own, other)
    farther = jnp.where(side == 0, other, own)
    return over(nearer, farther)


def from_partner(value, axis, bit):
    pairs = [(source, source ^ (1 << bit)) for source in range(lax.axis_size(axis))]
    return lax.ppermute(value, axis, pairs)


def on_device(volume, tf_color, tf_opacity):
    view_count = lax.axis_size("view")
    position = lax.axis_index("view")
    slices, height, width = volume.shape
    tile_rows = height // view_count
    tile = min(32, tile_rows)
    bits = view_count.bit_length() - 1
    group_bits = min(2, bits)
    groups = 1 << group_bits
    per_group = view_count // groups

    calls = {4: ([3, 1], [2], [0]), 2: ([1], [0]), 1: ([0],)}[groups]
    steps = tile_rows // tile
    count = per_group * steps
    blocks = (np.arange(per_group)[:, None] * groups * steps + np.arange(steps)).reshape(-1)
    first_side = len(AXES)
    first_id = first_side + bits
    scalars = jnp.concatenate(
        [
            jnp.stack(
                [lax.axis_index(axis) & 1 for axis in AXES]
                + [position >> bit & 1 for bit in range(bits)]
            )
        ]
        + [
            (position & (groups - 1) ^ distance) * steps + blocks
            for call in calls
            for distance in call
        ]
    ).astype(jnp.int32)

    volume = pltpu.with_memory_space_constraint(volume, pltpu.HBM)
    cells, *faces = prepare(volume, scalars)
    depth, lines, ends = (exchange(face, axis) for face, axis in zip(faces, AXES))
    depth, lines = (
        found if len(found) == 2 else found + [jnp.zeros_like(found[0])] for found in (depth, lines)
    )
    halos = (depth, lines, sum(ends[1:], ends[0]))

    def march_call(call, after=None):
        here = scalars
        if after is not None:
            here, _ = lax.optimization_barrier((scalars, after))
        start = first_id + count * sum(len(earlier) for earlier in calls[:call])
        return march(
            cells,
            halos,
            here,
            start,
            count * len(calls[call]),
            len(calls[call]),
            (tf_color, tf_opacity),
            slices * view_count,
            tile,
        )

    if groups == 4:
        far = march_call(0)
        received = from_partner(far, "view", 0)
        near = march_call(1, far)
        code = merge_pair(scalars, near, received, first_side)
        code_received = from_partner(code, "view", 1)
        near = march_call(2, code)
        image = merge_last(scalars, near, received, code_received, first_side, bits == 2)
    elif groups == 2:
        far = march_call(0)
        received = from_partner(far, "view", 0)
        image = merged(march_call(1, far)[0], received[0], position & 1)
    else:
        image = march_call(0)[0]
    if bits == 2:
        return image.reshape(4, 1, tile_rows, width)
    image = image.reshape((4,) + (2,) * (bits - group_bits) + (tile_rows, width))
    for bit in range(group_bits, bits):
        side = position >> bit & 1
        axis = bits - bit
        kept = lax.dynamic_index_in_dim(image, side, axis, keepdims=False)
        sent = lax.dynamic_index_in_dim(image, 1 - side, axis, keepdims=False)
        image = merged(kept, from_partner(sent, "view", bit), side)
    image = jnp.concatenate([image[:3], 1.0 - image[3:]], axis=0)
    return image.reshape(4, 1, tile_rows, width)


def solution(mesh):
    placed = (P("view", "row", "col"), P(), P())
    return jax.shard_map(
        on_device,
        mesh=mesh,
        in_specs=placed,
        out_specs=P(None, "view", "row", "col"),
        check_vma=False,
    )
```

```python
import functools
import itertools

import jax
import jax.numpy as jnp
import numpy as np
from jax import lax
from jax.experimental import pallas as pl
from jax.experimental.pallas import tpu as pltpu
from jax.sharding import PartitionSpec as P

BASIS = ((12.0, 15.0, 16.0), (-20.0, 0.0, 15.0), (9.0, -20.0, 12.0))
NORM = 25.0
VALUE_LOW = -3.0
VALUE_HIGH = 3.0
AMBIENT = 0.35
DIFFUSE = 0.65
LANES = 128
PACK = 16
HALF = 8
AXES = ("view", "row", "col")
DEPTH = 2
SLOTS = 4
CODE_SCALE = 240.0
CODE_SHIFT = 120.0
ALONG_SUBLANES = lax.GatherDimensionNumbers(
    offset_dims=(),
    collapsed_slice_dims=(0,),
    start_index_map=(0,),
    operand_batching_dims=(1,),
    start_indices_batching_dims=(1,),
)
SCALARS = pl.BlockSpec(memory_space=pltpu.SMEM)
VECTORS = pl.BlockSpec(memory_space=pltpu.VMEM)


def stencil(tile, knot_count):
    scale = (knot_count - 1) / (VALUE_HIGH - VALUE_LOW)
    width = 5 * tile + 3 * PACK
    after, before, above, centre, below, right, left, one = np.cumsum(
        [0, tile, tile, PACK, tile, PACK, tile, tile]
    )
    matrix = np.zeros((4 * tile, width), np.float32)
    for row in range(tile):
        for part, (along_z, along_y, along_x) in enumerate(BASIS):
            line = matrix[part * tile + row]
            line[after + row] += along_z / 2
            line[before + row] -= along_z / 2
            line[centre + row + 1 if row + 1 < tile else below] += along_y / 2
            line[centre + row - 1 if row > 0 else above + PACK - 1] -= along_y / 2
            line[right + row] += along_x / 2
            line[left + row] -= along_x / 2
        line = matrix[3 * tile + row]
        line[centre + row] = scale / 2
        line[one] = -VALUE_LOW * scale / 2 - 0.5
    rounded = matrix.astype(jnp.bfloat16)
    assert np.array_equal(rounded.astype(np.float32), matrix)
    return rounded


def exchange(faces, axis):
    count = lax.axis_size(axis)
    received = []
    for start, face in enumerate(faces):
        pairs = [(i, i + 1) for i in range(start, count - 1, 2)]
        both = pairs + [(j, i) for i, j in pairs]
        received.append(lax.ppermute(face, axis, both) if both else jnp.zeros_like(face))
    return received


def segment_lines(knot_count):
    segments = (knot_count + 1) // 2
    rows = -(-segments // HALF) * HALF
    lines = np.zeros((3, rows, knot_count), np.float32)
    for segment in range(segments):
        left, middle, right = (min(2 * segment + i, knot_count - 1) for i in range(3))
        lines[0, segment, middle] += 1.0
        lines[1, segment, middle] += 2.0
        lines[1, segment, left] -= 2.0
        lines[2, segment, right] += 2.0
        lines[2, segment, middle] -= 2.0
    return lines.reshape(3 * rows, knot_count)


def prepare_kernel(
    scalars_ref, volume_ref, cells_ref, depth_outs, row_outs, column_outs, arrived
):
    slices, height, width = cells_ref.shape
    chunks = arrived.shape[0]
    size = slices // chunks
    copies = [
        pltpu.make_async_copy(
            volume_ref.at[pl.ds(chunk * size, size)],
            cells_ref.at[pl.ds(chunk * size, size)],
            arrived.at[chunk],
        )
        for chunk in range(chunks)
    ]
    for copy in copies:
        copy.start()
    lane = lax.broadcasted_iota(jnp.int16, (height, LANES), 1)
    row = lax.broadcasted_iota(jnp.int16, (slices, width), 0)
    lines = [jnp.zeros((slices, width), cells_ref.dtype)] * len(row_outs)
    for chunk, copy in enumerate(copies):
        copy.wait()
        here = range(chunk * size, (chunk + 1) * size)
        for turn in range(len(row_outs)):
            is_first = scalars_ref[1] == 1 - turn
            for z in here:
                line = jnp.where(is_first, cells_ref[z, :1], cells_ref[z, height - 1 :])
                lines[turn] = jnp.where(
                    row == z, jnp.broadcast_to(line, (slices, width)), lines[turn]
                )

        def columns(turn, column, source, shift):
            found = (
                column_outs[turn][...] if chunk else jnp.zeros((height, LANES), cells_ref.dtype)
            )
            for z in here:
                target = (2 * z + shift) % LANES
                cells = cells_ref[z, :, pl.ds(column, LANES)]
                moved = pltpu.roll(cells, (target - source) % LANES, 1)
                found = jnp.where(lane == target, moved, found)
            column_outs[turn][...] = found

        for turn in range(len(column_outs)):
            pl.when(scalars_ref[2] == 1 - turn)(functools.partial(columns, turn, 0, 0, -1))
            pl.when(scalars_ref[2] == turn)(
                functools.partial(columns, turn, width - LANES, LANES - 1, 0)
            )
    for turn in range(len(row_outs)):
        row_outs[turn][...] = lines[turn]
    for turn in range(len(depth_outs)):
        face = jnp.where(scalars_ref[0] == 1 - turn, 0, slices - 1)
        depth_outs[turn][...] = cells_ref[face]


def prepare(volume, scalars):
    slices, height, width = volume.shape
    assert 2 * slices <= LANES
    shapes = [(height, width), (slices, width), (height, LANES)]
    turns = [2 if lax.axis_size(axis) > 2 else 1 for axis in AXES]
    out_shape = [jax.ShapeDtypeStruct(volume.shape, volume.dtype)] + [
        [jax.ShapeDtypeStruct(shape, volume.dtype)] * count for shape, count in zip(shapes, turns)
    ]
    return pl.pallas_call(
        prepare_kernel,
        in_specs=[pl.BlockSpec(memory_space=pltpu.SMEM), pl.BlockSpec(memory_space=pltpu.HBM)],
        out_specs=jax.tree.map(lambda _: VECTORS, out_shape),
        out_shape=out_shape,
        scratch_shapes=[pltpu.SemaphoreType.DMA((4 if slices % 4 == 0 else 1,))],
        compiler_params=pltpu.CompilerParams(vmem_limit_bytes=24 * 2**20),
    )(scalars, volume)


def march_kernel(
    scalars_ref,
    stencil_ref,
    lines_ref,
    color_ref,
    opacity_ref,
    cells_ref,
    depth_refs,
    line_refs,
    ends_ref,
    out_ref,
    parts_ref,
    sides_ref,
    *,
    first_id,
    count,
    tile,
    optical,
):
    slices, height, width = cells_ref.shape
    lane = lax.broadcasted_iota(jnp.int16, (tile, LANES), 1)
    ones = jnp.ones((PACK, width), cells_ref.dtype)
    knot_count = color_ref.shape[1]
    halves = -(-knot_count // (2 * HALF))
    rest = width - LANES
    half_width = width // 2 if width % (2 * LANES) == 0 else width
    tables = []
    for channel in range(4):
        knots = (
            color_ref[channel : channel + 1] * DIFFUSE if channel < 3 else opacity_ref[...] * optical
        )
        values = jnp.sum(lines_ref[...] * knots, axis=1, keepdims=True)
        for start in range(0, values.shape[0], HALF):
            tables.append(jnp.broadcast_to(values[start : start + HALF], (HALF, LANES)))

    def look_up(which, index, in_half):
        for half in range(halves):
            found = lax.gather(
                tables[which * halves + half],
                index[..., None],
                ALONG_SUBLANES,
                slice_sizes=(1, 1),
                mode=lax.GatherScatterMode.PROMISE_IN_BOUNDS,
            )
            value = found if half == 0 else jnp.where(in_half[half - 1], found, value)
        return value

    def shade(z, slot, row, column, state):
        lit, second, third, knot = (
            parts_ref[slot, pl.ds(part * tile + row, HALF), pl.ds(column, LANES)]
            for part in range(4)
        )
        knot = jnp.minimum(jnp.maximum(knot, -0.5), knot_count / 2 - 1.0)
        middle = jnp.round(knot)
        segment = middle.astype(jnp.int32)
        offset = knot - middle
        before_middle = offset < 0.0
        index = segment & (HALF - 1) if halves > 1 else segment
        in_half = [middle >= float(HALF * half) for half in range(1, halves)]
        inverse = lax.rsqrt((lit * lit + second * second) + (third * third + NORM * NORM))
        shading = jnp.abs(lit) * inverse + AMBIENT / DIFFUSE
        density = 1.2 / NORM**2 - inverse * inverse
        values = [
            look_up(3 * c, index, in_half)
            + offset
            * jnp.where(
                before_middle,
                look_up(3 * c + 1, index, in_half),
                look_up(3 * c + 2, index, in_half),
            )
            for c in range(4)
        ]
        kept = jnp.exp2(values[3] * density)
        if state is None:
            weight = (1.0 - kept) * shading
            return [value * weight for value in values[:3]] + [kept]
        through = state[3] * kept
        weight = (state[3] - through) * shading
        return [total + value * weight for total, value in zip(state, values[:3])] + [through]

    odd = [scalars_ref[axis] == 1 for axis in range(2)]
    for side in range(2):
        lines = jnp.where(odd[1], line_refs[side][...], line_refs[1 - side][...])
        for z in range(slices):
            sides_ref[side, z] = jnp.broadcast_to(lines[z : z + 1], (PACK, width))

    def gradients(i, z):
        start = pl.multiple_of(scalars_ref[first_id + i] * tile, tile)
        rows = pl.ds(start, tile)

        def across(side):
            return jnp.where(
                odd[0], depth_refs[side][rows, :], depth_refs[1 - side][rows, :]
            )

        def beside(side, at_face, near):
            near = pl.ds(pl.multiple_of(near, PACK), PACK)
            return jnp.where(at_face, sides_ref[side, z], cells_ref[z, near, :])

        cells = cells_ref[z, rows, :]
        before = cells_ref[z - 1, rows, :] if z > 0 else across(0)
        after = cells_ref[z + 1, rows, :] if z + 1 < slices else across(1)
        above = beside(0, start == 0, jnp.maximum(start - PACK, 0))
        below = beside(1, start == height - tile, jnp.minimum(start + tile, height - PACK))
        right = pltpu.roll(cells, width - 1, 1)
        left = pltpu.roll(cells, 1, 1)
        ends = ends_ref[rows, :]
        ends = pltpu.roll(ends, LANES - 2 * z, 1) if z else ends
        right_end = jnp.where(lane == LANES - 1, ends, right[:, rest:])
        left_end = jnp.where(lane == 0, ends, left[:, :LANES])
        if rest:
            right_end = jnp.concatenate([right[:, :rest], right_end], axis=1)
            left_end = jnp.concatenate([left_end, left[:, LANES:]], axis=1)
        stacked = jnp.concatenate(
            [after, before, above, cells, below, right_end, left_end, ones], axis=0
        )
        for column in range(0, width, half_width):
            parts_ref[z % SLOTS, :, pl.ds(column, half_width)] = jnp.dot(
                stencil_ref[...],
                stacked[:, column : column + half_width],
                preferred_element_type=jnp.float32,
            )
            yield

    def shades(i, first):
        group = i // steps
        target = pl.multiple_of((i - group * steps) * tile, tile)
        for column in range(0, width, LANES):
            for row in range(0, tile, HALF):
                here = (pl.ds(target + row, HALF), pl.ds(column, LANES))
                state = None if first == 0 else [out_ref[(group, c) + here] for c in range(4)]
                for z in range(first, first + DEPTH):
                    state = shade(z, z % SLOTS, row, column, state)
                for c in range(4):
                    out_ref[(group, c) + here] = state[c]
                yield

    def one_tile(i, carry):
        following = jnp.minimum(i + 1, count - 1)
        for z in range(0, slices, DEPTH):
            ahead = [
                gradients(i if later < slices else following, later % slices)
                for later in range(z + DEPTH, z + 2 * DEPTH)
            ]
            interleave(
                itertools.chain(*ahead),
                DEPTH * (width // half_width),
                shades(i, z),
                (tile // HALF) * (width // LANES),
            )
        return carry

    steps = count // out_ref.shape[0]
    for z in range(DEPTH):
        for _ in gradients(0, z):
            pass
    lax.fori_loop(0, count, one_tile, 0)


def interleave(first, first_count, second, second_count):
    done = 0
    for step in range(second_count):
        while done * second_count <= step * first_count and done < first_count:
            next(first, None)
            done += 1
        next(second)
    for _ in itertools.chain(first, second):
        pass


def march(cells, halos, scalars, first_id, count, groups, transfer, depth_total, tile):
    slices, height, width = cells.shape
    depth, lines, ends = halos
    assert slices % SLOTS == 0 and SLOTS == 2 * DEPTH
    tf_color, tf_opacity = transfer
    knot_count = tf_color.shape[1]
    optical = float(-2.0 / depth_total * NORM**2 * np.log2(np.e))
    return pl.pallas_call(
        functools.partial(
            march_kernel, first_id=first_id, count=count, tile=tile, optical=optical
        ),
        in_specs=[SCALARS] + [VECTORS] * 5 + [[VECTORS] * 2, [VECTORS] * 2, VECTORS],
        out_specs=VECTORS,
        out_shape=jax.ShapeDtypeStruct((groups, 4, count // groups * tile, width), jnp.float32),
        scratch_shapes=[
            pltpu.VMEM((SLOTS, 4 * tile, width), jnp.float32),
            pltpu.VMEM((2, slices, PACK, width), cells.dtype),
        ],
        compiler_params=pltpu.CompilerParams(vmem_limit_bytes=24 * 2**20),
    )(
        scalars,
        jnp.asarray(stencil(tile, knot_count)),
        jnp.asarray(segment_lines(knot_count)),
        tf_color,
        tf_opacity.reshape(1, knot_count),
        cells,
        depth,
        lines,
        ends,
    )


def ordered_over(first, second, swapped):
    colours = [
        jnp.where(swapped, b, a) + jnp.where(swapped, second[3], first[3]) * jnp.where(swapped, a, b)
        for a, b in zip(first[:3], second[:3])
    ]
    return colours + [first[3] * second[3]]


def pair_kernel(scalars_ref, own_ref, other_ref, code_ref, *, side):
    own = [own_ref[0, c] for c in range(4)]
    other = [other_ref[0, c] for c in range(4)]
    merged = ordered_over(own, other, scalars_ref[side] == 1)
    for c in range(4):
        code_ref[c] = jnp.exp2(CODE_SCALE * merged[c] - CODE_SHIFT).astype(code_ref.dtype)


def last_kernel(scalars_ref, own_ref, other_ref, code_ref, out_ref, *, side, finish):
    rows = pl.ds(pl.multiple_of(pl.program_id(0) * out_ref.shape[1], HALF), out_ref.shape[1])
    own = [own_ref[0, c, rows] for c in range(4)]
    other = [other_ref[1, c, rows] for c in range(4)]
    coded = pl.ds(pl.multiple_of(pl.program_id(0) * out_ref.shape[1], PACK), out_ref.shape[1])
    far = [
        (jnp.log2(code_ref[c, coded].astype(jnp.float32)) + CODE_SHIFT) * (1.0 / CODE_SCALE)
        for c in range(4)
    ]
    pair = ordered_over(own, other, scalars_ref[side] == 1)
    merged = ordered_over(pair, far, scalars_ref[side + 1] == 1)
    for c in range(3):
        out_ref[c] = merged[c]
    out_ref[3] = 1.0 - merged[3] if finish else merged[3]


def merge_pair(scalars, own, other, side):
    return pl.pallas_call(
        functools.partial(pair_kernel, side=side),
        in_specs=[SCALARS, VECTORS, VECTORS],
        out_specs=VECTORS,
        out_shape=jax.ShapeDtypeStruct(own.shape[1:], jnp.bfloat16),
        compiler_params=pltpu.CompilerParams(vmem_limit_bytes=24 * 2**20),
    )(scalars, own, other)


def merge_last(scalars, own, other, code, side, finish):
    _, _, rows, width = own.shape
    steps = 2 if rows % (2 * PACK) == 0 else 1
    return pl.pallas_call(
        functools.partial(last_kernel, side=side, finish=finish),
        grid=(steps,),
        in_specs=[SCALARS, VECTORS, VECTORS, VECTORS],
        out_specs=pl.BlockSpec((4, rows // steps, width), lambda i: (0, i, 0)),
        out_shape=jax.ShapeDtypeStruct(own.shape[1:], jnp.float32),
        compiler_params=pltpu.CompilerParams(vmem_limit_bytes=24 * 2**20),
    )(scalars, own, other, code)


def over(nearer, farther):
    through = nearer[3:]
    return jnp.concatenate([nearer[:3] + through * farther[:3], through * farther[3:]], axis=0)


def merged(own, other, side):
    nearer = jnp.where(side == 0, own, other)
    farther = jnp.where(side == 0, other, own)
    return over(nearer, farther)


def from_partner(value, axis, bit):
    pairs = [(source, source ^ (1 << bit)) for source in range(lax.axis_size(axis))]
    return lax.ppermute(value, axis, pairs)


def on_device(volume, tf_color, tf_opacity):
    view_count = lax.axis_size("view")
    position = lax.axis_index("view")
    slices, height, width = volume.shape
    tile_rows = height // view_count
    tile = min(32, tile_rows)
    bits = view_count.bit_length() - 1
    group_bits = min(2, bits)
    groups = 1 << group_bits
    per_group = view_count // groups

    calls = {4: ([3, 1], [2], [0]), 2: ([1], [0]), 1: ([0],)}[groups]
    steps = tile_rows // tile
    count = per_group * steps
    blocks = (np.arange(per_group)[:, None] * groups * steps + np.arange(steps)).reshape(-1)
    first_side = len(AXES)
    first_id = first_side + bits
    scalars = jnp.concatenate(
        [
            jnp.stack(
                [lax.axis_index(axis) & 1 for axis in AXES]
                + [position >> bit & 1 for bit in range(bits)]
            )
        ]
        + [
            (position & (groups - 1) ^ distance) * steps + blocks
            for call in calls
            for distance in call
        ]
    ).astype(jnp.int32)

    volume = pltpu.with_memory_space_constraint(volume, pltpu.HBM)
    cells, *faces = prepare(volume, scalars)
    depth, lines, ends = (exchange(face, axis) for face, axis in zip(faces, AXES))
    depth, lines = (
        found if len(found) == 2 else found + [jnp.zeros_like(found[0])] for found in (depth, lines)
    )
    halos = (depth, lines, sum(ends[1:], ends[0]))

    def march_call(call, after=None):
        here = scalars
        if after is not None:
            here, _ = lax.optimization_barrier((scalars, after))
        start = first_id + count * sum(len(earlier) for earlier in calls[:call])
        return march(
            cells,
            halos,
            here,
            start,
            count * len(calls[call]),
            len(calls[call]),
            (tf_color, tf_opacity),
            slices * view_count,
            tile,
        )

    if groups == 4:
        far = march_call(0)
        received = from_partner(far, "view", 0)
        near = march_call(1, far)
        code = merge_pair(scalars, near, received, first_side)
        code_received = from_partner(code, "view", 1)
        near = march_call(2, code)
        image = merge_last(scalars, near, received, code_received, first_side, bits == 2)
    elif groups == 2:
        far = march_call(0)
        received = from_partner(far, "view", 0)
        image = merged(march_call(1, far)[0], received[0], position & 1)
    else:
        image = march_call(0)[0]
    if bits == 2:
        return image.reshape(4, 1, tile_rows, width)
    image = image.reshape((4,) + (2,) * (bits - group_bits) + (tile_rows, width))
    for bit in range(group_bits, bits):
        side = position >> bit & 1
        axis = bits - bit
        kept = lax.dynamic_index_in_dim(image, side, axis, keepdims=False)
        sent = lax.dynamic_index_in_dim(image, 1 - side, axis, keepdims=False)
        image = merged(kept, from_partner(sent, "view", bit), side)
    image = jnp.concatenate([image[:3], 1.0 - image[3:]], axis=0)
    return image.reshape(4, 1, tile_rows, width)


def solution(mesh):
    placed = (P("view", "row", "col"), P(), P())
    return jax.shard_map(
        on_device,
        mesh=mesh,
        in_specs=placed,
        out_specs=P(None, "view", "row", "col"),
        check_vma=False,
    )
```

```python
import functools
import itertools

import jax
import jax.numpy as jnp
import numpy as np
from jax import lax
from jax.experimental import pallas as pl
from jax.experimental.pallas import tpu as pltpu
from jax.sharding import PartitionSpec as P

BASIS = ((12.0, 15.0, 16.0), (-20.0, 0.0, 15.0), (9.0, -20.0, 12.0))
NORM = 25.0
VALUE_LOW = -3.0
VALUE_HIGH = 3.0
AMBIENT = 0.35
DIFFUSE = 0.65
LANES = 128
PACK = 16
HALF = 8
AXES = ("view", "row", "col")
DEPTH = 2
SLOTS = 4
CODE_SCALE = 240.0
CODE_SHIFT = 120.0
ALONG_SUBLANES = lax.GatherDimensionNumbers(
    offset_dims=(),
    collapsed_slice_dims=(0,),
    start_index_map=(0,),
    operand_batching_dims=(1,),
    start_indices_batching_dims=(1,),
)
SCALARS = pl.BlockSpec(memory_space=pltpu.SMEM)
VECTORS = pl.BlockSpec(memory_space=pltpu.VMEM)
ANYWHERE = pl.BlockSpec(memory_space=pl.ANY)


def stencil(tile, knot_count):
    scale = (knot_count - 1) / (VALUE_HIGH - VALUE_LOW)
    width = 5 * tile + 3 * PACK
    after, before, above, centre, below, right, left, one = np.cumsum(
        [0, tile, tile, PACK, tile, PACK, tile, tile]
    )
    matrix = np.zeros((4 * tile, width), np.float32)
    for row in range(tile):
        for part, (along_z, along_y, along_x) in enumerate(BASIS):
            line = matrix[part * tile + row]
            line[after + row] += along_z / 2
            line[before + row] -= along_z / 2
            line[centre + row + 1 if row + 1 < tile else below] += along_y / 2
            line[centre + row - 1 if row > 0 else above + PACK - 1] -= along_y / 2
            line[right + row] += along_x / 2
            line[left + row] -= along_x / 2
        line = matrix[3 * tile + row]
        line[centre + row] = scale / 2
        line[one] = -VALUE_LOW * scale / 2 - 0.5
    rounded = matrix.astype(jnp.bfloat16)
    assert np.array_equal(rounded.astype(np.float32), matrix)
    return rounded


def exchange(faces, axis):
    count = lax.axis_size(axis)
    received = []
    for start, face in enumerate(faces):
        pairs = [(i, i + 1) for i in range(start, count - 1, 2)]
        both = pairs + [(j, i) for i, j in pairs]
        received.append(lax.ppermute(face, axis, both) if both else jnp.zeros_like(face))
    return received


def segment_lines(knot_count):
    segments = (knot_count + 1) // 2
    rows = -(-segments // HALF) * HALF
    lines = np.zeros((3, rows, knot_count), np.float32)
    for segment in range(segments):
        left, middle, right = (min(2 * segment + i, knot_count - 1) for i in range(3))
        lines[0, segment, middle] += 1.0
        lines[1, segment, middle] += 2.0
        lines[1, segment, left] -= 2.0
        lines[2, segment, right] += 2.0
        lines[2, segment, middle] -= 2.0
    return lines.reshape(3 * rows, knot_count)


def prepare_kernel(
    scalars_ref, volume_ref, cells_ref, depth_outs, row_outs, column_outs, arrived
):
    slices, height, width = cells_ref.shape
    chunks = arrived.shape[0]
    size = slices // chunks
    copies = [
        pltpu.make_async_copy(
            volume_ref.at[pl.ds(chunk * size, size)],
            cells_ref.at[pl.ds(chunk * size, size)],
            arrived.at[chunk],
        )
        for chunk in range(chunks)
    ]
    for copy in copies:
        copy.start()
    lane = lax.broadcasted_iota(jnp.int16, (height, LANES), 1)
    row = lax.broadcasted_iota(jnp.int16, (slices, width), 0)
    lines = [jnp.zeros((slices, width), cells_ref.dtype)] * len(row_outs)
    for chunk, copy in enumerate(copies):
        copy.wait()
        here = range(chunk * size, (chunk + 1) * size)
        for turn in range(len(row_outs)):
            is_first = scalars_ref[1] == 1 - turn
            for z in here:
                line = jnp.where(is_first, cells_ref[z, :1], cells_ref[z, height - 1 :])
                lines[turn] = jnp.where(
                    row == z, jnp.broadcast_to(line, (slices, width)), lines[turn]
                )

        def columns(turn, column, source, shift):
            found = (
                column_outs[turn][...] if chunk else jnp.zeros((height, LANES), cells_ref.dtype)
            )
            for z in here:
                target = (2 * z + shift) % LANES
                cells = cells_ref[z, :, pl.ds(column, LANES)]
                moved = pltpu.roll(cells, (target - source) % LANES, 1)
                found = jnp.where(lane == target, moved, found)
            column_outs[turn][...] = found

        for turn in range(len(column_outs)):
            pl.when(scalars_ref[2] == 1 - turn)(functools.partial(columns, turn, 0, 0, -1))
            pl.when(scalars_ref[2] == turn)(
                functools.partial(columns, turn, width - LANES, LANES - 1, 0)
            )
    for turn in range(len(row_outs)):
        row_outs[turn][...] = lines[turn]
    for turn in range(len(depth_outs)):
        face = jnp.where(scalars_ref[0] == 1 - turn, 0, slices - 1)
        depth_outs[turn][...] = cells_ref[face]


def prepare(volume, scalars):
    slices, height, width = volume.shape
    assert 2 * slices <= LANES
    shapes = [(height, width), (slices, width), (height, LANES)]
    turns = [2 if lax.axis_size(axis) > 2 else 1 for axis in AXES]
    out_shape = [jax.ShapeDtypeStruct(volume.shape, volume.dtype)] + [
        [jax.ShapeDtypeStruct(shape, volume.dtype)] * count for shape, count in zip(shapes, turns)
    ]
    return pl.pallas_call(
        prepare_kernel,
        in_specs=[pl.BlockSpec(memory_space=pltpu.SMEM), pl.BlockSpec(memory_space=pltpu.HBM)],
        out_specs=jax.tree.map(lambda _: VECTORS, out_shape),
        out_shape=out_shape,
        scratch_shapes=[pltpu.SemaphoreType.DMA((4 if slices % 4 == 0 else 1,))],
        compiler_params=pltpu.CompilerParams(vmem_limit_bytes=24 * 2**20),
    )(scalars, volume)


def march_kernel(*refs, first_id, count, tile, optical, with_lines, patch):
    scalars_ref, stencil_ref, lines_ref, color_ref, opacity_ref, cells_ref = refs[:6]
    depth_refs, ends_ref, refs = refs[6:8], refs[8], refs[9:]
    if with_lines:
        line_refs, refs = refs[:2], refs[2:]
    if patch:
        _, whole_ref, image_ref, parts_ref, sides_ref, copied = refs
    elif with_lines:
        image_ref, parts_ref, sides_ref = refs
    else:
        image_ref, parts_ref = refs
    per_group = image_ref.shape[2] // tile
    slices, height, width = cells_ref.shape
    lane = lax.broadcasted_iota(jnp.int16, (tile, LANES), 1)
    ones = jnp.ones((PACK, width), cells_ref.dtype)
    knot_count = color_ref.shape[1]
    halves = -(-knot_count // (2 * HALF))
    rest = width - LANES
    half_width = width // 2 if width % (2 * LANES) == 0 else width
    tables = []
    for channel in range(4):
        knots = (
            color_ref[channel : channel + 1] * DIFFUSE if channel < 3 else opacity_ref[...] * optical
        )
        values = jnp.sum(lines_ref[...] * knots, axis=1, keepdims=True)
        for start in range(0, values.shape[0], HALF):
            tables.append(jnp.broadcast_to(values[start : start + HALF], (HALF, LANES)))

    def look_up(which, index, in_half):
        for half in range(halves):
            found = lax.gather(
                tables[which * halves + half],
                index[..., None],
                ALONG_SUBLANES,
                slice_sizes=(1, 1),
                mode=lax.GatherScatterMode.PROMISE_IN_BOUNDS,
            )
            value = found if half == 0 else jnp.where(in_half[half - 1], found, value)
        return value

    def shade(z, slot, row, column, state):
        lit, second, third, knot = (
            parts_ref[slot, pl.ds(part * tile + row, HALF), pl.ds(column, LANES)]
            for part in range(4)
        )
        knot = jnp.minimum(jnp.maximum(knot, -0.5), knot_count / 2 - 1.0)
        middle = jnp.round(knot)
        segment = middle.astype(jnp.int32)
        offset = knot - middle
        before_middle = offset < 0.0
        index = segment & (HALF - 1) if halves > 1 else segment
        in_half = [middle >= float(HALF * half) for half in range(1, halves)]
        inverse = lax.rsqrt((lit * lit + second * second) + (third * third + NORM * NORM))
        shading = jnp.abs(lit) * inverse + AMBIENT / DIFFUSE
        density = 1.2 / NORM**2 - inverse * inverse
        values = [
            look_up(3 * c, index, in_half)
            + offset
            * jnp.where(
                before_middle,
                look_up(3 * c + 1, index, in_half),
                look_up(3 * c + 2, index, in_half),
            )
            for c in range(4)
        ]
        kept = jnp.exp2(values[3] * density)
        if state is None:
            weight = (1.0 - kept) * shading
            return [value * weight for value in values[:3]] + [kept]
        through = state[3] * kept
        weight = (state[3] - through) * shading
        return [total + value * weight for total, value in zip(state, values[:3])] + [through]

    odd = [scalars_ref[axis] == 1 for axis in range(2)]
    if with_lines:
        for side in range(2):
            lines = jnp.where(odd[1], line_refs[side][...], line_refs[1 - side][...])
            for z in range(slices):
                sides_ref[side, z] = jnp.broadcast_to(lines[z : z + 1], (PACK, width))

    def place(i):
        return scalars_ref[first_id + count + i]

    def gradients(i, z):
        start = pl.multiple_of(scalars_ref[first_id + i] * tile, tile)
        rows = pl.ds(start, tile)

        def across(side):
            return jnp.where(
                odd[0], depth_refs[side][rows, :], depth_refs[1 - side][rows, :]
            )

        def beside(side, at_face, near):
            inner = cells_ref[z, pl.ds(pl.multiple_of(near, PACK), PACK), :]
            return jnp.where(at_face, sides_ref[side, z], inner) if with_lines else inner

        cells = cells_ref[z, rows, :]
        before = cells_ref[z - 1, rows, :] if z > 0 else across(0)
        after = cells_ref[z + 1, rows, :] if z + 1 < slices else across(1)
        above = beside(0, start == 0, jnp.maximum(start - PACK, 0))
        below = beside(1, start == height - tile, jnp.minimum(start + tile, height - PACK))
        right = pltpu.roll(cells, width - 1, 1)
        left = pltpu.roll(cells, 1, 1)
        ends = ends_ref[rows, :]
        ends = pltpu.roll(ends, LANES - 2 * z, 1) if z else ends
        right_end = jnp.where(lane == LANES - 1, ends, right[:, rest:])
        left_end = jnp.where(lane == 0, ends, left[:, :LANES])
        if rest:
            right_end = jnp.concatenate([right[:, :rest], right_end], axis=1)
            left_end = jnp.concatenate([left_end, left[:, LANES:]], axis=1)
        stacked = jnp.concatenate(
            [after, before, above, cells, below, right_end, left_end, ones], axis=0
        )
        for column in range(0, width, half_width):
            parts_ref[z % SLOTS, :, pl.ds(column, half_width)] = jnp.dot(
                stencil_ref[...],
                stacked[:, column : column + half_width],
                preferred_element_type=jnp.float32,
            )
            yield

    def shades(i, first):
        group = 0 if patch else place(i) // per_group
        target = 0 if patch else pl.multiple_of((place(i) - group * per_group) * tile, tile)
        for column in range(0, width, LANES):
            for row in range(0, tile, HALF):
                here = (pl.ds(target + row, HALF), pl.ds(column, LANES))
                state = None if first == 0 else [image_ref[(group, c) + here] for c in range(4)]
                for z in range(first, first + DEPTH):
                    state = shade(z, z % SLOTS, row, column, state)
                for c in range(4):
                    image_ref[(group, c) + here] = state[c]
                yield

    def one_tile(i, carry):
        following = jnp.minimum(i + 1, count - 1)
        for z in range(0, slices, DEPTH):
            ahead = [
                gradients(i if later < slices else following, later % slices)
                for later in range(z + DEPTH, z + 2 * DEPTH)
            ]
            interleave(
                itertools.chain(*ahead),
                DEPTH * (width // half_width),
                shades(i, z),
                (tile // HALF) * (width // LANES),
            )
        return carry

    for z in range(DEPTH):
        for _ in gradients(0, z):
            pass
    lax.fori_loop(0, count, one_tile, 0)
    if patch:
        group = place(0) // (whole_ref.shape[2] // tile)
        rows = (place(0) - group * (whole_ref.shape[2] // tile)) * tile
        copy = pltpu.make_async_copy(
            image_ref.at[0], whole_ref.at[group, :, pl.ds(pl.multiple_of(rows, tile), tile)], copied
        )
        copy.start()
        copy.wait()


def interleave(first, first_count, second, second_count):
    done = 0
    for step in range(second_count):
        while done * second_count <= step * first_count and done < first_count:
            next(first, None)
            done += 1
        next(second)
    for _ in itertools.chain(first, second):
        pass


def march(cells, halos, scalars, first_id, count, image, transfer, depth_total, tile, partial=None):
    slices, height, width = cells.shape
    depth, ends, lines = halos
    assert slices % SLOTS == 0 and SLOTS == 2 * DEPTH
    tf_color, tf_opacity = transfer
    knot_count = tf_color.shape[1]
    optical = float(-2.0 / depth_total * NORM**2 * np.log2(np.e))
    groups, rows = image
    patch = partial is not None
    scratch = [pltpu.VMEM((SLOTS, 4 * tile, width), jnp.float32)]
    operands = [
        scalars,
        jnp.asarray(stencil(tile, knot_count)),
        jnp.asarray(segment_lines(knot_count)),
        tf_color,
        tf_opacity.reshape(1, knot_count),
        cells,
        *depth,
        ends,
    ]
    if lines is not None:
        operands += lines
        scratch.append(pltpu.VMEM((2, slices, PACK, width), cells.dtype))
    in_specs = [SCALARS] + [VECTORS] * (len(operands) - 1)
    if patch:
        operands.append(partial)
        in_specs.append(ANYWHERE)
        scratch = [pltpu.VMEM((1, 4, tile, width), jnp.float32)] + scratch
        scratch.append(pltpu.SemaphoreType.DMA)
    return pl.pallas_call(
        functools.partial(
            march_kernel,
            first_id=first_id,
            count=count,
            tile=tile,
            optical=optical,
            with_lines=lines is not None,
            patch=patch,
        ),
        in_specs=in_specs,
        out_specs=ANYWHERE if patch else VECTORS,
        out_shape=jax.ShapeDtypeStruct((groups, 4, rows, width), jnp.float32),
        input_output_aliases={len(operands) - 1: 0} if patch else {},
        scratch_shapes=scratch,
        compiler_params=pltpu.CompilerParams(vmem_limit_bytes=24 * 2**20),
    )(*operands)


def ordered_over(first, second, swapped):
    colours = [
        jnp.where(swapped, b, a) + jnp.where(swapped, second[3], first[3]) * jnp.where(swapped, a, b)
        for a, b in zip(first[:3], second[:3])
    ]
    return colours + [first[3] * second[3]]


def pair_kernel(scalars_ref, own_ref, other_ref, code_ref, *, side):
    own = [own_ref[0, c] for c in range(4)]
    other = [other_ref[0, c] for c in range(4)]
    merged = ordered_over(own, other, scalars_ref[side] == 1)
    for c in range(4):
        code_ref[c] = jnp.exp2(CODE_SCALE * merged[c] - CODE_SHIFT).astype(code_ref.dtype)


def last_kernel(scalars_ref, own_ref, other_ref, code_ref, out_ref, *, side, finish):
    rows = pl.ds(pl.multiple_of(pl.program_id(0) * out_ref.shape[1], HALF), out_ref.shape[1])
    own = [own_ref[0, c, rows] for c in range(4)]
    other = [other_ref[1, c, rows] for c in range(4)]
    coded = pl.ds(pl.multiple_of(pl.program_id(0) * out_ref.shape[1], PACK), out_ref.shape[1])
    far = [
        (jnp.log2(code_ref[c, coded].astype(jnp.float32)) + CODE_SHIFT) * (1.0 / CODE_SCALE)
        for c in range(4)
    ]
    pair = ordered_over(own, other, scalars_ref[side] == 1)
    merged = ordered_over(pair, far, scalars_ref[side + 1] == 1)
    for c in range(3):
        out_ref[c] = merged[c]
    out_ref[3] = 1.0 - merged[3] if finish else merged[3]


def merge_pair(scalars, own, other, side):
    return pl.pallas_call(
        functools.partial(pair_kernel, side=side),
        in_specs=[SCALARS, VECTORS, VECTORS],
        out_specs=VECTORS,
        out_shape=jax.ShapeDtypeStruct(own.shape[1:], jnp.bfloat16),
        compiler_params=pltpu.CompilerParams(vmem_limit_bytes=24 * 2**20),
    )(scalars, own, other)


def merge_last(scalars, own, other, code, side, finish):
    _, _, rows, width = own.shape
    steps = 2 if rows % (2 * PACK) == 0 else 1
    return pl.pallas_call(
        functools.partial(last_kernel, side=side, finish=finish),
        grid=(steps,),
        in_specs=[SCALARS, VECTORS, VECTORS, VECTORS],
        out_specs=pl.BlockSpec((4, rows // steps, width), lambda i: (0, i, 0)),
        out_shape=jax.ShapeDtypeStruct(own.shape[1:], jnp.float32),
        compiler_params=pltpu.CompilerParams(vmem_limit_bytes=24 * 2**20),
    )(scalars, own, other, code)


def over(nearer, farther):
    through = nearer[3:]
    return jnp.concatenate([nearer[:3] + through * farther[:3], through * farther[3:]], axis=0)


def merged(own, other, side):
    nearer = jnp.where(side == 0, own, other)
    farther = jnp.where(side == 0, other, own)
    return over(nearer, farther)


def from_partner(value, axis, bit):
    pairs = [(source, source ^ (1 << bit)) for source in range(lax.axis_size(axis))]
    return lax.ppermute(value, axis, pairs)


def on_device(volume, tf_color, tf_opacity):
    view_count = lax.axis_size("view")
    position = lax.axis_index("view")
    slices, height, width = volume.shape
    tile_rows = height // view_count
    tile = min(32, tile_rows)
    bits = view_count.bit_length() - 1
    group_bits = min(2, bits)
    groups = 1 << group_bits
    per_group = view_count // groups

    steps = tile_rows // tile
    count = per_group * steps
    blocks = (np.arange(per_group)[:, None] * groups * steps + np.arange(steps)).reshape(-1)
    place_in_group = position & (groups - 1)

    def tiles_of(*distances):
        return jnp.concatenate([(place_in_group ^ d) * steps + blocks for d in distances])

    def in_order(tiles):
        return [tiles, jnp.arange(tiles.shape[0])]

    if groups == 4:
        both = tiles_of(3, 1)
        last = 2 * count - 1
        missing = jnp.where(
            place_in_group & 1 == 1,
            jnp.where(place_in_group == 3, 0, count),
            jnp.where(place_in_group == 0, count - 1, last),
        )
        places = np.arange(2 * count)
        order = jnp.where(places == missing, last, places)
        order = order[:last]
        moved = jnp.sum(jnp.where(places == order[:, None], both, 0), axis=1)
        edge = jnp.sum(jnp.where(places == missing, both, 0))[None]
        calls = [[moved, order], [edge, missing[None]], in_order(tiles_of(2)), in_order(tiles_of(0))]
    elif groups == 2:
        calls = [in_order(tiles_of(1)), in_order(tiles_of(0))]
    else:
        calls = [in_order(tiles_of(0))]

    first_side = len(AXES)
    scalars = [lax.axis_index(axis) & 1 for axis in AXES] + [position >> i & 1 for i in range(bits)]
    first_ids = np.cumsum([len(scalars)] + [2 * call[0].shape[0] for call in calls])
    scalars = jnp.concatenate([jnp.stack(scalars)] + sum(calls, [])).astype(jnp.int32)

    volume = pltpu.with_memory_space_constraint(volume, pltpu.HBM)
    cells, *faces = prepare(volume, scalars)
    depth, lines, ends = (exchange(face, axis) for face, axis in zip(faces, AXES))
    depth, lines = (
        found if len(found) == 2 else found + [jnp.zeros_like(found[0])] for found in (depth, lines)
    )
    ends = sum(ends[1:], ends[0])

    def march_call(call, out_groups=1, after=None, partial=None, with_lines=True):
        here = scalars
        if after is not None:
            here, _ = lax.optimization_barrier((scalars, after))
        return march(
            cells,
            (depth, ends, lines if with_lines else None),
            here,
            int(first_ids[call]),
            calls[call][0].shape[0],
            (out_groups, count * tile),
            (tf_color, tf_opacity),
            slices * view_count,
            tile,
            partial,
        )

    if groups == 4:
        far = march_call(0, 2, with_lines=False)
        far = march_call(1, 2, partial=far)
        received = from_partner(far, "view", 0)
        near = march_call(2, after=far)
        code = merge_pair(scalars, near, received, first_side)
        code_received = from_partner(code, "view", 1)
        near = march_call(3, after=code)
        image = merge_last(scalars, near, received, code_received, first_side, bits == 2)
    elif groups == 2:
        far = march_call(0)
        received = from_partner(far, "view", 0)
        image = merged(march_call(1, after=far)[0], received[0], position & 1)
    else:
        image = march_call(0)[0]
    if bits == 2:
        return image.reshape(4, 1, tile_rows, width)
    image = image.reshape((4,) + (2,) * (bits - group_bits) + (tile_rows, width))
    for bit in range(group_bits, bits):
        side = position >> bit & 1
        axis = bits - bit
        kept = lax.dynamic_index_in_dim(image, side, axis, keepdims=False)
        sent = lax.dynamic_index_in_dim(image, 1 - side, axis, keepdims=False)
        image = merged(kept, from_partner(sent, "view", bit), side)
    image = jnp.concatenate([image[:3], 1.0 - image[3:]], axis=0)
    return image.reshape(4, 1, tile_rows, width)


def solution(mesh):
    placed = (P("view", "row", "col"), P(), P())
    return jax.shard_map(
        on_device,
        mesh=mesh,
        in_specs=placed,
        out_specs=P(None, "view", "row", "col"),
        check_vma=False,
    )
```

```python
import functools
import itertools

import jax
import jax.numpy as jnp
import numpy as np
from jax import lax
from jax.experimental import pallas as pl
from jax.experimental.pallas import tpu as pltpu
from jax.sharding import PartitionSpec as P

BASIS = ((12.0, 15.0, 16.0), (-20.0, 0.0, 15.0), (9.0, -20.0, 12.0))
NORM = 25.0
VALUE_LOW = -3.0
VALUE_HIGH = 3.0
AMBIENT = 0.35
DIFFUSE = 0.65
LANES = 128
PACK = 16
HALF = 8
AXES = ("view", "row", "col")
DEPTH = 2
SLOTS = 4
CODE_SCALE = 240.0
CODE_SHIFT = 120.0
ALONG_SUBLANES = lax.GatherDimensionNumbers(
    offset_dims=(),
    collapsed_slice_dims=(0,),
    start_index_map=(0,),
    operand_batching_dims=(1,),
    start_indices_batching_dims=(1,),
)
VECTORS = pl.BlockSpec(memory_space=pltpu.VMEM)
ANYWHERE = pl.BlockSpec(memory_space=pl.ANY)


def stencil(tile, knot_count):
    scale = (knot_count - 1) / (VALUE_HIGH - VALUE_LOW)
    width = 5 * tile + 3 * PACK
    after, before, above, centre, below, right, left, one = np.cumsum(
        [0, tile, tile, PACK, tile, PACK, tile, tile]
    )
    matrix = np.zeros((4 * tile, width), np.float32)
    for row in range(tile):
        for part, (along_z, along_y, along_x) in enumerate(BASIS):
            line = matrix[part * tile + row]
            line[after + row] += along_z / 2
            line[before + row] -= along_z / 2
            line[centre + row + 1 if row + 1 < tile else below] += along_y / 2
            line[centre + row - 1 if row > 0 else above + PACK - 1] -= along_y / 2
            line[right + row] += along_x / 2
            line[left + row] -= along_x / 2
        line = matrix[3 * tile + row]
        line[centre + row] = scale / 2
        line[one] = -VALUE_LOW * scale / 2 - 0.5
    rounded = matrix.astype(jnp.bfloat16)
    assert np.array_equal(rounded.astype(np.float32), matrix)
    return rounded


def exchange(faces, axis):
    count = lax.axis_size(axis)
    received = []
    for start, face in enumerate(faces):
        pairs = [(i, i + 1) for i in range(start, count - 1, 2)]
        both = pairs + [(j, i) for i, j in pairs]
        received.append(lax.ppermute(face, axis, both) if both else jnp.zeros_like(face))
    return received


def segment_lines(knot_count):
    segments = (knot_count + 1) // 2
    rows = -(-segments // HALF) * HALF
    lines = np.zeros((3, rows, knot_count), np.float32)
    for segment in range(segments):
        left, middle, right = (min(2 * segment + i, knot_count - 1) for i in range(3))
        lines[0, segment, middle] += 1.0
        lines[1, segment, middle] += 2.0
        lines[1, segment, left] -= 2.0
        lines[2, segment, right] += 2.0
        lines[2, segment, middle] -= 2.0
    return lines.reshape(3 * rows, knot_count)


def parities():
    return [lax.axis_index(axis) & 1 for axis in AXES]


def prepare_kernel(
    volume_ref, cells_ref, depth_outs, row_outs, column_outs, arrived
):
    slices, height, width = cells_ref.shape
    odd = parities()
    chunks = arrived.shape[0]
    size = slices // chunks
    copies = [
        pltpu.make_async_copy(
            volume_ref.at[pl.ds(chunk * size, size)],
            cells_ref.at[pl.ds(chunk * size, size)],
            arrived.at[chunk],
        )
        for chunk in range(chunks)
    ]
    for copy in copies:
        copy.start()
    lane = lax.broadcasted_iota(jnp.int16, (height, LANES), 1)
    row = lax.broadcasted_iota(jnp.int16, (slices, width), 0)
    lines = [jnp.zeros((slices, width), cells_ref.dtype)] * len(row_outs)
    for chunk, copy in enumerate(copies):
        copy.wait()
        here = range(chunk * size, (chunk + 1) * size)
        for turn in range(len(row_outs)):
            is_first = odd[1] == 1 - turn
            for z in here:
                line = jnp.where(is_first, cells_ref[z, :1], cells_ref[z, height - 1 :])
                lines[turn] = jnp.where(
                    row == z, jnp.broadcast_to(line, (slices, width)), lines[turn]
                )

        def columns(turn, column, source, shift):
            found = (
                column_outs[turn][...] if chunk else jnp.zeros((height, LANES), cells_ref.dtype)
            )
            for z in here:
                target = (2 * z + shift) % LANES
                cells = cells_ref[z, :, pl.ds(column, LANES)]
                moved = pltpu.roll(cells, (target - source) % LANES, 1)
                found = jnp.where(lane == target, moved, found)
            column_outs[turn][...] = found

        for turn in range(len(column_outs)):
            pl.when(odd[2] == 1 - turn)(functools.partial(columns, turn, 0, 0, -1))
            pl.when(odd[2] == turn)(
                functools.partial(columns, turn, width - LANES, LANES - 1, 0)
            )
    for turn in range(len(row_outs)):
        row_outs[turn][...] = lines[turn]
    for turn in range(len(depth_outs)):
        face = jnp.where(odd[0] == 1 - turn, 0, slices - 1)
        depth_outs[turn][...] = cells_ref[face]


def prepare(volume):
    slices, height, width = volume.shape
    assert 2 * slices <= LANES
    shapes = [(height, width), (slices, width), (height, LANES)]
    turns = [2 if lax.axis_size(axis) > 2 else 1 for axis in AXES]
    out_shape = [jax.ShapeDtypeStruct(volume.shape, volume.dtype)] + [
        [jax.ShapeDtypeStruct(shape, volume.dtype)] * count for shape, count in zip(shapes, turns)
    ]
    return pl.pallas_call(
        prepare_kernel,
        in_specs=[pl.BlockSpec(memory_space=pltpu.HBM)],
        out_specs=jax.tree.map(lambda _: VECTORS, out_shape),
        out_shape=out_shape,
        scratch_shapes=[pltpu.SemaphoreType.DMA((4 if slices % 4 == 0 else 1,))],
        compiler_params=pltpu.CompilerParams(vmem_limit_bytes=24 * 2**20),
    )(volume)


def march_kernel(*refs, tiles, count, tile, optical, with_lines, patch):
    stencil_ref, lines_ref, color_ref, opacity_ref, cells_ref = refs[:5]
    depth_refs, ends_ref, refs = refs[5:7], refs[7], refs[8:]
    if with_lines:
        line_refs, refs = refs[:2], refs[2:]
    if patch:
        _, whole_ref, image_ref, parts_ref, sides_ref, copied = refs
    elif with_lines:
        image_ref, parts_ref, sides_ref = refs
    else:
        image_ref, parts_ref = refs
    per_group = image_ref.shape[2] // tile
    slices, height, width = cells_ref.shape
    lane = lax.broadcasted_iota(jnp.int16, (tile, LANES), 1)
    ones = jnp.ones((PACK, width), cells_ref.dtype)
    knot_count = color_ref.shape[1]
    halves = -(-knot_count // (2 * HALF))
    rest = width - LANES
    half_width = width // 2 if width % (2 * LANES) == 0 else width
    tables = []
    for channel in range(4):
        knots = (
            color_ref[channel : channel + 1] * DIFFUSE if channel < 3 else opacity_ref[...] * optical
        )
        values = jnp.sum(lines_ref[...] * knots, axis=1, keepdims=True)
        for start in range(0, values.shape[0], HALF):
            tables.append(jnp.broadcast_to(values[start : start + HALF], (HALF, LANES)))

    def look_up(which, index, in_half):
        for half in range(halves):
            found = lax.gather(
                tables[which * halves + half],
                index[..., None],
                ALONG_SUBLANES,
                slice_sizes=(1, 1),
                mode=lax.GatherScatterMode.PROMISE_IN_BOUNDS,
            )
            value = found if half == 0 else jnp.where(in_half[half - 1], found, value)
        return value

    def shade(z, slot, row, column, state):
        lit, second, third, knot = (
            parts_ref[slot, pl.ds(part * tile + row, HALF), pl.ds(column, LANES)]
            for part in range(4)
        )
        knot = jnp.minimum(jnp.maximum(knot, -0.5), knot_count / 2 - 1.0)
        middle = jnp.round(knot)
        segment = middle.astype(jnp.int32)
        offset = knot - middle
        before_middle = offset < 0.0
        index = segment & (HALF - 1) if halves > 1 else segment
        in_half = [middle >= float(HALF * half) for half in range(1, halves)]
        inverse = lax.rsqrt((lit * lit + second * second) + (third * third + NORM * NORM))
        shading = jnp.abs(lit) * inverse + AMBIENT / DIFFUSE
        density = 1.2 / NORM**2 - inverse * inverse
        values = [
            look_up(3 * c, index, in_half)
            + offset
            * jnp.where(
                before_middle,
                look_up(3 * c + 1, index, in_half),
                look_up(3 * c + 2, index, in_half),
            )
            for c in range(4)
        ]
        kept = jnp.exp2(values[3] * density)
        if state is None:
            weight = (1.0 - kept) * shading
            return [value * weight for value in values[:3]] + [kept]
        through = state[3] * kept
        weight = (state[3] - through) * shading
        return [total + value * weight for total, value in zip(state, values[:3])] + [through]

    odd = [parity == 1 for parity in parities()[:2]]
    if with_lines:
        for side in range(2):
            lines = jnp.where(odd[1], line_refs[side][...], line_refs[1 - side][...])
            for z in range(slices):
                sides_ref[side, z] = jnp.broadcast_to(lines[z : z + 1], (PACK, width))

    def gradients(i, z):
        start = pl.multiple_of(tiles(i)[1] * tile, tile)
        rows = pl.ds(start, tile)

        def across(side):
            return jnp.where(
                odd[0], depth_refs[side][rows, :], depth_refs[1 - side][rows, :]
            )

        def beside(side, at_face, near):
            inner = cells_ref[z, pl.ds(pl.multiple_of(near, PACK), PACK), :]
            return jnp.where(at_face, sides_ref[side, z], inner) if with_lines else inner

        cells = cells_ref[z, rows, :]
        before = cells_ref[z - 1, rows, :] if z > 0 else across(0)
        after = cells_ref[z + 1, rows, :] if z + 1 < slices else across(1)
        above = beside(0, start == 0, jnp.maximum(start - PACK, 0))
        below = beside(1, start == height - tile, jnp.minimum(start + tile, height - PACK))
        right = pltpu.roll(cells, width - 1, 1)
        left = pltpu.roll(cells, 1, 1)
        ends = ends_ref[rows, :]
        ends = pltpu.roll(ends, LANES - 2 * z, 1) if z else ends
        right_end = jnp.where(lane == LANES - 1, ends, right[:, rest:])
        left_end = jnp.where(lane == 0, ends, left[:, :LANES])
        if rest:
            right_end = jnp.concatenate([right[:, :rest], right_end], axis=1)
            left_end = jnp.concatenate([left_end, left[:, LANES:]], axis=1)
        stacked = jnp.concatenate(
            [after, before, above, cells, below, right_end, left_end, ones], axis=0
        )
        for column in range(0, width, half_width):
            parts_ref[z % SLOTS, :, pl.ds(column, half_width)] = jnp.dot(
                stencil_ref[...],
                stacked[:, column : column + half_width],
                preferred_element_type=jnp.float32,
            )
            yield

    def shades(i, first):
        place = tiles(i)[0]
        group = 0 if patch else place // per_group
        target = 0 if patch else pl.multiple_of((place - group * per_group) * tile, tile)
        for column in range(0, width, LANES):
            for row in range(0, tile, HALF):
                here = (pl.ds(target + row, HALF), pl.ds(column, LANES))
                state = None if first == 0 else [image_ref[(group, c) + here] for c in range(4)]
                for z in range(first, first + DEPTH):
                    state = shade(z, z % SLOTS, row, column, state)
                for c in range(4):
                    image_ref[(group, c) + here] = state[c]
                yield

    def one_tile(i, carry):
        following = jnp.minimum(i + 1, count - 1)
        for z in range(0, slices, DEPTH):
            ahead = [
                gradients(i if later < slices else following, later % slices)
                for later in range(z + DEPTH, z + 2 * DEPTH)
            ]
            interleave(
                itertools.chain(*ahead),
                DEPTH * (width // half_width),
                shades(i, z),
                (tile // HALF) * (width // LANES),
            )
        return carry

    for z in range(DEPTH):
        for _ in gradients(0, z):
            pass
    lax.fori_loop(0, count, one_tile, 0)
    if patch:
        per_group = whole_ref.shape[2] // tile
        group = tiles(0)[0] // per_group
        rows = (tiles(0)[0] - group * per_group) * tile
        copy = pltpu.make_async_copy(
            image_ref.at[0], whole_ref.at[group, :, pl.ds(pl.multiple_of(rows, tile), tile)], copied
        )
        copy.start()
        copy.wait()


def interleave(first, first_count, second, second_count):
    done = 0
    for step in range(second_count):
        while done * second_count <= step * first_count and done < first_count:
            next(first, None)
            done += 1
        next(second)
    for _ in itertools.chain(first, second):
        pass


def march(cells, halos, tiles, count, image, transfer, depth_total, tile, partial=None):
    slices, height, width = cells.shape
    depth, ends, lines = halos
    assert slices % SLOTS == 0 and SLOTS == 2 * DEPTH
    tf_color, tf_opacity = transfer
    knot_count = tf_color.shape[1]
    optical = float(-2.0 / depth_total * NORM**2 * np.log2(np.e))
    groups, rows = image
    patch = partial is not None
    scratch = [pltpu.VMEM((SLOTS, 4 * tile, width), jnp.float32)]
    operands = [
        jnp.asarray(stencil(tile, knot_count)),
        jnp.asarray(segment_lines(knot_count)),
        tf_color,
        tf_opacity.reshape(1, knot_count),
        cells,
        *depth,
        ends,
    ]
    if lines is not None:
        operands += lines
        scratch.append(pltpu.VMEM((2, slices, PACK, width), cells.dtype))
    in_specs = [VECTORS] * len(operands)
    if patch:
        operands.append(partial)
        in_specs.append(ANYWHERE)
        scratch = [pltpu.VMEM((1, 4, tile, width), jnp.float32)] + scratch
        scratch.append(pltpu.SemaphoreType.DMA)
    return pl.pallas_call(
        functools.partial(
            march_kernel,
            tiles=tiles,
            count=count,
            tile=tile,
            optical=optical,
            with_lines=lines is not None,
            patch=patch,
        ),
        in_specs=in_specs,
        out_specs=ANYWHERE if patch else VECTORS,
        out_shape=jax.ShapeDtypeStruct((groups, 4, rows, width), jnp.float32),
        input_output_aliases={len(operands) - 1: 0} if patch else {},
        scratch_shapes=scratch,
        compiler_params=pltpu.CompilerParams(vmem_limit_bytes=24 * 2**20),
    )(*operands)


def ordered_over(first, second, swapped):
    colours = [
        jnp.where(swapped, b, a) + jnp.where(swapped, second[3], first[3]) * jnp.where(swapped, a, b)
        for a, b in zip(first[:3], second[:3])
    ]
    return colours + [first[3] * second[3]]


def pair_kernel(own_ref, other_ref, code_ref):
    own = [own_ref[0, c] for c in range(4)]
    other = [other_ref[0, c] for c in range(4)]
    merged = ordered_over(own, other, lax.axis_index("view") & 1 == 1)
    for c in range(4):
        code_ref[c] = jnp.exp2(CODE_SCALE * merged[c] - CODE_SHIFT).astype(code_ref.dtype)


def last_kernel(own_ref, other_ref, code_ref, out_ref, *, finish):
    rows = pl.ds(pl.multiple_of(pl.program_id(0) * out_ref.shape[1], HALF), out_ref.shape[1])
    own = [own_ref[0, c, rows] for c in range(4)]
    other = [other_ref[1, c, rows] for c in range(4)]
    coded = pl.ds(pl.multiple_of(pl.program_id(0) * out_ref.shape[1], PACK), out_ref.shape[1])
    far = [
        (jnp.log2(code_ref[c, coded].astype(jnp.float32)) + CODE_SHIFT) * (1.0 / CODE_SCALE)
        for c in range(4)
    ]
    pair = ordered_over(own, other, lax.axis_index("view") & 1 == 1)
    merged = ordered_over(pair, far, lax.axis_index("view") & 2 == 2)
    for c in range(3):
        out_ref[c] = merged[c]
    out_ref[3] = 1.0 - merged[3] if finish else merged[3]


def merge_pair(own, other):
    return pl.pallas_call(
        pair_kernel,
        in_specs=[VECTORS, VECTORS],
        out_specs=VECTORS,
        out_shape=jax.ShapeDtypeStruct(own.shape[1:], jnp.bfloat16),
        compiler_params=pltpu.CompilerParams(vmem_limit_bytes=24 * 2**20),
    )(own, other)


def merge_last(own, other, code, finish):
    _, _, rows, width = own.shape
    steps = 2 if rows % (2 * PACK) == 0 else 1
    return pl.pallas_call(
        functools.partial(last_kernel, finish=finish),
        grid=(steps,),
        in_specs=[VECTORS, VECTORS, VECTORS],
        out_specs=pl.BlockSpec((4, rows // steps, width), lambda i: (0, i, 0)),
        out_shape=jax.ShapeDtypeStruct(own.shape[1:], jnp.float32),
        compiler_params=pltpu.CompilerParams(vmem_limit_bytes=24 * 2**20),
    )(own, other, code)


def over(nearer, farther):
    through = nearer[3:]
    return jnp.concatenate([nearer[:3] + through * farther[:3], through * farther[3:]], axis=0)


def merged(own, other, side):
    nearer = jnp.where(side == 0, own, other)
    farther = jnp.where(side == 0, other, own)
    return over(nearer, farther)


def from_partner(value, axis, bit):
    pairs = [(source, source ^ (1 << bit)) for source in range(lax.axis_size(axis))]
    return lax.ppermute(value, axis, pairs)


def on_device(volume, tf_color, tf_opacity):
    view_count = lax.axis_size("view")
    position = lax.axis_index("view")
    slices, height, width = volume.shape
    tile_rows = height // view_count
    tile = min(32, tile_rows)
    bits = view_count.bit_length() - 1
    group_bits = min(2, bits)
    groups = 1 << group_bits
    per_group = view_count // groups

    steps = tile_rows // tile
    count = per_group * steps

    def tile_at(place, distances):
        at = lax.axis_index("view") & (groups - 1)
        group = place // count
        step = place - group * count
        block = step // steps
        distance = distances[0] + (distances[-1] - distances[0]) * group
        return ((at ^ distance) + block * groups) * steps + step - block * steps

    def all_tiles(distance):
        return lambda i: (i, tile_at(i, (distance,)))

    def missing_tile():
        at = lax.axis_index("view") & 3
        low = jnp.where(at == 3, 0, count)
        high = jnp.where(at == 0, count - 1, 2 * count - 1)
        return jnp.where(at & 1 == 1, low, high)

    def inner_tiles(i):
        place = jnp.where(i == missing_tile(), 2 * count - 1, i)
        return place, tile_at(place, (3, 1))

    def edge_tile(i):
        return missing_tile(), tile_at(missing_tile(), (3, 1))

    volume = pltpu.with_memory_space_constraint(volume, pltpu.HBM)
    cells, *faces = prepare(volume)
    depth, lines, ends = (exchange(face, axis) for face, axis in zip(faces, AXES))
    depth, lines = (
        found if len(found) == 2 else found + [jnp.zeros_like(found[0])] for found in (depth, lines)
    )
    ends = sum(ends[1:], ends[0])

    def march_call(tiles, tile_count, out_groups=1, after=None, partial=None, with_lines=True):
        here = ends
        if after is not None:
            here, _ = lax.optimization_barrier((ends, after))
        return march(
            cells,
            (depth, here, lines if with_lines else None),
            tiles,
            tile_count,
            (out_groups, count * tile),
            (tf_color, tf_opacity),
            slices * view_count,
            tile,
            partial,
        )

    if groups == 4:
        far = march_call(inner_tiles, 2 * count - 1, 2, with_lines=False)
        far = march_call(edge_tile, 1, 2, partial=far)
        received = from_partner(far, "view", 0)
        near = march_call(all_tiles(2), count, after=far)
        code = merge_pair(near, received)
        code_received = from_partner(code, "view", 1)
        near = march_call(all_tiles(0), count, after=code)
        image = merge_last(near, received, code_received, bits == 2)
    elif groups == 2:
        far = march_call(all_tiles(1), count)
        received = from_partner(far, "view", 0)
        image = merged(march_call(all_tiles(0), count, after=far)[0], received[0], position & 1)
    else:
        image = march_call(all_tiles(0), count)[0]
    if bits == 2:
        return image.reshape(4, 1, tile_rows, width)
    image = image.reshape((4,) + (2,) * (bits - group_bits) + (tile_rows, width))
    for bit in range(group_bits, bits):
        side = position >> bit & 1
        axis = bits - bit
        kept = lax.dynamic_index_in_dim(image, side, axis, keepdims=False)
        sent = lax.dynamic_index_in_dim(image, 1 - side, axis, keepdims=False)
        image = merged(kept, from_partner(sent, "view", bit), side)
    image = jnp.concatenate([image[:3], 1.0 - image[3:]], axis=0)
    return image.reshape(4, 1, tile_rows, width)


def solution(mesh):
    placed = (P("view", "row", "col"), P(), P())
    return jax.shard_map(
        on_device,
        mesh=mesh,
        in_specs=placed,
        out_specs=P(None, "view", "row", "col"),
        check_vma=False,
    )
```

```python
import functools
import itertools

import jax
import jax.numpy as jnp
import numpy as np
from jax import lax
from jax.experimental import pallas as pl
from jax.experimental.pallas import tpu as pltpu
from jax.sharding import PartitionSpec as P

BASIS = ((12.0, 15.0, 16.0), (-20.0, 0.0, 15.0), (9.0, -20.0, 12.0))
NORM = 25.0
VALUE_LOW = -3.0
VALUE_HIGH = 3.0
AMBIENT = 0.35
DIFFUSE = 0.65
LANES = 128
PACK = 16
HALF = 8
AXES = ("view", "row", "col")
DEPTH = 2
SLOTS = 4
CODE_SCALE = 240.0
CODE_SHIFT = 120.0
ALONG_SUBLANES = lax.GatherDimensionNumbers(
    offset_dims=(),
    collapsed_slice_dims=(0,),
    start_index_map=(0,),
    operand_batching_dims=(1,),
    start_indices_batching_dims=(1,),
)
VECTORS = pl.BlockSpec(memory_space=pltpu.VMEM)
ANYWHERE = pl.BlockSpec(memory_space=pl.ANY)


def stencil(tile, knot_count):
    scale = (knot_count - 1) / (VALUE_HIGH - VALUE_LOW)
    width = 5 * tile + 3 * PACK
    after, before, above, centre, below, right, left, one = np.cumsum(
        [0, tile, tile, PACK, tile, PACK, tile, tile]
    )
    matrix = np.zeros((4 * tile, width), np.float32)
    for row in range(tile):
        for part, (along_z, along_y, along_x) in enumerate(BASIS):
            line = matrix[part * tile + row]
            line[after + row] += along_z / 2
            line[before + row] -= along_z / 2
            line[centre + row + 1 if row + 1 < tile else below] += along_y / 2
            line[centre + row - 1 if row > 0 else above + PACK - 1] -= along_y / 2
            line[right + row] += along_x / 2
            line[left + row] -= along_x / 2
        line = matrix[3 * tile + row]
        line[centre + row] = scale / 2
        line[one] = -VALUE_LOW * scale / 2 - 0.5
    rounded = matrix.astype(jnp.bfloat16)
    assert np.array_equal(rounded.astype(np.float32), matrix)
    return rounded


def exchange(faces, axis):
    count = lax.axis_size(axis)
    received = []
    for start, face in enumerate(faces):
        pairs = [(i, i + 1) for i in range(start, count - 1, 2)]
        both = pairs + [(j, i) for i, j in pairs]
        received.append(lax.ppermute(face, axis, both) if both else jnp.zeros_like(face))
    return received


def segment_lines(knot_count):
    segments = (knot_count + 1) // 2
    rows = -(-segments // HALF) * HALF
    lines = np.zeros((3, rows, knot_count), np.float32)
    for segment in range(segments):
        left, middle, right = (min(2 * segment + i, knot_count - 1) for i in range(3))
        lines[0, segment, middle] += 1.0
        lines[1, segment, middle] += 2.0
        lines[1, segment, left] -= 2.0
        lines[2, segment, right] += 2.0
        lines[2, segment, middle] -= 2.0
    return lines.reshape(3 * rows, knot_count)


def parities():
    return [lax.axis_index(axis) & 1 for axis in AXES]


def prepare_kernel(volume_ref, depth_outs, row_outs, column_outs, lines_ref, columns_ref, arrived):
    slices, height, width = volume_ref.shape
    odd = parities()
    copies = {}
    for turn in range(len(column_outs)):
        start = pl.multiple_of(jnp.where(odd[2] == 1 - turn, 0, width - LANES), LANES)
        copies[2, turn] = (volume_ref.at[:, :, pl.ds(start, LANES)], columns_ref.at[turn])
    for turn in range(len(row_outs)):
        start = pl.multiple_of(jnp.where(odd[1] == 1 - turn, 0, height - PACK), PACK)
        copies[1, turn] = (volume_ref.at[:, pl.ds(start, PACK), :], lines_ref.at[turn])
    for turn in range(len(depth_outs)):
        face = jnp.where(odd[0] == 1 - turn, 0, slices - 1)
        copies[0, turn] = (volume_ref.at[face], depth_outs[turn])
    for i, (key, pair) in enumerate(copies.items()):
        copies[key] = pltpu.make_async_copy(*pair, arrived.at[i])
        copies[key].start()
    row = lax.broadcasted_iota(jnp.int16, (slices, width), 0)
    lane = lax.broadcasted_iota(jnp.int16, (height, LANES), 1)

    def columns(turn, source, shift):
        found = jnp.zeros((height, LANES), column_outs[turn].dtype)
        for z in range(slices):
            target = (2 * z + shift) % LANES
            moved = pltpu.roll(columns_ref[turn, z], (target - source) % LANES, 1)
            found = jnp.where(lane == target, moved, found)
        column_outs[turn][...] = found

    for turn in range(len(column_outs)):
        copies[2, turn].wait()
        pl.when(odd[2] == 1 - turn)(functools.partial(columns, turn, 0, -1))
        pl.when(odd[2] == turn)(functools.partial(columns, turn, LANES - 1, 0))
    for turn in range(len(row_outs)):
        copies[1, turn].wait()
        is_first = odd[1] == 1 - turn
        lines = jnp.zeros((slices, width), row_outs[turn].dtype)
        for z in range(slices):
            line = jnp.where(is_first, lines_ref[turn, z, :1], lines_ref[turn, z, PACK - 1 :])
            lines = jnp.where(row == z, jnp.broadcast_to(line, lines.shape), lines)
        row_outs[turn][...] = lines
    for turn in range(len(depth_outs)):
        copies[0, turn].wait()


def prepare(volume):
    slices, height, width = volume.shape
    assert 2 * slices <= LANES
    shapes = [(height, width), (slices, width), (height, LANES)]
    turns = [2 if lax.axis_size(axis) > 2 else 1 for axis in AXES]
    out_shape = [
        [jax.ShapeDtypeStruct(shape, volume.dtype)] * count for shape, count in zip(shapes, turns)
    ]
    return pl.pallas_call(
        prepare_kernel,
        in_specs=[pl.BlockSpec(memory_space=pltpu.HBM)],
        out_specs=jax.tree.map(lambda _: VECTORS, out_shape),
        out_shape=out_shape,
        scratch_shapes=[
            pltpu.VMEM((turns[1], slices, PACK, width), volume.dtype),
            pltpu.VMEM((turns[2], slices, height, LANES), volume.dtype),
            pltpu.SemaphoreType.DMA((sum(turns),)),
        ],
        compiler_params=pltpu.CompilerParams(vmem_limit_bytes=24 * 2**20),
    )(volume)


def march_kernel(*refs, tiles, count, tile, optical, with_lines, patch):
    stencil_ref, lines_ref, color_ref, opacity_ref, cells_ref = refs[:5]
    depth_refs, ends_ref, refs = refs[5:7], refs[7], refs[8:]
    if with_lines:
        line_refs, refs = refs[:2], refs[2:]
    if patch:
        _, whole_ref, image_ref, parts_ref, sides_ref, copied = refs
    elif with_lines:
        image_ref, parts_ref, sides_ref = refs
    else:
        image_ref, parts_ref = refs
    per_group = image_ref.shape[2] // tile
    slices, height, width = cells_ref.shape
    lane = lax.broadcasted_iota(jnp.int16, (tile, LANES), 1)
    ones = jnp.ones((PACK, width), cells_ref.dtype)
    knot_count = color_ref.shape[1]
    halves = -(-knot_count // (2 * HALF))
    rest = width - LANES
    half_width = width // 2 if width % (2 * LANES) == 0 else width
    tables = []
    for channel in range(4):
        knots = (
            color_ref[channel : channel + 1] * DIFFUSE if channel < 3 else opacity_ref[...] * optical
        )
        values = jnp.sum(lines_ref[...] * knots, axis=1, keepdims=True)
        for start in range(0, values.shape[0], HALF):
            tables.append(jnp.broadcast_to(values[start : start + HALF], (HALF, LANES)))

    def look_up(which, index, in_half):
        for half in range(halves):
            found = lax.gather(
                tables[which * halves + half],
                index[..., None],
                ALONG_SUBLANES,
                slice_sizes=(1, 1),
                mode=lax.GatherScatterMode.PROMISE_IN_BOUNDS,
            )
            value = found if half == 0 else jnp.where(in_half[half - 1], found, value)
        return value

    def shade(z, slot, row, column, state):
        lit, second, third, knot = (
            parts_ref[slot, pl.ds(part * tile + row, HALF), pl.ds(column, LANES)]
            for part in range(4)
        )
        knot = jnp.minimum(jnp.maximum(knot, -0.5), knot_count / 2 - 1.0)
        middle = jnp.round(knot)
        segment = middle.astype(jnp.int32)
        offset = knot - middle
        before_middle = offset < 0.0
        index = segment & (HALF - 1) if halves > 1 else segment
        in_half = [middle >= float(HALF * half) for half in range(1, halves)]
        inverse = lax.rsqrt((lit * lit + second * second) + (third * third + NORM * NORM))
        shading = jnp.abs(lit) * inverse + AMBIENT / DIFFUSE
        density = 1.2 / NORM**2 - inverse * inverse
        values = [
            look_up(3 * c, index, in_half)
            + offset
            * jnp.where(
                before_middle,
                look_up(3 * c + 1, index, in_half),
                look_up(3 * c + 2, index, in_half),
            )
            for c in range(4)
        ]
        kept = jnp.exp2(values[3] * density)
        if state is None:
            weight = (1.0 - kept) * shading
            return [value * weight for value in values[:3]] + [kept]
        through = state[3] * kept
        weight = (state[3] - through) * shading
        return [total + value * weight for total, value in zip(state, values[:3])] + [through]

    odd = [parity == 1 for parity in parities()[:2]]
    if with_lines:
        for side in range(2):
            lines = jnp.where(odd[1], line_refs[side][...], line_refs[1 - side][...])
            for z in range(slices):
                sides_ref[side, z] = jnp.broadcast_to(lines[z : z + 1], (PACK, width))

    def gradients(i, z):
        start = pl.multiple_of(tiles(i)[1] * tile, tile)
        rows = pl.ds(start, tile)

        def across(side):
            return jnp.where(
                odd[0], depth_refs[side][rows, :], depth_refs[1 - side][rows, :]
            )

        def beside(side, at_face, near):
            inner = cells_ref[z, pl.ds(pl.multiple_of(near, PACK), PACK), :]
            return jnp.where(at_face, sides_ref[side, z], inner) if with_lines else inner

        cells = cells_ref[z, rows, :]
        before = cells_ref[z - 1, rows, :] if z > 0 else across(0)
        after = cells_ref[z + 1, rows, :] if z + 1 < slices else across(1)
        above = beside(0, start == 0, jnp.maximum(start - PACK, 0))
        below = beside(1, start == height - tile, jnp.minimum(start + tile, height - PACK))
        right = pltpu.roll(cells, width - 1, 1)
        left = pltpu.roll(cells, 1, 1)
        ends = ends_ref[rows, :]
        ends = pltpu.roll(ends, LANES - 2 * z, 1) if z else ends
        right_end = jnp.where(lane == LANES - 1, ends, right[:, rest:])
        left_end = jnp.where(lane == 0, ends, left[:, :LANES])
        if rest:
            right_end = jnp.concatenate([right[:, :rest], right_end], axis=1)
            left_end = jnp.concatenate([left_end, left[:, LANES:]], axis=1)
        stacked = jnp.concatenate(
            [after, before, above, cells, below, right_end, left_end, ones], axis=0
        )
        for column in range(0, width, half_width):
            parts_ref[z % SLOTS, :, pl.ds(column, half_width)] = jnp.dot(
                stencil_ref[...],
                stacked[:, column : column + half_width],
                preferred_element_type=jnp.float32,
            )
            yield

    def shades(i, first):
        place = tiles(i)[0]
        group = 0 if patch else place // per_group
        target = 0 if patch else pl.multiple_of((place - group * per_group) * tile, tile)
        for column in range(0, width, LANES):
            for row in range(0, tile, HALF):
                here = (pl.ds(target + row, HALF), pl.ds(column, LANES))
                state = None if first == 0 else [image_ref[(group, c) + here] for c in range(4)]
                for z in range(first, first + DEPTH):
                    state = shade(z, z % SLOTS, row, column, state)
                for c in range(4):
                    image_ref[(group, c) + here] = state[c]
                yield

    def one_tile(i, carry):
        following = jnp.minimum(i + 1, count - 1)
        for z in range(0, slices, DEPTH):
            ahead = [
                gradients(i if later < slices else following, later % slices)
                for later in range(z + DEPTH, z + 2 * DEPTH)
            ]
            interleave(
                itertools.chain(*ahead),
                DEPTH * (width // half_width),
                shades(i, z),
                (tile // HALF) * (width // LANES),
            )
        return carry

    for z in range(DEPTH):
        for _ in gradients(0, z):
            pass
    lax.fori_loop(0, count, one_tile, 0)
    if patch:
        per_group = whole_ref.shape[2] // tile
        group = tiles(0)[0] // per_group
        rows = (tiles(0)[0] - group * per_group) * tile
        copy = pltpu.make_async_copy(
            image_ref.at[0], whole_ref.at[group, :, pl.ds(pl.multiple_of(rows, tile), tile)], copied
        )
        copy.start()
        copy.wait()


def interleave(first, first_count, second, second_count):
    done = 0
    for step in range(second_count):
        while done * second_count <= step * first_count and done < first_count:
            next(first, None)
            done += 1
        next(second)
    for _ in itertools.chain(first, second):
        pass


def march(cells, halos, tiles, count, image, transfer, depth_total, tile, partial=None):
    slices, height, width = cells.shape
    depth, ends, lines = halos
    assert slices % SLOTS == 0 and SLOTS == 2 * DEPTH
    tf_color, tf_opacity = transfer
    knot_count = tf_color.shape[1]
    optical = float(-2.0 / depth_total * NORM**2 * np.log2(np.e))
    groups, rows = image
    patch = partial is not None
    scratch = [pltpu.VMEM((SLOTS, 4 * tile, width), jnp.float32)]
    operands = [
        jnp.asarray(stencil(tile, knot_count)),
        jnp.asarray(segment_lines(knot_count)),
        tf_color,
        tf_opacity.reshape(1, knot_count),
        cells,
        *depth,
        ends,
    ]
    if lines is not None:
        operands += lines
        scratch.append(pltpu.VMEM((2, slices, PACK, width), cells.dtype))
    in_specs = [VECTORS] * len(operands)
    if patch:
        operands.append(partial)
        in_specs.append(ANYWHERE)
        scratch = [pltpu.VMEM((1, 4, tile, width), jnp.float32)] + scratch
        scratch.append(pltpu.SemaphoreType.DMA)
    return pl.pallas_call(
        functools.partial(
            march_kernel,
            tiles=tiles,
            count=count,
            tile=tile,
            optical=optical,
            with_lines=lines is not None,
            patch=patch,
        ),
        in_specs=in_specs,
        out_specs=ANYWHERE if patch else VECTORS,
        out_shape=jax.ShapeDtypeStruct((groups, 4, rows, width), jnp.float32),
        input_output_aliases={len(operands) - 1: 0} if patch else {},
        scratch_shapes=scratch,
        compiler_params=pltpu.CompilerParams(vmem_limit_bytes=24 * 2**20),
    )(*operands)


def ordered_over(first, second, swapped):
    colours = [
        jnp.where(swapped, b, a) + jnp.where(swapped, second[3], first[3]) * jnp.where(swapped, a, b)
        for a, b in zip(first[:3], second[:3])
    ]
    return colours + [first[3] * second[3]]


def pair_kernel(own_ref, other_ref, code_ref):
    own = [own_ref[0, c] for c in range(4)]
    other = [other_ref[0, c] for c in range(4)]
    merged = ordered_over(own, other, lax.axis_index("view") & 1 == 1)
    for c in range(4):
        code_ref[c] = jnp.exp2(CODE_SCALE * merged[c] - CODE_SHIFT).astype(code_ref.dtype)


def last_kernel(own_ref, other_ref, code_ref, out_ref, *, finish):
    rows = pl.ds(pl.multiple_of(pl.program_id(0) * out_ref.shape[1], HALF), out_ref.shape[1])
    own = [own_ref[0, c, rows] for c in range(4)]
    other = [other_ref[1, c, rows] for c in range(4)]
    coded = pl.ds(pl.multiple_of(pl.program_id(0) * out_ref.shape[1], PACK), out_ref.shape[1])
    far = [
        (jnp.log2(code_ref[c, coded].astype(jnp.float32)) + CODE_SHIFT) * (1.0 / CODE_SCALE)
        for c in range(4)
    ]
    pair = ordered_over(own, other, lax.axis_index("view") & 1 == 1)
    merged = ordered_over(pair, far, lax.axis_index("view") & 2 == 2)
    for c in range(3):
        out_ref[c] = merged[c]
    out_ref[3] = 1.0 - merged[3] if finish else merged[3]


def merge_pair(own, other):
    return pl.pallas_call(
        pair_kernel,
        in_specs=[VECTORS, VECTORS],
        out_specs=VECTORS,
        out_shape=jax.ShapeDtypeStruct(own.shape[1:], jnp.bfloat16),
        compiler_params=pltpu.CompilerParams(vmem_limit_bytes=24 * 2**20),
    )(own, other)


def merge_last(own, other, code, finish):
    _, _, rows, width = own.shape
    steps = 2 if rows % (2 * PACK) == 0 else 1
    return pl.pallas_call(
        functools.partial(last_kernel, finish=finish),
        grid=(steps,),
        in_specs=[VECTORS, VECTORS, VECTORS],
        out_specs=pl.BlockSpec((4, rows // steps, width), lambda i: (0, i, 0)),
        out_shape=jax.ShapeDtypeStruct(own.shape[1:], jnp.float32),
        compiler_params=pltpu.CompilerParams(vmem_limit_bytes=24 * 2**20),
    )(own, other, code)


def over(nearer, farther):
    through = nearer[3:]
    return jnp.concatenate([nearer[:3] + through * farther[:3], through * farther[3:]], axis=0)


def merged(own, other, side):
    nearer = jnp.where(side == 0, own, other)
    farther = jnp.where(side == 0, other, own)
    return over(nearer, farther)


def from_partner(value, axis, bit):
    pairs = [(source, source ^ (1 << bit)) for source in range(lax.axis_size(axis))]
    return lax.ppermute(value, axis, pairs)


def on_device(volume, tf_color, tf_opacity):
    view_count = lax.axis_size("view")
    position = lax.axis_index("view")
    slices, height, width = volume.shape
    tile_rows = height // view_count
    tile = min(32, tile_rows)
    bits = view_count.bit_length() - 1
    group_bits = min(2, bits)
    groups = 1 << group_bits
    per_group = view_count // groups

    steps = tile_rows // tile
    count = per_group * steps

    def tile_at(place, distances):
        at = lax.axis_index("view") & (groups - 1)
        group = place // count
        step = place - group * count
        block = step // steps
        distance = distances[0] + (distances[-1] - distances[0]) * group
        return ((at ^ distance) + block * groups) * steps + step - block * steps

    def all_tiles(distance):
        return lambda i: (i, tile_at(i, (distance,)))

    def missing_tile():
        at = lax.axis_index("view") & 3
        low = jnp.where(at == 3, 0, count)
        high = jnp.where(at == 0, count - 1, 2 * count - 1)
        return jnp.where(at & 1 == 1, low, high)

    def inner_tiles(i):
        place = jnp.where(i == missing_tile(), 2 * count - 1, i)
        return place, tile_at(place, (3, 1))

    def edge_tile(i):
        return missing_tile(), tile_at(missing_tile(), (3, 1))

    faces = prepare(pltpu.with_memory_space_constraint(volume, pltpu.HBM))
    depth, lines, ends = (exchange(face, axis) for face, axis in zip(faces, AXES))
    depth, lines = (
        found if len(found) == 2 else found + [jnp.zeros_like(found[0])] for found in (depth, lines)
    )
    ends = sum(ends[1:], ends[0])

    def march_call(tiles, tile_count, out_groups=1, after=None, partial=None, with_lines=True):
        here = ends
        if after is not None:
            here, _ = lax.optimization_barrier((ends, after))
        return march(
            volume,
            (depth, here, lines if with_lines else None),
            tiles,
            tile_count,
            (out_groups, count * tile),
            (tf_color, tf_opacity),
            slices * view_count,
            tile,
            partial,
        )

    if groups == 4:
        far = march_call(inner_tiles, 2 * count - 1, 2, with_lines=False)
        far = march_call(edge_tile, 1, 2, partial=far)
        received = from_partner(far, "view", 0)
        near = march_call(all_tiles(2), count, after=far)
        code = merge_pair(near, received)
        code_received = from_partner(code, "view", 1)
        near = march_call(all_tiles(0), count, after=code)
        image = merge_last(near, received, code_received, bits == 2)
    elif groups == 2:
        far = march_call(all_tiles(1), count)
        received = from_partner(far, "view", 0)
        image = merged(march_call(all_tiles(0), count, after=far)[0], received[0], position & 1)
    else:
        image = march_call(all_tiles(0), count)[0]
    if bits == 2:
        return image.reshape(4, 1, tile_rows, width)
    image = image.reshape((4,) + (2,) * (bits - group_bits) + (tile_rows, width))
    for bit in range(group_bits, bits):
        side = position >> bit & 1
        axis = bits - bit
        kept = lax.dynamic_index_in_dim(image, side, axis, keepdims=False)
        sent = lax.dynamic_index_in_dim(image, 1 - side, axis, keepdims=False)
        image = merged(kept, from_partner(sent, "view", bit), side)
    image = jnp.concatenate([image[:3], 1.0 - image[3:]], axis=0)
    return image.reshape(4, 1, tile_rows, width)


def solution(mesh):
    placed = (P("view", "row", "col"), P(), P())
    return jax.shard_map(
        on_device,
        mesh=mesh,
        in_specs=placed,
        out_specs=P(None, "view", "row", "col"),
        check_vma=False,
    )
```

```python
import functools
import itertools

import jax
import jax.numpy as jnp
import numpy as np
from jax import lax
from jax.experimental import pallas as pl
from jax.experimental.pallas import tpu as pltpu
from jax.sharding import PartitionSpec as P

BASIS = ((12.0, 15.0, 16.0), (-20.0, 0.0, 15.0), (9.0, -20.0, 12.0))
NORM = 25.0
VALUE_LOW = -3.0
VALUE_HIGH = 3.0
AMBIENT = 0.35
DIFFUSE = 0.65
LANES = 128
PACK = 16
HALF = 8
AXES = ("view", "row", "col")
DEPTH = 2
SLOTS = 4
CODE_SCALE = 240.0
CODE_SHIFT = 120.0
ALONG_SUBLANES = lax.GatherDimensionNumbers(
    offset_dims=(),
    collapsed_slice_dims=(0,),
    start_index_map=(0,),
    operand_batching_dims=(1,),
    start_indices_batching_dims=(1,),
)
VECTORS = pl.BlockSpec(memory_space=pltpu.VMEM)
ANYWHERE = pl.BlockSpec(memory_space=pl.ANY)


def stencil(tile, knot_count):
    scale = (knot_count - 1) / (VALUE_HIGH - VALUE_LOW)
    width = 5 * tile + 3 * PACK
    after, before, above, centre, below, right, left, one = np.cumsum(
        [0, tile, tile, PACK, tile, PACK, tile, tile]
    )
    matrix = np.zeros((4 * tile, width), np.float32)
    for row in range(tile):
        for part, (along_z, along_y, along_x) in enumerate(BASIS):
            line = matrix[part * tile + row]
            line[after + row] += along_z / 2
            line[before + row] -= along_z / 2
            line[centre + row + 1 if row + 1 < tile else below] += along_y / 2
            line[centre + row - 1 if row > 0 else above + PACK - 1] -= along_y / 2
            line[right + row] += along_x / 2
            line[left + row] -= along_x / 2
        line = matrix[3 * tile + row]
        line[centre + row] = scale / 2
        line[one] = -VALUE_LOW * scale / 2 - 0.5
    rounded = matrix.astype(jnp.bfloat16)
    assert np.array_equal(rounded.astype(np.float32), matrix)
    return rounded


def exchange(faces, axis):
    count = lax.axis_size(axis)
    received = []
    for start, face in enumerate(faces):
        pairs = [(i, i + 1) for i in range(start, count - 1, 2)]
        both = pairs + [(j, i) for i, j in pairs]
        received.append(lax.ppermute(face, axis, both) if both else jnp.zeros_like(face))
    return received


def segment_lines(knot_count, first):
    segment = first + lax.broadcasted_iota(jnp.int32, (HALF, knot_count), 0)
    knot = lax.broadcasted_iota(jnp.int32, (HALF, knot_count), 1)
    left, middle, right = (
        jnp.where(knot == jnp.minimum(2 * segment + i, knot_count - 1), 1.0, 0.0) for i in range(3)
    )
    return middle, 2.0 * (middle - left), 2.0 * (right - middle)


def parities():
    return [lax.axis_index(axis) & 1 for axis in AXES]


def prepare_kernel(
    volume_ref,
    stencil_ref,
    matrix_ref,
    depth_outs,
    row_outs,
    column_outs,
    lines_ref,
    columns_ref,
    arrived,
):
    slices, height, width = volume_ref.shape
    odd = parities()
    copies = {}
    for turn in range(len(column_outs)):
        start = pl.multiple_of(jnp.where(odd[2] == 1 - turn, 0, width - LANES), LANES)
        copies[2, turn] = (volume_ref.at[:, :, pl.ds(start, LANES)], columns_ref.at[turn])
    for turn in range(len(row_outs)):
        start = pl.multiple_of(jnp.where(odd[1] == 1 - turn, 0, height - PACK), PACK)
        copies[1, turn] = (volume_ref.at[:, pl.ds(start, PACK), :], lines_ref.at[turn])
    for turn in range(len(depth_outs)):
        face = jnp.where(odd[0] == 1 - turn, 0, slices - 1)
        copies[0, turn] = (volume_ref.at[face], depth_outs[turn])
    copies[None] = (stencil_ref, matrix_ref)
    for i, (key, pair) in enumerate(copies.items()):
        copies[key] = pltpu.make_async_copy(*pair, arrived.at[i])
        copies[key].start()
    row = lax.broadcasted_iota(jnp.int16, (slices, width), 0)
    lane = lax.broadcasted_iota(jnp.int16, (height, LANES), 1)

    def columns(turn, source, shift):
        found = jnp.zeros((height, LANES), column_outs[turn].dtype)
        for z in range(slices):
            target = (2 * z + shift) % LANES
            moved = pltpu.roll(columns_ref[turn, z], (target - source) % LANES, 1)
            found = jnp.where(lane == target, moved, found)
        column_outs[turn][...] = found

    for turn in range(len(column_outs)):
        copies[2, turn].wait()
        pl.when(odd[2] == 1 - turn)(functools.partial(columns, turn, 0, -1))
        pl.when(odd[2] == turn)(functools.partial(columns, turn, LANES - 1, 0))
    for turn in range(len(row_outs)):
        copies[1, turn].wait()
        is_first = odd[1] == 1 - turn
        lines = jnp.zeros((slices, width), row_outs[turn].dtype)
        for z in range(slices):
            line = jnp.where(is_first, lines_ref[turn, z, :1], lines_ref[turn, z, PACK - 1 :])
            lines = jnp.where(row == z, jnp.broadcast_to(line, lines.shape), lines)
        row_outs[turn][...] = lines
    for turn in range(len(depth_outs)):
        copies[0, turn].wait()
    copies[None].wait()


def prepare(volume, matrix):
    slices, height, width = volume.shape
    assert 2 * slices <= LANES
    shapes = [(height, width), (slices, width), (height, LANES)]
    turns = [2 if lax.axis_size(axis) > 2 else 1 for axis in AXES]
    out_shape = [jax.ShapeDtypeStruct(matrix.shape, matrix.dtype)] + [
        [jax.ShapeDtypeStruct(shape, volume.dtype)] * count for shape, count in zip(shapes, turns)
    ]
    return pl.pallas_call(
        prepare_kernel,
        in_specs=[pl.BlockSpec(memory_space=pltpu.HBM)] * 2,
        out_specs=jax.tree.map(lambda _: VECTORS, out_shape),
        out_shape=out_shape,
        scratch_shapes=[
            pltpu.VMEM((turns[1], slices, PACK, width), volume.dtype),
            pltpu.VMEM((turns[2], slices, height, LANES), volume.dtype),
            pltpu.SemaphoreType.DMA((sum(turns) + 1,)),
        ],
        compiler_params=pltpu.CompilerParams(vmem_limit_bytes=24 * 2**20),
    )(volume, matrix)


def march_kernel(*refs, tiles, count, tile, optical, with_lines, patch):
    stencil_ref, color_ref, opacity_ref, cells_ref = refs[:4]
    depth_refs, ends_ref, refs = refs[4:6], refs[6], refs[7:]
    if with_lines:
        line_refs, refs = refs[:2], refs[2:]
    if patch:
        _, whole_ref, image_ref, parts_ref, sides_ref, copied = refs
    elif with_lines:
        image_ref, parts_ref, sides_ref = refs
    else:
        image_ref, parts_ref = refs
    per_group = image_ref.shape[2] // tile
    slices, height, width = cells_ref.shape
    lane = lax.broadcasted_iota(jnp.int16, (tile, LANES), 1)
    ones = jnp.ones((PACK, width), cells_ref.dtype)
    knot_count = color_ref.shape[1]
    halves = -(-knot_count // (2 * HALF))
    rest = width - LANES
    half_width = width // 2 if width % (2 * LANES) == 0 else width
    tables = [None] * (12 * halves)
    for half in range(halves):
        for part, weights in enumerate(segment_lines(knot_count, HALF * half)):
            for channel in range(4):
                knots = (
                    color_ref[channel : channel + 1] * DIFFUSE
                    if channel < 3
                    else opacity_ref[...] * optical
                )
                values = jnp.sum(weights * knots, axis=1, keepdims=True)
                tables[(3 * channel + part) * halves + half] = jnp.broadcast_to(
                    values, (HALF, LANES)
                )

    def look_up(which, index, in_half):
        for half in range(halves):
            found = lax.gather(
                tables[which * halves + half],
                index[..., None],
                ALONG_SUBLANES,
                slice_sizes=(1, 1),
                mode=lax.GatherScatterMode.PROMISE_IN_BOUNDS,
            )
            value = found if half == 0 else jnp.where(in_half[half - 1], found, value)
        return value

    def shade(z, slot, row, column, state):
        lit, second, third, knot = (
            parts_ref[slot, pl.ds(part * tile + row, HALF), pl.ds(column, LANES)]
            for part in range(4)
        )
        knot = jnp.minimum(jnp.maximum(knot, -0.5), knot_count / 2 - 1.0)
        middle = jnp.round(knot)
        segment = middle.astype(jnp.int32)
        offset = knot - middle
        before_middle = offset < 0.0
        index = segment & (HALF - 1) if halves > 1 else segment
        in_half = [middle >= float(HALF * half) for half in range(1, halves)]
        inverse = lax.rsqrt((lit * lit + second * second) + (third * third + NORM * NORM))
        shading = jnp.abs(lit) * inverse + AMBIENT / DIFFUSE
        density = 1.2 / NORM**2 - inverse * inverse
        values = [
            look_up(3 * c, index, in_half)
            + offset
            * jnp.where(
                before_middle,
                look_up(3 * c + 1, index, in_half),
                look_up(3 * c + 2, index, in_half),
            )
            for c in range(4)
        ]
        kept = jnp.exp2(values[3] * density)
        if state is None:
            weight = (1.0 - kept) * shading
            return [value * weight for value in values[:3]] + [kept]
        through = state[3] * kept
        weight = (state[3] - through) * shading
        return [total + value * weight for total, value in zip(state, values[:3])] + [through]

    odd = [parity == 1 for parity in parities()[:2]]
    if with_lines:
        for side in range(2):
            lines = jnp.where(odd[1], line_refs[side][...], line_refs[1 - side][...])
            for z in range(slices):
                sides_ref[side, z] = jnp.broadcast_to(lines[z : z + 1], (PACK, width))

    def gradients(i, z):
        start = pl.multiple_of(tiles(i)[1] * tile, tile)
        rows = pl.ds(start, tile)

        def across(side):
            return jnp.where(
                odd[0], depth_refs[side][rows, :], depth_refs[1 - side][rows, :]
            )

        def beside(side, at_face, near):
            inner = cells_ref[z, pl.ds(pl.multiple_of(near, PACK), PACK), :]
            return jnp.where(at_face, sides_ref[side, z], inner) if with_lines else inner

        cells = cells_ref[z, rows, :]
        before = cells_ref[z - 1, rows, :] if z > 0 else across(0)
        after = cells_ref[z + 1, rows, :] if z + 1 < slices else across(1)
        above = beside(0, start == 0, jnp.maximum(start - PACK, 0))
        below = beside(1, start == height - tile, jnp.minimum(start + tile, height - PACK))
        right = pltpu.roll(cells, width - 1, 1)
        left = pltpu.roll(cells, 1, 1)
        ends = ends_ref[rows, :]
        ends = pltpu.roll(ends, LANES - 2 * z, 1) if z else ends
        right_end = jnp.where(lane == LANES - 1, ends, right[:, rest:])
        left_end = jnp.where(lane == 0, ends, left[:, :LANES])
        if rest:
            right_end = jnp.concatenate([right[:, :rest], right_end], axis=1)
            left_end = jnp.concatenate([left_end, left[:, LANES:]], axis=1)
        stacked = jnp.concatenate(
            [after, before, above, cells, below, right_end, left_end, ones], axis=0
        )
        for column in range(0, width, half_width):
            parts_ref[z % SLOTS, :, pl.ds(column, half_width)] = jnp.dot(
                stencil_ref[...],
                stacked[:, column : column + half_width],
                preferred_element_type=jnp.float32,
            )
            yield

    def shades(i, first):
        place = tiles(i)[0]
        group = 0 if patch else place // per_group
        target = 0 if patch else pl.multiple_of((place - group * per_group) * tile, tile)
        for column in range(0, width, LANES):
            for row in range(0, tile, HALF):
                here = (pl.ds(target + row, HALF), pl.ds(column, LANES))
                state = None if first == 0 else [image_ref[(group, c) + here] for c in range(4)]
                for z in range(first, first + DEPTH):
                    state = shade(z, z % SLOTS, row, column, state)
                for c in range(4):
                    image_ref[(group, c) + here] = state[c]
                yield

    def one_tile(i, carry):
        following = jnp.minimum(i + 1, count - 1)
        for z in range(0, slices, DEPTH):
            ahead = [
                gradients(i if later < slices else following, later % slices)
                for later in range(z + DEPTH, z + 2 * DEPTH)
            ]
            interleave(
                itertools.chain(*ahead),
                DEPTH * (width // half_width),
                shades(i, z),
                (tile // HALF) * (width // LANES),
            )
        return carry

    for z in range(DEPTH):
        for _ in gradients(0, z):
            pass
    lax.fori_loop(0, count, one_tile, 0)
    if patch:
        per_group = whole_ref.shape[2] // tile
        group = tiles(0)[0] // per_group
        rows = (tiles(0)[0] - group * per_group) * tile
        copy = pltpu.make_async_copy(
            image_ref.at[0], whole_ref.at[group, :, pl.ds(pl.multiple_of(rows, tile), tile)], copied
        )
        copy.start()
        copy.wait()


def interleave(first, first_count, second, second_count):
    done = 0
    for step in range(second_count):
        while done * second_count <= step * first_count and done < first_count:
            next(first, None)
            done += 1
        next(second)
    for _ in itertools.chain(first, second):
        pass


def march(cells, matrix, halos, tiles, count, image, transfer, depth_total, tile, partial=None):
    slices, height, width = cells.shape
    depth, ends, lines = halos
    assert slices % SLOTS == 0 and SLOTS == 2 * DEPTH
    tf_color, tf_opacity = transfer
    knot_count = tf_color.shape[1]
    optical = float(-2.0 / depth_total * NORM**2 * np.log2(np.e))
    groups, rows = image
    patch = partial is not None
    scratch = [pltpu.VMEM((SLOTS, 4 * tile, width), jnp.float32)]
    operands = [
        matrix,
        tf_color,
        tf_opacity.reshape(1, knot_count),
        cells,
        *depth,
        ends,
    ]
    if lines is not None:
        operands += lines
        scratch.append(pltpu.VMEM((2, slices, PACK, width), cells.dtype))
    in_specs = [VECTORS] * len(operands)
    if patch:
        operands.append(partial)
        in_specs.append(ANYWHERE)
        scratch = [pltpu.VMEM((1, 4, tile, width), jnp.float32)] + scratch
        scratch.append(pltpu.SemaphoreType.DMA)
    return pl.pallas_call(
        functools.partial(
            march_kernel,
            tiles=tiles,
            count=count,
            tile=tile,
            optical=optical,
            with_lines=lines is not None,
            patch=patch,
        ),
        in_specs=in_specs,
        out_specs=ANYWHERE if patch else VECTORS,
        out_shape=jax.ShapeDtypeStruct((groups, 4, rows, width), jnp.float32),
        input_output_aliases={len(operands) - 1: 0} if patch else {},
        scratch_shapes=scratch,
        compiler_params=pltpu.CompilerParams(vmem_limit_bytes=24 * 2**20),
    )(*operands)


def ordered_over(first, second, swapped):
    colours = [
        jnp.where(swapped, b, a) + jnp.where(swapped, second[3], first[3]) * jnp.where(swapped, a, b)
        for a, b in zip(first[:3], second[:3])
    ]
    return colours + [first[3] * second[3]]


def pair_kernel(own_ref, other_ref, code_ref):
    own = [own_ref[0, c] for c in range(4)]
    other = [other_ref[0, c] for c in range(4)]
    merged = ordered_over(own, other, lax.axis_index("view") & 1 == 1)
    for c in range(4):
        code_ref[c] = jnp.exp2(CODE_SCALE * merged[c] - CODE_SHIFT).astype(code_ref.dtype)


def last_kernel(own_ref, other_ref, code_ref, out_ref, *, finish):
    rows = pl.ds(pl.multiple_of(pl.program_id(0) * out_ref.shape[1], HALF), out_ref.shape[1])
    own = [own_ref[0, c, rows] for c in range(4)]
    other = [other_ref[1, c, rows] for c in range(4)]
    coded = pl.ds(pl.multiple_of(pl.program_id(0) * out_ref.shape[1], PACK), out_ref.shape[1])
    far = [
        (jnp.log2(code_ref[c, coded].astype(jnp.float32)) + CODE_SHIFT) * (1.0 / CODE_SCALE)
        for c in range(4)
    ]
    pair = ordered_over(own, other, lax.axis_index("view") & 1 == 1)
    merged = ordered_over(pair, far, lax.axis_index("view") & 2 == 2)
    for c in range(3):
        out_ref[c] = merged[c]
    out_ref[3] = 1.0 - merged[3] if finish else merged[3]


def merge_pair(own, other):
    return pl.pallas_call(
        pair_kernel,
        in_specs=[VECTORS, VECTORS],
        out_specs=VECTORS,
        out_shape=jax.ShapeDtypeStruct(own.shape[1:], jnp.bfloat16),
        compiler_params=pltpu.CompilerParams(vmem_limit_bytes=24 * 2**20),
    )(own, other)


def merge_last(own, other, code, finish):
    _, _, rows, width = own.shape
    steps = 2 if rows % (2 * PACK) == 0 else 1
    return pl.pallas_call(
        functools.partial(last_kernel, finish=finish),
        grid=(steps,),
        in_specs=[VECTORS, VECTORS, VECTORS],
        out_specs=pl.BlockSpec((4, rows // steps, width), lambda i: (0, i, 0)),
        out_shape=jax.ShapeDtypeStruct(own.shape[1:], jnp.float32),
        compiler_params=pltpu.CompilerParams(vmem_limit_bytes=24 * 2**20),
    )(own, other, code)


def over(nearer, farther):
    through = nearer[3:]
    return jnp.concatenate([nearer[:3] + through * farther[:3], through * farther[3:]], axis=0)


def merged(own, other, side):
    nearer = jnp.where(side == 0, own, other)
    farther = jnp.where(side == 0, other, own)
    return over(nearer, farther)


def from_partner(value, axis, bit):
    pairs = [(source, source ^ (1 << bit)) for source in range(lax.axis_size(axis))]
    return lax.ppermute(value, axis, pairs)


def on_device(volume, tf_color, tf_opacity):
    view_count = lax.axis_size("view")
    position = lax.axis_index("view")
    slices, height, width = volume.shape
    tile_rows = height // view_count
    tile = min(32, tile_rows)
    bits = view_count.bit_length() - 1
    group_bits = min(2, bits)
    groups = 1 << group_bits
    per_group = view_count // groups

    steps = tile_rows // tile
    count = per_group * steps

    def tile_at(place, distances):
        at = lax.axis_index("view") & (groups - 1)
        group = place // count
        step = place - group * count
        block = step // steps
        distance = distances[0] + (distances[-1] - distances[0]) * group
        return ((at ^ distance) + block * groups) * steps + step - block * steps

    def all_tiles(distance):
        return lambda i: (i, tile_at(i, (distance,)))

    def missing_tile():
        at = lax.axis_index("view") & 3
        low = jnp.where(at == 3, 0, count)
        high = jnp.where(at == 0, count - 1, 2 * count - 1)
        return jnp.where(at & 1 == 1, low, high)

    def inner_tiles(i):
        place = jnp.where(i == missing_tile(), 2 * count - 1, i)
        return place, tile_at(place, (3, 1))

    def edge_tile(i):
        return missing_tile(), tile_at(missing_tile(), (3, 1))

    matrix = jnp.asarray(stencil(tile, tf_color.shape[1]))
    matrix, *faces = prepare(
        *(pltpu.with_memory_space_constraint(part, pltpu.HBM) for part in (volume, matrix))
    )
    depth, lines, ends = (exchange(face, axis) for face, axis in zip(faces, AXES))
    depth, lines = (
        found if len(found) == 2 else found + [jnp.zeros_like(found[0])] for found in (depth, lines)
    )
    ends = sum(ends[1:], ends[0])

    def march_call(tiles, tile_count, out_groups=1, after=None, partial=None, with_lines=True):
        here = ends
        if after is not None:
            here, _ = lax.optimization_barrier((ends, after))
        return march(
            volume,
            matrix,
            (depth, here, lines if with_lines else None),
            tiles,
            tile_count,
            (out_groups, count * tile),
            (tf_color, tf_opacity),
            slices * view_count,
            tile,
            partial,
        )

    if groups == 4:
        far = march_call(inner_tiles, 2 * count - 1, 2, with_lines=False)
        far = march_call(edge_tile, 1, 2, partial=far)
        received = from_partner(far, "view", 0)
        near = march_call(all_tiles(2), count, after=far)
        code = merge_pair(near, received)
        code_received = from_partner(code, "view", 1)
        near = march_call(all_tiles(0), count, after=code)
        image = merge_last(near, received, code_received, bits == 2)
    elif groups == 2:
        far = march_call(all_tiles(1), count)
        received = from_partner(far, "view", 0)
        image = merged(march_call(all_tiles(0), count, after=far)[0], received[0], position & 1)
    else:
        image = march_call(all_tiles(0), count)[0]
    if bits == 2:
        return image.reshape(4, 1, tile_rows, width)
    image = image.reshape((4,) + (2,) * (bits - group_bits) + (tile_rows, width))
    for bit in range(group_bits, bits):
        side = position >> bit & 1
        axis = bits - bit
        kept = lax.dynamic_index_in_dim(image, side, axis, keepdims=False)
        sent = lax.dynamic_index_in_dim(image, 1 - side, axis, keepdims=False)
        image = merged(kept, from_partner(sent, "view", bit), side)
    image = jnp.concatenate([image[:3], 1.0 - image[3:]], axis=0)
    return image.reshape(4, 1, tile_rows, width)


def solution(mesh):
    placed = (P("view", "row", "col"), P(), P())
    return jax.shard_map(
        on_device,
        mesh=mesh,
        in_specs=placed,
        out_specs=P(None, "view", "row", "col"),
        check_vma=False,
    )
```

```python
import functools
import itertools

import jax
import jax.numpy as jnp
import numpy as np
from jax import lax
from jax.experimental import pallas as pl
from jax.experimental.pallas import tpu as pltpu
from jax.sharding import PartitionSpec as P

BASIS = ((12.0, 15.0, 16.0), (-20.0, 0.0, 15.0), (9.0, -20.0, 12.0))
NORM = 25.0
VALUE_LOW = -3.0
VALUE_HIGH = 3.0
AMBIENT = 0.35
DIFFUSE = 0.65
LANES = 128
PACK = 16
HALF = 8
AXES = ("view", "row", "col")
DEPTH = 2
SLOTS = 4
CODE_SCALE = 240.0
CODE_SHIFT = 120.0
ALONG_SUBLANES = lax.GatherDimensionNumbers(
    offset_dims=(),
    collapsed_slice_dims=(0,),
    start_index_map=(0,),
    operand_batching_dims=(1,),
    start_indices_batching_dims=(1,),
)
VECTORS = pl.BlockSpec(memory_space=pltpu.VMEM)
ANYWHERE = pl.BlockSpec(memory_space=pl.ANY)


def stencil(tile, knot_count):
    scale = (knot_count - 1) / (VALUE_HIGH - VALUE_LOW)
    width = 5 * tile + 3 * PACK
    after, before, above, centre, below, right, left, one = np.cumsum(
        [0, tile, tile, PACK, tile, PACK, tile, tile]
    )
    matrix = np.zeros((4 * tile, width), np.float32)
    for row in range(tile):
        for part, (along_z, along_y, along_x) in enumerate(BASIS):
            line = matrix[part * tile + row]
            line[after + row] += along_z / 2
            line[before + row] -= along_z / 2
            line[centre + row + 1 if row + 1 < tile else below] += along_y / 2
            line[centre + row - 1 if row > 0 else above + PACK - 1] -= along_y / 2
            line[right + row] += along_x / 2
            line[left + row] -= along_x / 2
        line = matrix[3 * tile + row]
        line[centre + row] = scale / 2
        line[one] = -VALUE_LOW * scale / 2 - 0.5
    rounded = matrix.astype(jnp.bfloat16)
    assert np.array_equal(rounded.astype(np.float32), matrix)
    return rounded


def exchange(faces, axis):
    count = lax.axis_size(axis)
    received = []
    for start, face in enumerate(faces):
        pairs = [(i, i + 1) for i in range(start, count - 1, 2)]
        both = pairs + [(j, i) for i, j in pairs]
        received.append(lax.ppermute(face, axis, both) if both else jnp.zeros_like(face))
    return received


def segment_lines(knot_count, first):
    segment = first + lax.broadcasted_iota(jnp.int32, (HALF, knot_count), 0)
    knot = lax.broadcasted_iota(jnp.int32, (HALF, knot_count), 1)
    left, middle, right = (
        jnp.where(knot == jnp.minimum(2 * segment + i, knot_count - 1), 1.0, 0.0) for i in range(3)
    )
    return middle, 2.0 * (middle - left), 2.0 * (right - middle)


def parities():
    return [lax.axis_index(axis) & 1 for axis in AXES]


def prepare_kernel(
    volume_ref,
    stencil_ref,
    matrix_ref,
    depth_outs,
    row_outs,
    column_outs,
    lines_ref,
    columns_ref,
    arrived,
):
    slices, height, width = volume_ref.shape
    odd = parities()
    copies = {}
    for turn in range(len(column_outs)):
        start = pl.multiple_of(jnp.where(odd[2] == 1 - turn, 0, width - LANES), LANES)
        copies[2, turn] = (volume_ref.at[:, :, pl.ds(start, LANES)], columns_ref.at[turn])
    for turn in range(len(row_outs)):
        start = pl.multiple_of(jnp.where(odd[1] == 1 - turn, 0, height - PACK), PACK)
        copies[1, turn] = (volume_ref.at[:, pl.ds(start, PACK), :], lines_ref.at[turn])
    for turn in range(len(depth_outs)):
        face = jnp.where(odd[0] == 1 - turn, 0, slices - 1)
        copies[0, turn] = (volume_ref.at[face], depth_outs[turn])
    copies[None] = (stencil_ref, matrix_ref)
    for i, (key, pair) in enumerate(copies.items()):
        copies[key] = pltpu.make_async_copy(*pair, arrived.at[i])
        copies[key].start()
    row = lax.broadcasted_iota(jnp.int16, (slices, width), 0)
    lane = lax.broadcasted_iota(jnp.int16, (height, LANES), 1)

    def columns(turn, source, shift):
        found = jnp.zeros((height, LANES), column_outs[turn].dtype)
        for z in range(slices):
            target = (2 * z + shift) % LANES
            moved = pltpu.roll(columns_ref[turn, z], (target - source) % LANES, 1)
            found = jnp.where(lane == target, moved, found)
        column_outs[turn][...] = found

    for turn in range(len(column_outs)):
        copies[2, turn].wait()
        pl.when(odd[2] == 1 - turn)(functools.partial(columns, turn, 0, -1))
        pl.when(odd[2] == turn)(functools.partial(columns, turn, LANES - 1, 0))
    for turn in range(len(row_outs)):
        copies[1, turn].wait()
        is_first = odd[1] == 1 - turn
        lines = jnp.zeros((slices, width), row_outs[turn].dtype)
        for z in range(slices):
            line = jnp.where(is_first, lines_ref[turn, z, :1], lines_ref[turn, z, PACK - 1 :])
            lines = jnp.where(row == z, jnp.broadcast_to(line, lines.shape), lines)
        row_outs[turn][...] = lines
    for turn in range(len(depth_outs)):
        copies[0, turn].wait()
    copies[None].wait()


def prepare(volume, matrix):
    slices, height, width = volume.shape
    assert 2 * slices <= LANES
    shapes = [(height, width), (slices, width), (height, LANES)]
    turns = [2 if lax.axis_size(axis) > 2 else 1 for axis in AXES]
    out_shape = [jax.ShapeDtypeStruct(matrix.shape, matrix.dtype)] + [
        [jax.ShapeDtypeStruct(shape, volume.dtype)] * count for shape, count in zip(shapes, turns)
    ]
    return pl.pallas_call(
        prepare_kernel,
        in_specs=[pl.BlockSpec(memory_space=pltpu.HBM)] * 2,
        out_specs=jax.tree.map(lambda _: VECTORS, out_shape),
        out_shape=out_shape,
        scratch_shapes=[
            pltpu.VMEM((turns[1], slices, PACK, width), volume.dtype),
            pltpu.VMEM((turns[2], slices, height, LANES), volume.dtype),
            pltpu.SemaphoreType.DMA((sum(turns) + 1,)),
        ],
        compiler_params=pltpu.CompilerParams(vmem_limit_bytes=24 * 2**20),
    )(volume, matrix)


def march_kernel(*refs, tiles, count, tile, optical, with_lines, patch):
    stencil_ref, color_ref, opacity_ref, cells_ref = refs[:4]
    depth_refs, ends_ref, refs = refs[4:6], refs[6], refs[7:]
    if with_lines:
        line_refs, refs = refs[:2], refs[2:]
    if patch:
        _, whole_ref, image_ref, parts_ref, sides_ref, copied = refs
    elif with_lines:
        image_ref, parts_ref, sides_ref = refs
    else:
        image_ref, parts_ref = refs
    per_group = image_ref.shape[2] // tile
    slices, height, width = cells_ref.shape
    lane = lax.broadcasted_iota(jnp.int16, (tile, LANES), 1)
    ones = jnp.ones((PACK, width), cells_ref.dtype)
    knot_count = color_ref.shape[1]
    halves = -(-knot_count // (2 * HALF))
    rest = width - LANES
    half_width = width // 2 if width % (2 * LANES) == 0 else width
    tables = [None] * (12 * halves)
    for half in range(halves):
        for part, weights in enumerate(segment_lines(knot_count, HALF * half)):
            for channel in range(4):
                knots = (
                    color_ref[channel : channel + 1] * DIFFUSE
                    if channel < 3
                    else opacity_ref[...] * optical
                )
                values = jnp.sum(weights * knots, axis=1, keepdims=True)
                tables[(3 * channel + part) * halves + half] = jnp.broadcast_to(
                    values, (HALF, LANES)
                )

    def look_up(which, index, in_half):
        for half in range(halves):
            found = lax.gather(
                tables[which * halves + half],
                index[..., None],
                ALONG_SUBLANES,
                slice_sizes=(1, 1),
                mode=lax.GatherScatterMode.PROMISE_IN_BOUNDS,
            )
            value = found if half == 0 else jnp.where(in_half[half - 1], found, value)
        return value

    def shade(z, slot, row, column, state):
        lit, second, third, knot = (
            parts_ref[slot, pl.ds(part * tile + row, HALF), pl.ds(column, LANES)]
            for part in range(4)
        )
        knot = jnp.minimum(jnp.maximum(knot, -0.5), knot_count / 2 - 1.0)
        middle = jnp.round(knot)
        segment = middle.astype(jnp.int32)
        offset = knot - middle
        before_middle = offset < 0.0
        index = segment & (HALF - 1) if halves > 1 else segment
        in_half = [middle >= float(HALF * half) for half in range(1, halves)]
        inverse = lax.rsqrt((lit * lit + second * second) + (third * third + NORM * NORM))
        shading = jnp.abs(lit) * inverse + AMBIENT / DIFFUSE
        density = 1.2 / NORM**2 - inverse * inverse
        values = [
            look_up(3 * c, index, in_half)
            + offset
            * jnp.where(
                before_middle,
                look_up(3 * c + 1, index, in_half),
                look_up(3 * c + 2, index, in_half),
            )
            for c in range(4)
        ]
        kept = jnp.exp2(values[3] * density)
        if state is None:
            weight = (1.0 - kept) * shading
            return [value * weight for value in values[:3]] + [kept]
        through = state[3] * kept
        weight = (state[3] - through) * shading
        return [total + value * weight for total, value in zip(state, values[:3])] + [through]

    odd = [parity == 1 for parity in parities()[:2]]
    if with_lines:
        for side in range(2):
            lines = jnp.where(odd[1], line_refs[side][...], line_refs[1 - side][...])
            for z in range(slices):
                sides_ref[side, z] = jnp.broadcast_to(lines[z : z + 1], (PACK, width))

    def gradients(i, z):
        start = pl.multiple_of(tiles(i)[1] * tile, tile)
        rows = pl.ds(start, tile)

        def across(side):
            return jnp.where(
                odd[0], depth_refs[side][rows, :], depth_refs[1 - side][rows, :]
            )

        def beside(side, at_face, near):
            inner = cells_ref[z, pl.ds(pl.multiple_of(near, PACK), PACK), :]
            return jnp.where(at_face, sides_ref[side, z], inner) if with_lines else inner

        cells = cells_ref[z, rows, :]
        before = cells_ref[z - 1, rows, :] if z > 0 else across(0)
        after = cells_ref[z + 1, rows, :] if z + 1 < slices else across(1)
        above = beside(0, start == 0, jnp.maximum(start - PACK, 0))
        below = beside(1, start == height - tile, jnp.minimum(start + tile, height - PACK))
        right = pltpu.roll(cells, width - 1, 1)
        left = pltpu.roll(cells, 1, 1)
        ends = ends_ref[rows, :]
        ends = pltpu.roll(ends, LANES - 2 * z, 1) if z else ends
        right_end = jnp.where(lane == LANES - 1, ends, right[:, rest:])
        left_end = jnp.where(lane == 0, ends, left[:, :LANES])
        if rest:
            right_end = jnp.concatenate([right[:, :rest], right_end], axis=1)
            left_end = jnp.concatenate([left_end, left[:, LANES:]], axis=1)
        stacked = jnp.concatenate(
            [after, before, above, cells, below, right_end, left_end, ones], axis=0
        )
        for column in range(0, width, half_width):
            parts_ref[z % SLOTS, :, pl.ds(column, half_width)] = jnp.dot(
                stencil_ref[...],
                stacked[:, column : column + half_width],
                preferred_element_type=jnp.float32,
            )
            yield

    def shades(i, first):
        place = tiles(i)[0]
        group = 0 if patch else place // per_group
        target = 0 if patch else pl.multiple_of((place - group * per_group) * tile, tile)
        for column in range(0, width, LANES):
            for row in range(0, tile, HALF):
                here = (pl.ds(target + row, HALF), pl.ds(column, LANES))
                state = None if first == 0 else [image_ref[(group, c) + here] for c in range(4)]
                for z in range(first, first + DEPTH):
                    state = shade(z, z % SLOTS, row, column, state)
                for c in range(4):
                    image_ref[(group, c) + here] = state[c]
                yield

    def one_tile(i, carry):
        following = jnp.minimum(i + 1, count - 1)
        for z in range(0, slices, DEPTH):
            ahead = [
                gradients(i if later < slices else following, later % slices)
                for later in range(z + DEPTH, z + 2 * DEPTH)
            ]
            interleave(
                itertools.chain(*ahead),
                DEPTH * (width // half_width),
                shades(i, z),
                (tile // HALF) * (width // LANES),
            )
        return carry

    for z in range(DEPTH):
        for _ in gradients(0, z):
            pass
    lax.fori_loop(0, count, one_tile, 0)
    if patch:
        per_group = whole_ref.shape[2] // tile
        group = tiles(0)[0] // per_group
        rows = (tiles(0)[0] - group * per_group) * tile
        copy = pltpu.make_async_copy(
            image_ref.at[0], whole_ref.at[group, :, pl.ds(pl.multiple_of(rows, tile), tile)], copied
        )
        copy.start()
        copy.wait()


def interleave(first, first_count, second, second_count):
    done = 0
    for step in range(second_count):
        while done * second_count <= step * first_count and done < first_count:
            next(first, None)
            done += 1
        next(second)
    for _ in itertools.chain(first, second):
        pass


def march(cells, matrix, halos, tiles, count, image, transfer, depth_total, tile, partial=None):
    slices, height, width = cells.shape
    depth, ends, lines = halos
    assert slices % SLOTS == 0 and SLOTS == 2 * DEPTH
    tf_color, tf_opacity = transfer
    knot_count = tf_color.shape[1]
    optical = float(-2.0 / depth_total * NORM**2 * np.log2(np.e))
    groups, rows = image
    patch = partial is not None
    scratch = [pltpu.VMEM((SLOTS, 4 * tile, width), jnp.float32)]
    operands = [
        matrix,
        tf_color,
        tf_opacity.reshape(1, knot_count),
        cells,
        *depth,
        ends,
    ]
    if lines is not None:
        operands += lines
        scratch.append(pltpu.VMEM((2, slices, PACK, width), cells.dtype))
    in_specs = [VECTORS] * len(operands)
    if patch:
        operands.append(partial)
        in_specs.append(ANYWHERE)
        scratch = [pltpu.VMEM((1, 4, tile, width), jnp.float32)] + scratch
        scratch.append(pltpu.SemaphoreType.DMA)
    return pl.pallas_call(
        functools.partial(
            march_kernel,
            tiles=tiles,
            count=count,
            tile=tile,
            optical=optical,
            with_lines=lines is not None,
            patch=patch,
        ),
        in_specs=in_specs,
        out_specs=ANYWHERE if patch else VECTORS,
        out_shape=jax.ShapeDtypeStruct((groups, 4, rows, width), jnp.float32),
        input_output_aliases={len(operands) - 1: 0} if patch else {},
        scratch_shapes=scratch,
        compiler_params=pltpu.CompilerParams(vmem_limit_bytes=24 * 2**20),
    )(*operands)


def ordered_over(first, second, swapped):
    colours = [
        jnp.where(swapped, b, a) + jnp.where(swapped, second[3], first[3]) * jnp.where(swapped, a, b)
        for a, b in zip(first[:3], second[:3])
    ]
    return colours + [first[3] * second[3]]


def pair_kernel(own_ref, other_ref, code_ref, *, first_row):
    rows = pl.ds(first_row, own_ref.shape[2])
    own = [own_ref[0, c] for c in range(4)]
    other = [other_ref[0, c, rows] for c in range(4)]
    merged = ordered_over(own, other, lax.axis_index("view") & 1 == 1)
    for c in range(4):
        code_ref[c] = jnp.exp2(CODE_SCALE * merged[c] - CODE_SHIFT).astype(code_ref.dtype)


def last_kernel(own_ref, other_ref, *refs, finish):
    code_refs, out_ref = refs[:-1], refs[-1]
    step, size = pl.program_id(0), out_ref.shape[1]
    rows = pl.ds(pl.multiple_of(step * size, PACK), size)
    own = [own_ref[0, c, rows] for c in range(4)]
    other = [other_ref[1, c, rows] for c in range(4)]
    codes = [code_refs[0][c] for c in range(4)]
    for part, code_ref in enumerate(code_refs[1:], 1):
        codes = [jnp.where(step >= part, code_ref[c], codes[c]) for c in range(4)]
    far = [(jnp.log2(code.astype(jnp.float32)) + CODE_SHIFT) * (1.0 / CODE_SCALE) for code in codes]
    pair = ordered_over(own, other, lax.axis_index("view") & 1 == 1)
    merged = ordered_over(pair, far, lax.axis_index("view") & 2 == 2)
    for c in range(3):
        out_ref[c] = merged[c]
    out_ref[3] = 1.0 - merged[3] if finish else merged[3]


def merge_pair(own, other, first_row):
    return pl.pallas_call(
        functools.partial(pair_kernel, first_row=first_row),
        in_specs=[VECTORS, VECTORS],
        out_specs=VECTORS,
        out_shape=jax.ShapeDtypeStruct(own.shape[1:], jnp.bfloat16),
        compiler_params=pltpu.CompilerParams(vmem_limit_bytes=24 * 2**20),
    )(own, other)


def merge_last(own, other, codes, finish):
    _, _, rows, width = own.shape
    steps = len(codes)
    return pl.pallas_call(
        functools.partial(last_kernel, finish=finish),
        grid=(steps,),
        in_specs=[VECTORS] * (2 + steps),
        out_specs=pl.BlockSpec((4, rows // steps, width), lambda i: (0, i, 0)),
        out_shape=jax.ShapeDtypeStruct(own.shape[1:], jnp.float32),
        compiler_params=pltpu.CompilerParams(vmem_limit_bytes=24 * 2**20),
    )(own, other, *codes)


def over(nearer, farther):
    through = nearer[3:]
    return jnp.concatenate([nearer[:3] + through * farther[:3], through * farther[3:]], axis=0)


def merged(own, other, side):
    nearer = jnp.where(side == 0, own, other)
    farther = jnp.where(side == 0, other, own)
    return over(nearer, farther)


def from_partner(value, axis, bit):
    pairs = [(source, source ^ (1 << bit)) for source in range(lax.axis_size(axis))]
    return lax.ppermute(value, axis, pairs)


def on_device(volume, tf_color, tf_opacity):
    view_count = lax.axis_size("view")
    position = lax.axis_index("view")
    slices, height, width = volume.shape
    tile_rows = height // view_count
    tile = min(32, tile_rows)
    bits = view_count.bit_length() - 1
    group_bits = min(2, bits)
    groups = 1 << group_bits
    per_group = view_count // groups

    steps = tile_rows // tile
    count = per_group * steps

    def tile_at(place, distances):
        at = lax.axis_index("view") & (groups - 1)
        group = place // count
        step = place - group * count
        block = step // steps
        distance = distances[0] + (distances[-1] - distances[0]) * group
        return ((at ^ distance) + block * groups) * steps + step - block * steps

    def all_tiles(distance, first=0):
        return lambda i: (i, tile_at(first + i, (distance,)))

    def missing_tile():
        at = lax.axis_index("view") & 3
        low = jnp.where(at == 3, 0, count)
        high = jnp.where(at == 0, count - 1, 2 * count - 1)
        return jnp.where(at & 1 == 1, low, high)

    def inner_tiles(i):
        place = jnp.where(i == missing_tile(), 2 * count - 1, i)
        return place, tile_at(place, (3, 1))

    def edge_tile(i):
        return missing_tile(), tile_at(missing_tile(), (3, 1))

    matrix = jnp.asarray(stencil(tile, tf_color.shape[1]))
    matrix, *faces = prepare(
        *(pltpu.with_memory_space_constraint(part, pltpu.HBM) for part in (volume, matrix))
    )
    depth, lines, ends = (exchange(face, axis) for face, axis in zip(faces, AXES))
    depth, lines = (
        found if len(found) == 2 else found + [jnp.zeros_like(found[0])] for found in (depth, lines)
    )
    ends = sum(ends[1:], ends[0])

    def march_call(tiles, tile_count, out_groups=1, after=None, partial=None, with_lines=True):
        here = ends
        if after is not None:
            here, _ = lax.optimization_barrier((ends, after))
        return march(
            volume,
            matrix,
            (depth, here, lines if with_lines else None),
            tiles,
            tile_count,
            (out_groups, tile_count * tile if out_groups == 1 else count * tile),
            (tf_color, tf_opacity),
            slices * view_count,
            tile,
            partial,
        )

    if groups == 4:
        far = march_call(inner_tiles, 2 * count - 1, 2, with_lines=False)
        far = march_call(edge_tile, 1, 2, partial=far)
        received = from_partner(far, "view", 0)
        parts = 2 if count % 2 == 0 and count * tile % (2 * PACK) == 0 else 1
        size = count // parts
        before, codes = far, []
        for first in range(0, count, size):
            near = march_call(all_tiles(2, first), size, after=before)
            before = merge_pair(near, received, first * tile)
            codes.append(from_partner(before, "view", 1))
        near = march_call(all_tiles(0), count, after=[before] + codes[:-1])
        image = merge_last(near, received, codes, bits == 2)
    elif groups == 2:
        far = march_call(all_tiles(1), count)
        received = from_partner(far, "view", 0)
        image = merged(march_call(all_tiles(0), count, after=far)[0], received[0], position & 1)
    else:
        image = march_call(all_tiles(0), count)[0]
    if bits == 2:
        return image.reshape(4, 1, tile_rows, width)
    image = image.reshape((4,) + (2,) * (bits - group_bits) + (tile_rows, width))
    for bit in range(group_bits, bits):
        side = position >> bit & 1
        axis = bits - bit
        kept = lax.dynamic_index_in_dim(image, side, axis, keepdims=False)
        sent = lax.dynamic_index_in_dim(image, 1 - side, axis, keepdims=False)
        image = merged(kept, from_partner(sent, "view", bit), side)
    image = jnp.concatenate([image[:3], 1.0 - image[3:]], axis=0)
    return image.reshape(4, 1, tile_rows, width)


def solution(mesh):
    placed = (P("view", "row", "col"), P(), P())
    return jax.shard_map(
        on_device,
        mesh=mesh,
        in_specs=placed,
        out_specs=P(None, "view", "row", "col"),
        check_vma=False,
    )
```

```python
import functools
import itertools

import jax
import jax.numpy as jnp
import numpy as np
from jax import lax
from jax.experimental import pallas as pl
from jax.experimental.pallas import tpu as pltpu
from jax.sharding import PartitionSpec as P

BASIS = ((12.0, 15.0, 16.0), (-20.0, 0.0, 15.0), (9.0, -20.0, 12.0))
NORM = 25.0
VALUE_LOW = -3.0
VALUE_HIGH = 3.0
AMBIENT = 0.35
DIFFUSE = 0.65
LANES = 128
PACK = 16
HALF = 8
AXES = ("view", "row", "col")
DEPTH = 2
SLOTS = 4
CODE_SCALE = 240.0
CODE_SHIFT = 120.0
ALONG_SUBLANES = lax.GatherDimensionNumbers(
    offset_dims=(),
    collapsed_slice_dims=(0,),
    start_index_map=(0,),
    operand_batching_dims=(1,),
    start_indices_batching_dims=(1,),
)
VECTORS = pl.BlockSpec(memory_space=pltpu.VMEM)
ANYWHERE = pl.BlockSpec(memory_space=pl.ANY)


def stencil(tile, knot_count):
    scale = (knot_count - 1) / (VALUE_HIGH - VALUE_LOW)
    width = 5 * tile + 3 * PACK
    after, before, above, centre, below, right, left, one = np.cumsum(
        [0, tile, tile, PACK, tile, PACK, tile, tile]
    )
    matrix = np.zeros((4 * tile, width), np.float32)
    for row in range(tile):
        for part, (along_z, along_y, along_x) in enumerate(BASIS):
            line = matrix[part * tile + row]
            line[after + row] += along_z / 2
            line[before + row] -= along_z / 2
            line[centre + row + 1 if row + 1 < tile else below] += along_y / 2
            line[centre + row - 1 if row > 0 else above + PACK - 1] -= along_y / 2
            line[right + row] += along_x / 2
            line[left + row] -= along_x / 2
        line = matrix[3 * tile + row]
        line[centre + row] = scale / 2
        line[one] = -VALUE_LOW * scale / 2 - 0.5
    rounded = matrix.astype(jnp.bfloat16)
    assert np.array_equal(rounded.astype(np.float32), matrix)
    return rounded


def exchange(faces, axis):
    count = lax.axis_size(axis)
    received = []
    for start, face in enumerate(faces):
        pairs = [(i, i + 1) for i in range(start, count - 1, 2)]
        both = pairs + [(j, i) for i, j in pairs]
        received.append(lax.ppermute(face, axis, both) if both else jnp.zeros_like(face))
    return received


def segment_lines(knot_count, first):
    segment = first + lax.broadcasted_iota(jnp.int32, (HALF, knot_count), 0)
    knot = lax.broadcasted_iota(jnp.int32, (HALF, knot_count), 1)
    left, middle, right = (
        jnp.where(knot == jnp.minimum(2 * segment + i, knot_count - 1), 1.0, 0.0) for i in range(3)
    )
    return middle, 2.0 * (middle - left), 2.0 * (right - middle)


def parities():
    return [lax.axis_index(axis) & 1 for axis in AXES]


def prepare_kernel(
    volume_ref,
    stencil_ref,
    matrix_ref,
    depth_outs,
    row_outs,
    column_outs,
    lines_ref,
    columns_ref,
    arrived,
):
    slices, height, width = volume_ref.shape
    odd = parities()
    copies = {}
    for turn in range(len(column_outs)):
        start = pl.multiple_of(jnp.where(odd[2] == 1 - turn, 0, width - LANES), LANES)
        copies[2, turn] = (volume_ref.at[:, :, pl.ds(start, LANES)], columns_ref.at[turn])
    for turn in range(len(row_outs)):
        start = pl.multiple_of(jnp.where(odd[1] == 1 - turn, 0, height - PACK), PACK)
        copies[1, turn] = (volume_ref.at[:, pl.ds(start, PACK), :], lines_ref.at[turn])
    for turn in range(len(depth_outs)):
        face = jnp.where(odd[0] == 1 - turn, 0, slices - 1)
        copies[0, turn] = (volume_ref.at[face], depth_outs[turn])
    copies[None] = (stencil_ref, matrix_ref)
    for i, (key, pair) in enumerate(copies.items()):
        copies[key] = pltpu.make_async_copy(*pair, arrived.at[i])
        copies[key].start()
    row = lax.broadcasted_iota(jnp.int16, (slices, width), 0)
    lane = lax.broadcasted_iota(jnp.int16, (height, LANES), 1)

    def columns(turn, source, shift):
        found = jnp.zeros((height, LANES), column_outs[turn].dtype)
        for z in range(slices):
            target = (2 * z + shift) % LANES
            moved = pltpu.roll(columns_ref[turn, z], (target - source) % LANES, 1)
            found = jnp.where(lane == target, moved, found)
        column_outs[turn][...] = found

    for turn in range(len(column_outs)):
        copies[2, turn].wait()
        pl.when(odd[2] == 1 - turn)(functools.partial(columns, turn, 0, -1))
        pl.when(odd[2] == turn)(functools.partial(columns, turn, LANES - 1, 0))
    for turn in range(len(row_outs)):
        copies[1, turn].wait()
        is_first = odd[1] == 1 - turn
        lines = jnp.zeros((slices, width), row_outs[turn].dtype)
        for z in range(slices):
            line = jnp.where(is_first, lines_ref[turn, z, :1], lines_ref[turn, z, PACK - 1 :])
            lines = jnp.where(row == z, jnp.broadcast_to(line, lines.shape), lines)
        row_outs[turn][...] = lines
    for turn in range(len(depth_outs)):
        copies[0, turn].wait()
    copies[None].wait()


def prepare(volume, matrix):
    slices, height, width = volume.shape
    assert 2 * slices <= LANES
    shapes = [(height, width), (slices, width), (height, LANES)]
    turns = [2 if lax.axis_size(axis) > 2 else 1 for axis in AXES]
    out_shape = [jax.ShapeDtypeStruct(matrix.shape, matrix.dtype)] + [
        [jax.ShapeDtypeStruct(shape, volume.dtype)] * count for shape, count in zip(shapes, turns)
    ]
    return pl.pallas_call(
        prepare_kernel,
        in_specs=[pl.BlockSpec(memory_space=pltpu.HBM)] * 2,
        out_specs=jax.tree.map(lambda _: VECTORS, out_shape),
        out_shape=out_shape,
        scratch_shapes=[
            pltpu.VMEM((turns[1], slices, PACK, width), volume.dtype),
            pltpu.VMEM((turns[2], slices, height, LANES), volume.dtype),
            pltpu.SemaphoreType.DMA((sum(turns) + 1,)),
        ],
        compiler_params=pltpu.CompilerParams(vmem_limit_bytes=24 * 2**20),
    )(volume, matrix)


def march_kernel(*refs, tiles, count, tile, optical, with_lines, patch):
    stencil_ref, color_ref, opacity_ref, cells_ref = refs[:4]
    depth_refs, ends_ref, refs = refs[4:6], refs[6], refs[7:]
    if with_lines:
        line_refs, refs = refs[:2], refs[2:]
    if patch:
        _, whole_ref, image_ref, parts_ref, sides_ref, copied = refs
    elif with_lines:
        image_ref, parts_ref, sides_ref = refs
    else:
        image_ref, parts_ref = refs
    per_group = image_ref.shape[2] // tile
    slices, height, width = cells_ref.shape
    lane = lax.broadcasted_iota(jnp.int16, (tile, LANES), 1)
    ones = jnp.ones((PACK, width), cells_ref.dtype)
    knot_count = color_ref.shape[1]
    halves = -(-knot_count // (2 * HALF))
    rest = width - LANES
    half_width = width // 2 if width % (2 * LANES) == 0 else width
    tables = [None] * (12 * halves)
    for half in range(halves):
        for part, weights in enumerate(segment_lines(knot_count, HALF * half)):
            for channel in range(4):
                knots = (
                    color_ref[channel : channel + 1] * DIFFUSE
                    if channel < 3
                    else opacity_ref[...] * optical
                )
                values = jnp.sum(weights * knots, axis=1, keepdims=True)
                tables[(3 * channel + part) * halves + half] = jnp.broadcast_to(
                    values, (HALF, LANES)
                )

    def look_up(which, index, in_half):
        for half in range(halves):
            found = lax.gather(
                tables[which * halves + half],
                index[..., None],
                ALONG_SUBLANES,
                slice_sizes=(1, 1),
                mode=lax.GatherScatterMode.PROMISE_IN_BOUNDS,
            )
            value = found if half == 0 else jnp.where(in_half[half - 1], found, value)
        return value

    def shade(z, slot, row, column, state):
        lit, second, third, knot = (
            parts_ref[slot, pl.ds(part * tile + row, HALF), pl.ds(column, LANES)]
            for part in range(4)
        )
        knot = jnp.minimum(jnp.maximum(knot, -0.5), knot_count / 2 - 1.0)
        middle = jnp.round(knot)
        segment = middle.astype(jnp.int32)
        offset = knot - middle
        before_middle = offset < 0.0
        index = segment & (HALF - 1) if halves > 1 else segment
        in_half = [middle >= float(HALF * half) for half in range(1, halves)]
        inverse = lax.rsqrt((lit * lit + second * second) + (third * third + NORM * NORM))
        shading = jnp.abs(lit) * inverse + AMBIENT / DIFFUSE
        density = 1.2 / NORM**2 - inverse * inverse
        values = [
            look_up(3 * c, index, in_half)
            + offset
            * jnp.where(
                before_middle,
                look_up(3 * c + 1, index, in_half),
                look_up(3 * c + 2, index, in_half),
            )
            for c in range(4)
        ]
        kept = jnp.exp2(values[3] * density)
        if state is None:
            weight = (1.0 - kept) * shading
            return [value * weight for value in values[:3]] + [kept]
        through = state[3] * kept
        weight = (state[3] - through) * shading
        return [total + value * weight for total, value in zip(state, values[:3])] + [through]

    odd = [parity == 1 for parity in parities()[:2]]
    if with_lines:
        for side in range(2):
            lines = jnp.where(odd[1], line_refs[side][...], line_refs[1 - side][...])
            for z in range(slices):
                sides_ref[side, z] = jnp.broadcast_to(lines[z : z + 1], (PACK, width))

    def gradients(i, z):
        start = pl.multiple_of(tiles(i)[1] * tile, tile)
        rows = pl.ds(start, tile)

        def across(side):
            return jnp.where(
                odd[0], depth_refs[side][rows, :], depth_refs[1 - side][rows, :]
            )

        def beside(side, at_face, near):
            inner = cells_ref[z, pl.ds(pl.multiple_of(near, PACK), PACK), :]
            return jnp.where(at_face, sides_ref[side, z], inner) if with_lines else inner

        cells = cells_ref[z, rows, :]
        before = cells_ref[z - 1, rows, :] if z > 0 else across(0)
        after = cells_ref[z + 1, rows, :] if z + 1 < slices else across(1)
        above = beside(0, start == 0, jnp.maximum(start - PACK, 0))
        below = beside(1, start == height - tile, jnp.minimum(start + tile, height - PACK))
        right = pltpu.roll(cells, width - 1, 1)
        left = pltpu.roll(cells, 1, 1)
        ends = ends_ref[rows, :]
        ends = pltpu.roll(ends, LANES - 2 * z, 1) if z else ends
        right_end = jnp.where(lane == LANES - 1, ends, right[:, rest:])
        left_end = jnp.where(lane == 0, ends, left[:, :LANES])
        if rest:
            right_end = jnp.concatenate([right[:, :rest], right_end], axis=1)
            left_end = jnp.concatenate([left_end, left[:, LANES:]], axis=1)
        stacked = jnp.concatenate(
            [after, before, above, cells, below, right_end, left_end, ones], axis=0
        )
        for column in range(0, width, half_width):
            parts_ref[z % SLOTS, :, pl.ds(column, half_width)] = jnp.dot(
                stencil_ref[...],
                stacked[:, column : column + half_width],
                preferred_element_type=jnp.float32,
            )
            yield

    def shades(i, first):
        place = tiles(i)[0]
        group = 0 if patch else place // per_group
        target = 0 if patch else pl.multiple_of((place - group * per_group) * tile, tile)
        for column in range(0, width, LANES):
            for row in range(0, tile, HALF):
                here = (pl.ds(target + row, HALF), pl.ds(column, LANES))
                state = None if first == 0 else [image_ref[(group, c) + here] for c in range(4)]
                for z in range(first, first + DEPTH):
                    state = shade(z, z % SLOTS, row, column, state)
                for c in range(4):
                    image_ref[(group, c) + here] = state[c]
                yield

    def one_tile(i, carry):
        following = jnp.minimum(i + 1, count - 1)
        for z in range(0, slices, DEPTH):
            ahead = [
                gradients(i if later < slices else following, later % slices)
                for later in range(z + DEPTH, z + 2 * DEPTH)
            ]
            interleave(
                itertools.chain(*ahead),
                DEPTH * (width // half_width),
                shades(i, z),
                (tile // HALF) * (width // LANES),
            )
        return carry

    for z in range(DEPTH):
        for _ in gradients(0, z):
            pass
    lax.fori_loop(0, count, one_tile, 0)
    if patch:
        per_group = whole_ref.shape[2] // tile
        group = tiles(0)[0] // per_group
        rows = (tiles(0)[0] - group * per_group) * tile
        copy = pltpu.make_async_copy(
            image_ref.at[0], whole_ref.at[group, :, pl.ds(pl.multiple_of(rows, tile), tile)], copied
        )
        copy.start()
        copy.wait()


def interleave(first, first_count, second, second_count):
    done = 0
    for step in range(second_count):
        while done * second_count <= step * first_count and done < first_count:
            next(first, None)
            done += 1
        next(second)
    for _ in itertools.chain(first, second):
        pass


def march(cells, matrix, halos, tiles, count, image, transfer, depth_total, tile, partial=None, short=False):
    slices, height, width = cells.shape
    depth, ends, lines = halos
    assert slices % SLOTS == 0 and SLOTS == 2 * DEPTH
    tf_color, tf_opacity = transfer
    knot_count = tf_color.shape[1]
    optical = float(-2.0 / depth_total * NORM**2 * np.log2(np.e))
    groups, rows = image
    patch = partial is not None
    scratch = [pltpu.VMEM((SLOTS, 4 * tile, width), jnp.float32)]
    operands = [
        matrix,
        tf_color,
        tf_opacity.reshape(1, knot_count),
        cells,
        *depth,
        ends,
    ]
    if lines is not None:
        operands += lines
        scratch.append(pltpu.VMEM((2, slices, PACK, width), cells.dtype))
    in_specs = [VECTORS] * len(operands)
    if patch:
        operands.append(partial)
        in_specs.append(ANYWHERE)
        scratch = [pltpu.VMEM((1, 4, tile, width), jnp.float32)] + scratch
        scratch.append(pltpu.SemaphoreType.DMA)
    return pl.pallas_call(
        functools.partial(
            march_kernel,
            tiles=tiles,
            count=count,
            tile=tile,
            optical=optical,
            with_lines=lines is not None,
            patch=patch,
        ),
        in_specs=in_specs,
        out_specs=ANYWHERE if patch else VECTORS,
        out_shape=jax.ShapeDtypeStruct((groups, 4, rows, width), jnp.float32),
        input_output_aliases={len(operands) - 1: 0} if patch else {},
        scratch_shapes=scratch,
        cost_estimate=pl.CostEstimate(flops=1, transcendentals=0, bytes_accessed=1) if short else None,
        compiler_params=pltpu.CompilerParams(vmem_limit_bytes=24 * 2**20),
    )(*operands)


def ordered_over(first, second, swapped):
    colours = [
        jnp.where(swapped, b, a) + jnp.where(swapped, second[3], first[3]) * jnp.where(swapped, a, b)
        for a, b in zip(first[:3], second[:3])
    ]
    return colours + [first[3] * second[3]]


def pair_kernel(own_ref, other_ref, code_ref, *, first_row):
    rows = pl.ds(first_row, own_ref.shape[2])
    own = [own_ref[0, c] for c in range(4)]
    other = [other_ref[0, c, rows] for c in range(4)]
    merged = ordered_over(own, other, lax.axis_index("view") & 1 == 1)
    for c in range(4):
        code_ref[c] = jnp.exp2(CODE_SCALE * merged[c] - CODE_SHIFT).astype(code_ref.dtype)


def last_kernel(*refs, parts, finish):
    own_refs, other_ref, code_refs, out_ref = refs[:parts], refs[parts], refs[parts + 1 : -1], refs[-1]
    step, size = pl.program_id(0), out_ref.shape[1]
    rows = pl.ds(pl.multiple_of(step * size, PACK), size)
    own = [own_refs[0][0, c] for c in range(4)]
    other = [other_ref[1, c, rows] for c in range(4)]
    codes = [code_refs[0][c] for c in range(4)]
    for part in range(1, parts):
        own = [jnp.where(step >= part, own_refs[part][0, c], own[c]) for c in range(4)]
        codes = [jnp.where(step >= part, code_refs[part][c], codes[c]) for c in range(4)]
    far = [(jnp.log2(code.astype(jnp.float32)) + CODE_SHIFT) * (1.0 / CODE_SCALE) for code in codes]
    pair = ordered_over(own, other, lax.axis_index("view") & 1 == 1)
    merged = ordered_over(pair, far, lax.axis_index("view") & 2 == 2)
    for c in range(3):
        out_ref[c] = merged[c]
    out_ref[3] = 1.0 - merged[3] if finish else merged[3]


def merge_pair(own, other, first_row):
    return pl.pallas_call(
        functools.partial(pair_kernel, first_row=first_row),
        in_specs=[VECTORS, VECTORS],
        out_specs=VECTORS,
        out_shape=jax.ShapeDtypeStruct(own.shape[1:], jnp.bfloat16),
        compiler_params=pltpu.CompilerParams(vmem_limit_bytes=24 * 2**20),
    )(own, other)


def merge_last(own, other, codes, finish):
    parts = len(codes)
    _, _, rows, width = own[0].shape
    return pl.pallas_call(
        functools.partial(last_kernel, parts=parts, finish=finish),
        grid=(parts,),
        in_specs=[VECTORS] * (2 * parts + 1),
        out_specs=pl.BlockSpec((4, rows, width), lambda i: (0, i, 0)),
        out_shape=jax.ShapeDtypeStruct((4, parts * rows, width), jnp.float32),
        compiler_params=pltpu.CompilerParams(vmem_limit_bytes=24 * 2**20),
    )(*own, other, *codes)


def over(nearer, farther):
    through = nearer[3:]
    return jnp.concatenate([nearer[:3] + through * farther[:3], through * farther[3:]], axis=0)


def merged(own, other, side):
    nearer = jnp.where(side == 0, own, other)
    farther = jnp.where(side == 0, other, own)
    return over(nearer, farther)


def from_partner(value, axis, bit):
    pairs = [(source, source ^ (1 << bit)) for source in range(lax.axis_size(axis))]
    return lax.ppermute(value, axis, pairs)


def on_device(volume, tf_color, tf_opacity):
    view_count = lax.axis_size("view")
    position = lax.axis_index("view")
    slices, height, width = volume.shape
    tile_rows = height // view_count
    tile = min(32, tile_rows)
    bits = view_count.bit_length() - 1
    group_bits = min(2, bits)
    groups = 1 << group_bits
    per_group = view_count // groups

    steps = tile_rows // tile
    count = per_group * steps

    def tile_at(place, distances):
        at = lax.axis_index("view") & (groups - 1)
        group = place // count
        step = place - group * count
        block = step // steps
        distance = distances[0] + (distances[-1] - distances[0]) * group
        return ((at ^ distance) + block * groups) * steps + step - block * steps

    def all_tiles(distance, first=0):
        return lambda i: (i, tile_at(first + i, (distance,)))

    def missing_tile():
        at = lax.axis_index("view") & 3
        low = jnp.where(at == 3, 0, count)
        high = jnp.where(at == 0, count - 1, 2 * count - 1)
        return jnp.where(at & 1 == 1, low, high)

    def inner_tiles(i):
        place = jnp.where(i == missing_tile(), 2 * count - 1, i)
        return place, tile_at(place, (3, 1))

    def edge_tile(i):
        return missing_tile(), tile_at(missing_tile(), (3, 1))

    matrix = jnp.asarray(stencil(tile, tf_color.shape[1]))
    matrix, *faces = prepare(
        *(pltpu.with_memory_space_constraint(part, pltpu.HBM) for part in (volume, matrix))
    )
    depth, lines, ends = (exchange(face, axis) for face, axis in zip(faces, AXES))
    depth, lines = (
        found if len(found) == 2 else found + [jnp.zeros_like(found[0])] for found in (depth, lines)
    )
    ends = sum(ends[1:], ends[0])

    def march_call(
        tiles, tile_count, out_groups=1, after=None, partial=None, with_lines=True, short=False
    ):
        here = ends
        if after is not None:
            here, _ = lax.optimization_barrier((ends, after))
        return march(
            volume,
            matrix,
            (depth, here, lines if with_lines else None),
            tiles,
            tile_count,
            (out_groups, tile_count * tile if out_groups == 1 else count * tile),
            (tf_color, tf_opacity),
            slices * view_count,
            tile,
            partial,
            short,
        )

    if groups == 4:
        far = march_call(inner_tiles, 2 * count - 1, 2, with_lines=False)
        far = march_call(edge_tile, 1, 2, partial=far)
        received = from_partner(far, "view", 0)
        parts = 2 if count % 2 == 0 and count * tile % (2 * PACK) == 0 else 1
        size = count // parts
        before, codes = far, []
        for first in range(0, count, size):
            near = march_call(all_tiles(2, first), size, after=before)
            before = merge_pair(near, received, first * tile)
            codes.append(from_partner(before, "view", 1))
        nears = [march_call(all_tiles(0), size, after=before)]
        for first in range(size, count, size):
            after = [nears[-1]] + codes[:-1]
            nears.append(march_call(all_tiles(0, first), size, after=after, short=True))
        image = merge_last(nears, received, codes, bits == 2)
    elif groups == 2:
        far = march_call(all_tiles(1), count)
        received = from_partner(far, "view", 0)
        image = merged(march_call(all_tiles(0), count, after=far)[0], received[0], position & 1)
    else:
        image = march_call(all_tiles(0), count)[0]
    if bits == 2:
        return image.reshape(4, 1, tile_rows, width)
    image = image.reshape((4,) + (2,) * (bits - group_bits) + (tile_rows, width))
    for bit in range(group_bits, bits):
        side = position >> bit & 1
        axis = bits - bit
        kept = lax.dynamic_index_in_dim(image, side, axis, keepdims=False)
        sent = lax.dynamic_index_in_dim(image, 1 - side, axis, keepdims=False)
        image = merged(kept, from_partner(sent, "view", bit), side)
    image = jnp.concatenate([image[:3], 1.0 - image[3:]], axis=0)
    return image.reshape(4, 1, tile_rows, width)


def solution(mesh):
    placed = (P("view", "row", "col"), P(), P())
    return jax.shard_map(
        on_device,
        mesh=mesh,
        in_specs=placed,
        out_specs=P(None, "view", "row", "col"),
        check_vma=False,
    )
```
